32 devices in a mesh: blk: 4 (over z), leaf: 4 (over y, x), samp: 2 (over core).
Axes of the slice: x: 2, y: 2, z: 4, core: 2. Of those that a mesh axis runs over, the one named last changes fastest.
Arguments:
- points: float32 [3, 4096], P(None, ('blk', 'leaf')), may hold values from 0 to 8, as said below
- neighbors: int32 [16, 8], P(('blk', 'leaf')), may hold values from -1 to 15, as said below
- omega: float32 [512, 4096], P(None, ('blk', 'leaf')), may hold values from -6 to 6
- observed: float32 [4096], P(('blk', 'leaf')), may hold values from -6 to 6
- prior_draws: float32 [64, 4096], P('samp', ('blk', 'leaf')), may hold values from -6 to 6
Outputs:
- weights: float32 [64, 4096], P('samp', ('blk', 'leaf'))
- residual: float32 [64, 4096], P('samp', ('blk', 'leaf'))
The draws below stay inside these ranges and needn't reach their ends.
Inputs may be any that keep to these rules, and one draw needn't show every extreme that they name: Block g's points lie in the unit cell with integer corner (cx, cy, cz), where cx // 2 = g // 4 and 0 <= cy, cz < 3. `neighbors`: row g lists in ascending order every block h whose unit cell touches g's (cells at most one apart in every coordinate, the first taken periodic of period 2 * 4), which includes every block with a point within distance 1 of a point of g, followed by -1 in the unused slots; the relation is symmetric, and every listed block has a slab index h // 4 equal to or cyclically next to g // 4.
All inputs are finite; a program needn't handle non-finite values.
Results may differ from the reference program's by a relative error of at most 0.0003.
Values sent between devices are 32-bit elements; how exact they have to be, the bound alone decides.
No kernel may reach another device: no remote copies, remote signals or barrier semaphores. Data moves between devices by JAX's collectives and lax.ppermute only.
A program may use at most 64 MiB of HBM per device.

```python
import jax
import jax.numpy as jnp
from jax import lax

PB = 256
S = 512
SAMPLES = 64
ITERS = 2
CELLS = 3
BPS = 4
NB = 8
NBLOCKS = 16
NPTS = 4096
N_BLK = 4


def cell_table(key):
    folded = jax.random.fold_in(key, 7)
    draw_x, draw_y, draw_z = jax.random.split(folded, 3)
    block_ids = jnp.arange(NBLOCKS, dtype=jnp.int32)
    slab_ids = block_ids // BPS
    cell_x = 2 * slab_ids + jax.random.randint(draw_x, (NBLOCKS,), 0, 2, dtype=jnp.int32)
    cell_y = jax.random.randint(draw_y, (NBLOCKS,), 0, CELLS, dtype=jnp.int32)
    cell_z = jax.random.randint(draw_z, (NBLOCKS,), 0, CELLS, dtype=jnp.int32)
    return (cell_x, cell_y, cell_z)


def draw_points(key, part):
    cell_x, cell_y, cell_z = cell_table(key)
    offsets = jax.random.uniform(jax.random.fold_in(key, 11), (3, NBLOCKS, PB), jnp.float32)
    corner = jnp.stack([cell_x, cell_y, cell_z]).astype(jnp.float32)
    return (corner[:, :, None] + offsets).reshape(3, NPTS)


def draw_neighbors(key, part):
    cell_x, cell_y, cell_z = cell_table(key)
    block_ids = jnp.arange(NBLOCKS, dtype=jnp.int32)
    slab_ids = block_ids // BPS
    shifts = jnp.arange(3, dtype=jnp.int32) - 1
    within = jnp.arange(BPS, dtype=jnp.int32)
    candidates = jnp.mod(slab_ids[:, None, None] + shifts[None, :, None], N_BLK) * BPS + within[None, None, :]
    candidates = candidates.reshape(NBLOCKS, 3 * BPS)
    gap_x = jnp.mod(cell_x[candidates] - cell_x[:, None], 2 * N_BLK)
    adjacent = (gap_x <= 1) | (gap_x >= 2 * N_BLK - 1)
    adjacent = adjacent & (jnp.abs(cell_y[candidates] - cell_y[:, None]) <= 1)
    adjacent = adjacent & (jnp.abs(cell_z[candidates] - cell_z[:, None]) <= 1)
    sort_keys = jnp.where(adjacent, candidates, NBLOCKS)
    ordered = jnp.sort(sort_keys, axis=1)[:, :NB]
    return jnp.where(ordered == NBLOCKS, -1, ordered).astype(jnp.int32)


def block_scale(own_key, shape, cuts, smallest, largest):
    gain, own = 1.0, jax.random.fold_in(own_key, 6)
    for position, parts in cuts:
        steps = jnp.exp(jax.random.uniform(jax.random.fold_in(own, position), (parts,), jnp.float32, smallest / len(cuts), largest / len(cuts)))
        gain = gain * jnp.repeat(steps, shape[position] // parts).reshape([-1 if axis == position else 1 for axis in range(len(shape))])
    return gain


def gaussian(own_key, shape, deviation, reach, cuts=(), held_as=jnp.bfloat16):
    loudness = block_scale(own_key, shape, cuts, -0.22, 0.18) if cuts else 1.0
    entries = jax.random.normal(own_key, shape, jnp.float32) * deviation * loudness
    return jnp.minimum(jnp.maximum(entries, -reach), reach).astype(held_as)


def setup_inputs(seed: int = 0) -> dict:
    keys = jax.random.split(jax.random.key(seed), 6)
    return {
        "points": draw_points(jax.random.fold_in(keys[5], 71), 0),
        "neighbors": draw_neighbors(jax.random.fold_in(keys[5], 71), 0),
        "omega": gaussian(keys[2], (S, NPTS), 1.0, 6.0, ((1, 16),), jnp.float32),
        "observed": gaussian(keys[3], (NPTS,), 1.0, 6.0, ((0, 16),), jnp.float32),
        "prior_draws": gaussian(keys[4], (SAMPLES, NPTS), 1.0, 6.0, ((0, 2), (1, 16)), jnp.float32),
    }


support_radius = 0.8
noise_variance = 1.0
sketch_shift = 1.0

def wendland(row_points, column_points, period):
    offset = row_points[None, :, :, None] - column_points[:, :, None, :]
    half_period = 0.5 * period
    along_x = jnp.mod(offset[:, 0] + half_period, period) - half_period
    squared = along_x * along_x + offset[:, 1] * offset[:, 1] + offset[:, 2] * offset[:, 2]
    radius = jnp.sqrt(squared) / support_radius
    remain = jnp.maximum(1.0 - radius, 0.0)
    return remain ** 4 * (4.0 * radius + 1.0)

def apply_kernel(values, points, neighbors):
    width = values.shape[0]
    point_blocks = points.reshape(3, NBLOCKS, PB).transpose(1, 0, 2)
    value_blocks = values.reshape(width, NBLOCKS, PB)
    period = 2.0 * N_BLK

    def block_rows(packed):
        row_points, listed = packed
        usable = listed >= 0
        safe_ids = jnp.where(usable, listed, 0).astype(jnp.int32)
        kernel_tile = wendland(row_points, point_blocks[safe_ids], period)
        kernel_tile = kernel_tile * usable[:, None, None].astype(kernel_tile.dtype)
        picked = jnp.take(value_blocks, safe_ids, axis=1)
        return jnp.einsum('cnj,nij->ci', picked, kernel_tile, precision=lax.Precision.HIGHEST)
    applied = lax.map(block_rows, (point_blocks, neighbors))
    return applied.transpose(1, 0, 2).reshape(width, NPTS)

def high_dot(left, right):
    return jnp.dot(left, right, precision=lax.Precision.HIGHEST, preferred_element_type=left.dtype)

def inverse_apply(vectors, basis, wood_factor):
    projected = high_dot(basis, vectors.T)
    first_solve = lax.linalg.triangular_solve(wood_factor, projected, left_side=True, lower=True)
    solved = lax.linalg.triangular_solve(wood_factor, first_solve, left_side=True, lower=True, transpose_a=True)
    return (vectors - high_dot(solved.T, basis)) / noise_variance

def reference(points, neighbors, omega, observed, prior_draws):
    sketch = apply_kernel(omega, points, neighbors) + sketch_shift * omega
    core_gram = high_dot(omega, sketch.T)
    core_gram = 0.5 * (core_gram + core_gram.T)
    factor = jnp.linalg.cholesky(core_gram)
    basis = lax.linalg.triangular_solve(factor, sketch, left_side=True, lower=True)
    basis_gram = high_dot(basis, basis.T)
    woodbury = noise_variance * jnp.eye(S, dtype=basis.dtype) + 0.5 * (basis_gram + basis_gram.T)
    wood_factor = jnp.linalg.cholesky(woodbury)
    rhs = observed[None, :] - prior_draws
    weights = jnp.zeros_like(rhs)
    residual = rhs
    precond = inverse_apply(residual, basis, wood_factor)
    direction = precond
    inner_now = lax.optimization_barrier(jnp.sum(residual * precond, axis=1))
    for step_index in range(ITERS):
        image = apply_kernel(direction, points, neighbors) + noise_variance * direction
        step_size = inner_now / lax.optimization_barrier(jnp.sum(direction * image, axis=1))
        weights = weights + step_size[:, None] * direction
        residual = residual - step_size[:, None] * image
        if step_index + 1 < ITERS:
            precond = inverse_apply(residual, basis, wood_factor)
            inner_next = lax.optimization_barrier(jnp.sum(residual * precond, axis=1))
            direction = precond + (inner_next / inner_now)[:, None] * direction
            inner_now = inner_next
    return (weights, residual)
```

```python
import functools

import jax
import jax.numpy as jnp
from jax import lax
from jax.experimental import pallas as pl
from jax.experimental.pallas import tpu as pltpu
from jax.sharding import PartitionSpec as P

support_radius = 0.8
noise_variance = 1.0
sketch_shift = 1.0
HIGHEST = lax.Precision.HIGHEST
POINT_AXES = ("blk", "leaf")
TILE = 128


def mm(left, right):
    return jnp.dot(left, right, precision=HIGHEST, preferred_element_type=jnp.float32)


def mm_t(left, right):
    return lax.dot_general(
        left, right, (((1,), (1,)), ((), ())), precision=HIGHEST, preferred_element_type=jnp.float32
    )


def reciprocal(value):
    guess = pl.reciprocal(value, approx=True)
    guess = guess * (2.0 - value * guess)
    return guess * (2.0 - value * guess)


def small_inverse(entries, size):
    def at(table, a, b):
        return table[(min(a, b), max(a, b))]

    if size == 1:
        return {(0, 0): reciprocal(entries[(0, 0)])}
    if size == 2:
        det = entries[(0, 0)] * entries[(1, 1)] - entries[(0, 1)] * entries[(0, 1)]
        inv = reciprocal(det)
        return {(0, 0): entries[(1, 1)] * inv, (1, 1): entries[(0, 0)] * inv, (0, 1): -entries[(0, 1)] * inv}
    half = size // 2
    idx = range(half)
    upper = [(a, b) for a in idx for b in range(a, half)]
    first = small_inverse({(a, b): entries[(a, b)] for a, b in upper}, half)
    cross = [[entries[(a, half + b)] for b in idx] for a in idx]
    lift = [[sum(at(first, a, c) * cross[c][b] for c in idx) for b in idx] for a in idx]
    schur = {
        (a, b): entries[(half + a, half + b)] - sum(cross[c][a] * lift[c][b] for c in idx) for a, b in upper
    }
    last = small_inverse(schur, half)
    mixed = [[sum(lift[a][c] * at(last, c, b) for c in idx) for b in idx] for a in idx]
    result = {}
    for a, b in upper:
        result[(half + a, half + b)] = last[(a, b)]
        result[(a, b)] = first[(a, b)] + sum(mixed[a][c] * lift[b][c] for c in idx)
    for a in idx:
        for b in idx:
            result[(a, half + b)] = -mixed[a][b]
    return result


def block_inverse(matrix, pivot):
    size = matrix.shape[0]
    lane = lax.broadcasted_iota(jnp.int32, (8, size), 1)
    sub = lax.broadcasted_iota(jnp.int32, (8, size), 0)
    parts = [matrix[8 * i : 8 * i + 8, :] for i in range(size // 8)]
    for k in range(0, size, pivot):
        home, first = k // 8, k % 8
        rows = [jnp.broadcast_to(parts[home][first + a : first + a + 1, :], (8, size)) for a in range(pivot)]
        entries = {
            (a, b): jnp.broadcast_to(rows[a][:, k + b : k + b + 1], (8, size))
            for a in range(pivot)
            for b in range(a, pivot)
        }
        inverse = small_inverse(entries, pivot)
        here = (lane >= k) & (lane < k + pivot)
        rows = [jnp.where(here, jnp.where(lane == k + a, 1.0, 0.0), rows[a]) for a in range(pivot)]
        scaled = [
            sum(inverse[(min(a, b), max(a, b))] * rows[b] for b in range(pivot)) for a in range(pivot)
        ]
        updated = []
        for i, part in enumerate(parts):
            columns = [jnp.broadcast_to(part[:, k + a : k + a + 1], (8, size)) for a in range(pivot)]
            base = jnp.where(here, 0.0, part)
            if i == home:
                inside = (sub >= first) & (sub < first + pivot)
                base = jnp.where(inside, 0.0, base)
                columns = [
                    jnp.where(inside, jnp.where(sub == first + a, -1.0, 0.0), column)
                    for a, column in enumerate(columns)
                ]
            taken = columns[0] * scaled[0]
            for a in range(1, pivot):
                taken = taken + columns[a] * scaled[a]
            updated.append(base - taken)
        parts = updated
    return jnp.concatenate(parts, axis=0)


def inverse_kernel(first_ref, second_ref, rhs_ref, system_ref, inverse_ref, solved_ref, *, pivot):
    half = system_ref.shape[0] // 2
    count = half // TILE

    def put(row, column, block):
        system_ref[row : row + TILE, column : column + TILE] = block

    for ref, corner in ((first_ref, 0), (second_ref, half)):
        at = 0
        for i in range(count):
            for j in range(i, count):
                block = ref[at : at + TILE, :]
                at += TILE
                if i == j:
                    put(corner + i * TILE, corner + i * TILE, 0.5 * (block + block.T))
                else:
                    put(corner + i * TILE, corner + j * TILE, block)
                    put(corner + j * TILE, corner + i * TILE, block.T)
    share = count // 2
    for ref, begin in ((first_ref, 0), (second_ref, share)):
        at = count * (count + 1) // 2 * TILE
        for j in range(begin, begin + share):
            for i in range(count):
                block = ref[at : at + TILE, :]
                at += TILE
                put(i * TILE, half + j * TILE, block)
                put(half + j * TILE, i * TILE, block.T)

    size = system_ref.shape[0]
    inverse_ref[...] = system_ref[...]
    for k in range(0, size, TILE):
        own = slice(k, k + TILE)
        block = block_inverse(inverse_ref[own, own], pivot)
        row_id = lax.broadcasted_iota(jnp.int32, (TILE, TILE), 0)
        column_id = lax.broadcasted_iota(jnp.int32, (TILE, TILE), 1)
        inverse_ref[own, own] = jnp.where(row_id == column_id, 1.0, 0.0)
        scaled = mm(block, inverse_ref[own, :])
        for i in range(0, size, TILE):
            if i != k:
                other = slice(i, i + TILE)
                column = inverse_ref[other, own]
                inverse_ref[other, own] = jnp.zeros((TILE, TILE), jnp.float32)
                inverse_ref[other, :] = inverse_ref[other, :] - mm(column, scaled)
        inverse_ref[own, :] = scaled
    solved_ref[...] = refined_solve(system_ref[...], inverse_ref[...], rhs_ref[...])


def refined_solve(system, inverse, rhs):
    guess = mm(rhs, inverse)
    return guess + mm(rhs - mm(guess, system), inverse)


def inverse_and_solve(first, second, rhs):
    size = rhs.shape[1]
    vmem = pl.BlockSpec(memory_space=pltpu.VMEM)
    matrix = jax.ShapeDtypeStruct((size, size), jnp.float32)
    return pl.pallas_call(
        functools.partial(inverse_kernel, pivot=4),
        out_shape=(matrix, matrix, jax.ShapeDtypeStruct(rhs.shape, jnp.float32)),
        in_specs=[vmem] * 3,
        out_specs=(vmem,) * 3,
        name="inverse_and_solve",
        compiler_params=pltpu.CompilerParams(vmem_limit_bytes=32 * 2**20),
        cost_estimate=pl.CostEstimate(flops=40 * 10**9, bytes_accessed=4 * 2**20, transcendentals=0),
    )(first, second, rhs)


def shifted(values, axis, distance):
    size = lax.axis_size(axis)
    return lax.ppermute(values, axis, [(i, (i + distance) % size) for i in range(size)])


def swapped(values, axis, mask):
    size = lax.axis_size(axis)
    return lax.ppermute(values, axis, [(i, i ^ mask) for i in range(size)])


def slab(values):
    return [values] + [swapped(values, "leaf", m) for m in range(1, lax.axis_size("leaf"))]


def group_size():
    return lax.axis_size(POINT_AXES)


def exchange(values):
    return lax.all_to_all(values, POINT_AXES, 0, 0, tiled=True)


def share_sum(values):
    count = group_size()
    return exchange(values).reshape(count, values.shape[0] // count, values.shape[1]).sum(axis=0)


def spread(values):
    count = group_size()
    sent = jnp.broadcast_to(values[None], (count,) + values.shape).reshape(-1, values.shape[1])
    return exchange(sent).reshape((count,) + values.shape)


def to_tiles(values):
    return jnp.concatenate([values[:, c : c + TILE] for c in range(0, values.shape[1], TILE)], axis=0)


def from_tiles(tiles, rows):
    return jnp.concatenate([tiles[r : r + rows] for r in range(0, tiles.shape[0], rows)], axis=1)


def dot_rows(left, right):
    return jnp.sum(left * right, axis=1)


def local(points, neighbors, omega, observed, prior_draws):
    cycle = lax.axis_size("blk")
    leaves = lax.axis_size("leaf")
    cores = lax.axis_size("samp")
    own_slab, own_leaf, own_core = (lax.axis_index(a) for a in ("blk", "leaf", "samp"))
    sketch_size, width = omega.shape
    half = sketch_size // cores
    samples = prior_draws.shape[0]
    period = 2.0 * cycle
    first_core = own_core == 0

    rhs = observed[None, :] - prior_draws
    omega_half = lax.dynamic_slice_in_dim(omega, own_core * half, half, axis=0)
    listed = jnp.pad(neighbors.astype(jnp.float32), ((0, 0), (0, width - neighbors.shape[1])))
    meta = jnp.concatenate([points, listed, jnp.zeros((4, width), jnp.float32)], axis=0)

    above, below = shifted(meta, "blk", -1), shifted(meta, "blk", 1)
    metas = slab(meta)
    sources = jnp.concatenate([m[:3] for m in metas], axis=1)
    targets = [above, meta, below]
    source_ids = own_slab * leaves + jnp.stack([own_leaf ^ m for m in range(leaves)])
    target_lists = jnp.stack([t[3, : neighbors.shape[1]] for t in targets])
    usable = (target_lists[None] == source_ids[:, None, None].astype(jnp.float32)).astype(jnp.float32).sum(axis=2)

    def kernel_columns(index):
        offset = sources[:, :, None] - targets[index][:3, None, :]
        along = offset[0]
        along = jnp.where(along >= 0.5 * period, along - period, along)
        along = jnp.where(along < -0.5 * period, along + period, along)
        squared = along * along + offset[1] * offset[1] + offset[2] * offset[2]
        radius = jnp.sqrt(squared) / support_radius
        remain = jnp.maximum(1.0 - radius, 0.0)
        squared_remain = remain * remain
        values = squared_remain * squared_remain * (4.0 * radius + 1.0)
        weight = jnp.repeat(usable[:, index], width)
        return values * weight[:, None]

    columns = [kernel_columns(i) for i in range(3)]

    def apply_kernel(values):
        gathered = jnp.concatenate(slab(values), axis=1)
        from_below = shifted(mm(gathered, columns[0]), "blk", 1)
        from_above = shifted(mm(gathered, columns[2]), "blk", -1)
        return mm(gathered, columns[1]) + from_below + from_above

    def both_halves(values):
        other = swapped(values, "samp", 1)
        return jnp.where(
            first_core,
            jnp.concatenate([values, other], axis=0),
            jnp.concatenate([other, values], axis=0),
        ), other

    applied = apply_kernel(jnp.concatenate([omega_half, rhs], axis=0))
    sketch_half = applied[:half] + sketch_shift * omega_half
    image_rhs = applied[half:] + noise_variance * rhs
    sketch, sketch_other = both_halves(sketch_half)

    lifted_half = omega_half + sketch_half
    count = half // TILE
    split = half // 2
    corner = mm_t(lifted_half, sketch_half)
    left = jnp.where(first_core, lifted_half, sketch_other)
    right = jnp.where(first_core, sketch_other[:split], lifted_half[split:])
    cross = mm_t(left, right)
    projected = mm_t(rhs, sketch)
    pieces = [corner[i * TILE : (i + 1) * TILE, j * TILE : (j + 1) * TILE] for i in range(count) for j in range(i, count)]
    payload = jnp.concatenate(pieces + [to_tiles(cross), to_tiles(projected)], axis=0)
    reduced = spread(share_sum(payload)).reshape(payload.shape)
    matrix_rows = payload.shape[0] - samples * (sketch_size // TILE)
    own_share = reduced[:matrix_rows]
    projected = from_tiles(reduced[matrix_rows:], samples)
    other_share = swapped(own_share, "samp", 1)
    system, inverse, solved = inverse_and_solve(
        jnp.where(first_core, own_share, other_share), jnp.where(first_core, other_share, own_share), projected
    )

    image_sketch_half = apply_kernel(sketch_half) + noise_variance * sketch_half
    image_sketch, _ = both_halves(image_sketch_half)

    direction = (rhs - mm(solved, sketch)) / noise_variance
    image = (image_rhs - mm(solved, image_sketch)) / noise_variance
    image_twice = apply_kernel(image) + noise_variance * image
    moved_share = share_sum(to_tiles(mm_t(image, sketch)))
    dots = jnp.stack([dot_rows(rhs, direction), dot_rows(direction, image)])
    dots = jnp.pad(dots, ((0, 6), (0, TILE - samples)))
    arrived = spread(jnp.concatenate([moved_share, dots], axis=0))
    rows = moved_share.shape[0]
    moved = from_tiles(arrived[:, :rows].reshape(-1, TILE), samples)
    dots = arrived[:, rows:].sum(axis=0)
    inner_first, curvature = dots[0, :samples, None], dots[1, :samples, None]
    step = inner_first / curvature
    residual = rhs - step * image

    solved = refined_solve(system, inverse, projected - step * moved)
    precond = (residual - mm(solved, sketch)) / noise_variance
    image_precond = (image_rhs - step * image_twice - mm(solved, image_sketch)) / noise_variance
    dots = jnp.stack([dot_rows(residual, precond), dot_rows(precond, image_precond), dot_rows(precond, image)])
    dots = spread(jnp.pad(dots, ((0, 5), (0, TILE - samples)))).sum(axis=0)
    inner_second, curvature_precond, mixed = (dots[i, :samples, None] for i in range(3))
    beta = inner_second / inner_first
    step_second = inner_second / (curvature_precond + beta * (2.0 * mixed + beta * curvature))
    weights = step * direction + step_second * (precond + beta * direction)
    residual = residual - step_second * (image_precond + beta * image)
    return (weights, residual)


def solution(mesh):
    in_specs = (
        P(None, ("blk", "leaf")),
        P(("blk", "leaf"), None),
        P(None, ("blk", "leaf")),
        P(("blk", "leaf")),
        P("samp", ("blk", "leaf")),
    )
    out_specs = (P("samp", ("blk", "leaf")), P("samp", ("blk", "leaf")))
    return jax.shard_map(local, mesh=mesh, in_specs=in_specs, out_specs=out_specs, check_vma=False)
```

```python
import jax
import jax.numpy as jnp
from jax import lax
from jax.experimental import pallas as pl
from jax.experimental.pallas import tpu as pltpu
from jax.sharding import PartitionSpec as P

support_radius = 0.8
noise_variance = 1.0
sketch_shift = 1.0
HIGHEST = lax.Precision.HIGHEST
POINT_AXES = ("blk", "leaf")
TILE = 128
PIVOT, BASE, AHEAD, REFINES = 8, 128, False, 1


def mm(left, right):
    return jnp.dot(left, right, precision=HIGHEST, preferred_element_type=jnp.float32)


def rough_mm(left, right):
    return jnp.dot(left, right, preferred_element_type=jnp.float32)


def mm_t(left, right):
    return lax.dot_general(
        left, right, (((1,), (1,)), ((), ())), precision=HIGHEST, preferred_element_type=jnp.float32
    )


def tree_sum(terms):
    terms = list(terms)
    while len(terms) > 1:
        terms = [
            terms[i] + terms[i + 1] if i + 1 < len(terms) else terms[i] for i in range(0, len(terms), 2)
        ]
    return terms[0]


def reciprocal(value):
    guess = pl.reciprocal(value, approx=True)
    for _ in range(REFINES):
        guess = guess * (2.0 - value * guess)
    return guess


def small_inverse(entries, size):
    def at(table, a, b):
        return table[(min(a, b), max(a, b))]

    if size == 1:
        return {(0, 0): reciprocal(entries[(0, 0)])}
    if size == 2:
        det = entries[(0, 0)] * entries[(1, 1)] - entries[(0, 1)] * entries[(0, 1)]
        inv = reciprocal(det)
        return {(0, 0): entries[(1, 1)] * inv, (1, 1): entries[(0, 0)] * inv, (0, 1): -entries[(0, 1)] * inv}
    half = size // 2
    idx = range(half)
    upper = [(a, b) for a in idx for b in range(a, half)]
    first = small_inverse({(a, b): entries[(a, b)] for a, b in upper}, half)
    cross = [[entries[(a, half + b)] for b in idx] for a in idx]
    lift = [[tree_sum(at(first, a, c) * cross[c][b] for c in idx) for b in idx] for a in idx]
    schur = {
        (a, b): entries[(half + a, half + b)] - tree_sum(cross[c][a] * lift[c][b] for c in idx)
        for a, b in upper
    }
    last = small_inverse(schur, half)
    mixed = [[tree_sum(lift[a][c] * at(last, c, b) for c in idx) for b in idx] for a in idx]
    result = {}
    for a, b in upper:
        result[(half + a, half + b)] = last[(a, b)]
        result[(a, b)] = first[(a, b)] + tree_sum(mixed[a][c] * lift[b][c] for c in idx)
    for a in idx:
        for b in idx:
            result[(a, half + b)] = -mixed[a][b]
    return result


def pivot_inverse(matrix):
    size = matrix.shape[0]
    lane = lax.broadcasted_iota(jnp.int32, (8, size), 1)
    sub = lax.broadcasted_iota(jnp.int32, (8, size), 0)
    parts = [matrix[8 * i : 8 * i + 8, :] for i in range(size // 8)]
    idx = range(PIVOT)
    upper = [(a, b) for a in idx for b in range(a, PIVOT)]

    def row(r):
        return jnp.broadcast_to(parts[r // 8][r % 8 : r % 8 + 1, :], (8, size))

    def entry(values, c):
        return jnp.broadcast_to(values[:, c : c + 1], (8, size))

    entries = None
    for k in range(0, size, PIVOT):
        home, first = k // 8, k % 8
        rows = [row(k + a) for a in idx]
        if entries is None:
            entries = {(a, b): entry(rows[a], k + b) for a, b in upper}
        ahead = AHEAD and k + PIVOT < size
        if ahead:
            later = k + PIVOT
            side = [[entry(rows[a], later + b) for b in idx] for a in idx]
            later_rows = [row(later + a) for a in idx]
            later_entries = {(a, b): entry(later_rows[a], later + b) for a, b in upper}
        inverse = small_inverse(entries, PIVOT)
        full = [[inverse[(min(a, b), max(a, b))] for b in idx] for a in idx]
        entries = None
        if ahead:
            lift = [[tree_sum(full[a][c] * side[c][b] for c in idx) for b in idx] for a in idx]
            entries = {
                (a, b): later_entries[(a, b)] - tree_sum(side[c][a] * lift[c][b] for c in idx)
                for a, b in upper
            }
        here = (lane >= k) & (lane < k + PIVOT)
        rows = [jnp.where(here, jnp.where(lane == k + a, 1.0, 0.0), rows[a]) for a in idx]
        scaled = [tree_sum(full[a][b] * rows[b] for b in idx) for a in idx]
        updated = []
        for i, part in enumerate(parts):
            columns = [entry(part, k + a) for a in idx]
            base = jnp.where(here, 0.0, part)
            if i == home:
                inside = (sub >= first) & (sub < first + PIVOT)
                base = jnp.where(inside, 0.0, base)
                columns = [
                    jnp.where(inside, jnp.where(sub == first + a, -1.0, 0.0), column)
                    for a, column in enumerate(columns)
                ]
            updated.append(base - tree_sum(columns[a] * scaled[a] for a in idx))
        parts = updated
    return jnp.concatenate(parts, axis=0)


def block_inverse(matrix):
    size = matrix.shape[0]
    if size <= BASE:
        return pivot_inverse(matrix)
    half = size // 2
    corner, side = matrix[:half, :half], matrix[:half, half:]
    first = block_inverse(corner)
    lift = mm(first, side)
    last = block_inverse(matrix[half:, half:] - mm(side.T, lift))
    mixed = mm(lift, last)
    top = jnp.concatenate([first + mm(mixed, lift.T), -mixed], axis=1)
    return jnp.concatenate([top, jnp.concatenate([-mixed.T, last], axis=1)], axis=0)


def assemble(first_ref, second_ref, system_ref):
    half = system_ref.shape[0] // 2
    count = half // TILE

    def put(row, column, block):
        system_ref[row : row + TILE, column : column + TILE] = block

    for ref, corner in ((first_ref, 0), (second_ref, half)):
        at = 0
        for i in range(count):
            for j in range(i, count):
                block = ref[at : at + TILE, :]
                at += TILE
                if i == j:
                    put(corner + i * TILE, corner + i * TILE, 0.5 * (block + block.T))
                else:
                    put(corner + i * TILE, corner + j * TILE, block)
                    put(corner + j * TILE, corner + i * TILE, block.T)
    share = count // 2
    for ref, begin in ((first_ref, 0), (second_ref, share)):
        at = count * (count + 1) // 2 * TILE
        for j in range(begin, begin + share):
            for i in range(count):
                block = ref[at : at + TILE, :]
                at += TILE
                put(i * TILE, half + j * TILE, block)
                put(half + j * TILE, i * TILE, block.T)


def eliminate(inverse_ref, begin, end):
    size = inverse_ref.shape[0]
    row_id = lax.broadcasted_iota(jnp.int32, (TILE, TILE), 0)
    column_id = lax.broadcasted_iota(jnp.int32, (TILE, TILE), 1)
    for k in range(begin, end, TILE):
        own = slice(k, k + TILE)
        block = block_inverse(inverse_ref[own, own])
        inverse_ref[own, own] = jnp.where(row_id == column_id, 1.0, 0.0)
        scaled = mm(block, inverse_ref[own, :])
        for i in range(0, size, TILE):
            if i != k:
                other = slice(i, i + TILE)
                column = inverse_ref[other, own]
                inverse_ref[other, own] = jnp.zeros((TILE, TILE), jnp.float32)
                inverse_ref[other, :] = inverse_ref[other, :] - mm(column, scaled)
        inverse_ref[own, :] = scaled


def inverse_kernel(first_ref, second_ref, rhs_ref, system_ref, inverse_ref, solved_ref):
    assemble(first_ref, second_ref, system_ref)
    inverse_ref[...] = system_ref[...]
    eliminate(inverse_ref, 0, system_ref.shape[0])
    guess = mm(rhs_ref[...], inverse_ref[...])
    solved_ref[...] = guess + rough_mm(rhs_ref[...] - mm(guess, system_ref[...]), inverse_ref[...])


def kernel_call(kernel, name, outputs, *operands):
    vmem = pl.BlockSpec(memory_space=pltpu.VMEM)
    return pl.pallas_call(
        kernel,
        out_shape=tuple(jax.ShapeDtypeStruct(shape, jnp.float32) for shape in outputs),
        in_specs=[vmem] * len(operands),
        out_specs=(vmem,) * len(outputs),
        name=name,
        compiler_params=pltpu.CompilerParams(vmem_limit_bytes=32 * 2**20),
        cost_estimate=pl.CostEstimate(flops=20 * 10**9, bytes_accessed=4 * 2**20, transcendentals=0),
    )(*operands)


def shifted(values, axis, distance):
    size = lax.axis_size(axis)
    return lax.ppermute(values, axis, [(i, (i + distance) % size) for i in range(size)])


def swapped(values, axis, mask):
    size = lax.axis_size(axis)
    return lax.ppermute(values, axis, [(i, i ^ mask) for i in range(size)])


def slab(values):
    return [values] + [swapped(values, "leaf", m) for m in range(1, lax.axis_size("leaf"))]


def group_size():
    return lax.axis_size(POINT_AXES)


def exchange(values):
    return lax.all_to_all(values, POINT_AXES, 0, 0, tiled=True)


def share_sum(values):
    count = group_size()
    return exchange(values).reshape(count, values.shape[0] // count, values.shape[1]).sum(axis=0)


def spread(values):
    count = group_size()
    sent = jnp.broadcast_to(values[None], (count,) + values.shape).reshape(-1, values.shape[1])
    return exchange(sent).reshape((count,) + values.shape)


def to_tiles(values):
    return jnp.concatenate([values[:, c : c + TILE] for c in range(0, values.shape[1], TILE)], axis=0)


def from_tiles(tiles, rows):
    return jnp.concatenate([tiles[r : r + rows] for r in range(0, tiles.shape[0], rows)], axis=1)


def dot_rows(left, right):
    return jnp.sum(left * right, axis=1)


def local(points, neighbors, omega, observed, prior_draws):
    cycle = lax.axis_size("blk")
    leaves = lax.axis_size("leaf")
    cores = lax.axis_size("samp")
    own_slab, own_leaf, own_core = (lax.axis_index(a) for a in ("blk", "leaf", "samp"))
    sketch_size, width = omega.shape
    half = sketch_size // cores
    samples = prior_draws.shape[0]
    period = 2.0 * cycle
    first_core = own_core == 0

    rhs = observed[None, :] - prior_draws
    omega_half = lax.dynamic_slice_in_dim(omega, own_core * half, half, axis=0)
    listed = jnp.pad(neighbors.astype(jnp.float32), ((0, 0), (0, width - neighbors.shape[1])))
    meta = jnp.concatenate([points, listed, jnp.zeros((4, width), jnp.float32)], axis=0)

    blocks = slab(jnp.concatenate([omega_half, rhs, meta], axis=0))
    metas = [block[half + samples :] for block in blocks]

    above, below = shifted(meta, "blk", -1), shifted(meta, "blk", 1)
    sources = jnp.concatenate([m[:3] for m in metas], axis=1)
    targets = [above, meta, below]
    source_ids = own_slab * leaves + jnp.stack([own_leaf ^ m for m in range(leaves)])
    target_lists = jnp.stack([t[3, : neighbors.shape[1]] for t in targets])
    usable = (target_lists[None] == source_ids[:, None, None].astype(jnp.float32)).astype(jnp.float32).sum(axis=2)

    def kernel_columns(index):
        offset = sources[:, :, None] - targets[index][:3, None, :]
        along = offset[0]
        along = jnp.where(along >= 0.5 * period, along - period, along)
        along = jnp.where(along < -0.5 * period, along + period, along)
        squared = along * along + offset[1] * offset[1] + offset[2] * offset[2]
        radius = jnp.sqrt(squared) / support_radius
        remain = jnp.maximum(1.0 - radius, 0.0)
        squared_remain = remain * remain
        values = squared_remain * squared_remain * (4.0 * radius + 1.0)
        weight = jnp.repeat(usable[:, index], width)
        return values * weight[:, None]

    columns = [kernel_columns(i) for i in range(3)]

    def partial_sums(gathered):
        return mm(gathered, columns[0]), mm(gathered, columns[2])

    def collect(gathered, upward, downward):
        return mm(gathered, columns[1]) + shifted(upward, "blk", 1) + shifted(downward, "blk", -1)

    def apply_kernel(values):
        gathered = jnp.concatenate(slab(values), axis=1)
        return collect(gathered, *partial_sums(gathered))

    def both_halves(values):
        other = swapped(values, "samp", 1)
        return jnp.where(
            first_core,
            jnp.concatenate([values, other], axis=0),
            jnp.concatenate([other, values], axis=0),
        ), other

    gathered = jnp.concatenate([block[: half + samples] for block in blocks], axis=1)
    applied = collect(gathered, *partial_sums(gathered))
    sketch_half = applied[:half] + sketch_shift * omega_half
    image_rhs = applied[half:] + noise_variance * rhs
    sketch, sketch_other = both_halves(sketch_half)

    lifted_half = noise_variance * omega_half + sketch_half
    count = half // TILE
    split = half // 2
    corner = mm_t(lifted_half, sketch_half)
    left = jnp.where(first_core, lifted_half, sketch_other)
    right = jnp.where(first_core, sketch_other[:split], lifted_half[split:])
    cross = mm_t(left, right)
    projected = mm_t(rhs, sketch)
    pieces = [corner[i * TILE : (i + 1) * TILE, j * TILE : (j + 1) * TILE] for i in range(count) for j in range(i, count)]
    payload = jnp.concatenate(pieces + [to_tiles(cross), to_tiles(projected)], axis=0)
    payload, late_sketch = lax.optimization_barrier((payload, sketch_half))
    gathered = jnp.concatenate(slab(late_sketch), axis=1)
    reduced = spread(share_sum(payload)).reshape(payload.shape)
    matrix_rows = payload.shape[0] - samples * (sketch_size // TILE)
    projected = from_tiles(reduced[matrix_rows:], samples)
    own_share = reduced[:matrix_rows]
    other_share = swapped(own_share, "samp", 1)

    upward, downward = partial_sums(gathered)
    here = mm(gathered, columns[1]) + noise_variance * sketch_half
    own_share, projected, upward, downward = lax.optimization_barrier((own_share, projected, upward, downward))
    from_below, from_above = shifted(upward, "blk", 1), shifted(downward, "blk", -1)
    system, inverse, solved = kernel_call(
        inverse_kernel,
        "inverse_and_solve",
        [(sketch_size, sketch_size)] * 2 + [(samples, sketch_size)],
        jnp.where(first_core, own_share, other_share),
        jnp.where(first_core, other_share, own_share),
        projected,
    )
    from_below, from_above, solved = lax.optimization_barrier((from_below, from_above, solved))
    image_sketch, _ = both_halves(here + from_below + from_above)
    sketches = jnp.concatenate([sketch, image_sketch], axis=1)

    taken = mm(solved, sketches)
    direction = (rhs - taken[:, :width]) / noise_variance
    image = (image_rhs - taken[:, width:]) / noise_variance
    moved = to_tiles(mm_t(image, sketch))
    moved, late_image = lax.optimization_barrier((moved, image))
    image_twice = apply_kernel(late_image) + noise_variance * late_image
    moved_share = share_sum(moved)
    dots = jnp.stack([dot_rows(rhs, direction), dot_rows(direction, image)])
    dots = jnp.pad(dots, ((0, 6), (0, TILE - samples)))
    arrived = spread(jnp.concatenate([moved_share, dots], axis=0))
    rows = moved_share.shape[0]
    moved = from_tiles(arrived[:, :rows].reshape(-1, TILE), samples)
    dots = arrived[:, rows:].sum(axis=0)
    inner_first, curvature = dots[0, :samples, None], dots[1, :samples, None]
    step = inner_first / curvature

    solves = mm(inverse, sketches)
    solves = solves + rough_mm(inverse, sketches - mm(system, solves))

    taken = mm(moved, solves)
    precond = direction - step * ((image - taken[:, :width]) / noise_variance)
    image_precond = image - step * ((image_twice - taken[:, width:]) / noise_variance)
    residual = rhs - step * image
    dots = jnp.stack([dot_rows(residual, precond), dot_rows(precond, image_precond), dot_rows(precond, image)])
    dots = spread(jnp.pad(dots, ((0, 5), (0, TILE - samples)))).sum(axis=0)
    inner_second, curvature_precond, mixed = (dots[i, :samples, None] for i in range(3))
    beta = inner_second / inner_first
    step_second = inner_second / (curvature_precond + beta * (2.0 * mixed + beta * curvature))
    weights = step * direction + step_second * (precond + beta * direction)
    residual = residual - step_second * (image_precond + beta * image)
    return (weights, residual)


def solution(mesh):
    in_specs = (
        P(None, ("blk", "leaf")),
        P(("blk", "leaf"), None),
        P(None, ("blk", "leaf")),
        P(("blk", "leaf")),
        P("samp", ("blk", "leaf")),
    )
    out_specs = (P("samp", ("blk", "leaf")), P("samp", ("blk", "leaf")))
    return jax.shard_map(local, mesh=mesh, in_specs=in_specs, out_specs=out_specs, check_vma=False)
```

```python
import functools

import jax
import jax.numpy as jnp
from jax import lax
from jax.experimental import pallas as pl
from jax.experimental.pallas import tpu as pltpu
from jax.sharding import PartitionSpec as P

support_radius = 0.8
noise_variance = 1.0
sketch_shift = 1.0
HIGHEST = lax.Precision.HIGHEST
POINT_AXES = ("blk", "leaf")
TILE = 128
PIVOT, BASE, AHEAD, REFINES = 8, 128, False, 1


def mm(left, right):
    return jnp.dot(left, right, precision=HIGHEST, preferred_element_type=jnp.float32)


def rough_mm(left, right):
    return jnp.dot(left, right, preferred_element_type=jnp.float32)


def mm_t(left, right):
    return lax.dot_general(
        left, right, (((1,), (1,)), ((), ())), precision=HIGHEST, preferred_element_type=jnp.float32
    )


def tree_sum(terms):
    terms = list(terms)
    while len(terms) > 1:
        terms = [
            terms[i] + terms[i + 1] if i + 1 < len(terms) else terms[i] for i in range(0, len(terms), 2)
        ]
    return terms[0]


def reciprocal(value):
    guess = pl.reciprocal(value, approx=True)
    for _ in range(REFINES):
        guess = guess * (2.0 - value * guess)
    return guess


def small_inverse(entries, size):
    def at(table, a, b):
        return table[(min(a, b), max(a, b))]

    if size == 1:
        return {(0, 0): reciprocal(entries[(0, 0)])}
    if size == 2:
        det = entries[(0, 0)] * entries[(1, 1)] - entries[(0, 1)] * entries[(0, 1)]
        inv = reciprocal(det)
        return {(0, 0): entries[(1, 1)] * inv, (1, 1): entries[(0, 0)] * inv, (0, 1): -entries[(0, 1)] * inv}
    half = size // 2
    idx = range(half)
    upper = [(a, b) for a in idx for b in range(a, half)]
    first = small_inverse({(a, b): entries[(a, b)] for a, b in upper}, half)
    cross = [[entries[(a, half + b)] for b in idx] for a in idx]
    lift = [[tree_sum(at(first, a, c) * cross[c][b] for c in idx) for b in idx] for a in idx]
    schur = {
        (a, b): entries[(half + a, half + b)] - tree_sum(cross[c][a] * lift[c][b] for c in idx)
        for a, b in upper
    }
    last = small_inverse(schur, half)
    mixed = [[tree_sum(lift[a][c] * at(last, c, b) for c in idx) for b in idx] for a in idx]
    result = {}
    for a, b in upper:
        result[(half + a, half + b)] = last[(a, b)]
        result[(a, b)] = first[(a, b)] + tree_sum(mixed[a][c] * lift[b][c] for c in idx)
    for a in idx:
        for b in idx:
            result[(a, half + b)] = -mixed[a][b]
    return result


def pivot_inverse(matrix):
    size = matrix.shape[0]
    lane = lax.broadcasted_iota(jnp.int32, (8, size), 1)
    sub = lax.broadcasted_iota(jnp.int32, (8, size), 0)
    parts = [matrix[8 * i : 8 * i + 8, :] for i in range(size // 8)]
    idx = range(PIVOT)
    upper = [(a, b) for a in idx for b in range(a, PIVOT)]

    def row(r):
        return jnp.broadcast_to(parts[r // 8][r % 8 : r % 8 + 1, :], (8, size))

    def entry(values, c):
        return jnp.broadcast_to(values[:, c : c + 1], (8, size))

    entries = None
    for k in range(0, size, PIVOT):
        home, first = k // 8, k % 8
        rows = [row(k + a) for a in idx]
        if entries is None:
            entries = {(a, b): entry(rows[a], k + b) for a, b in upper}
        ahead = AHEAD and k + PIVOT < size
        if ahead:
            later = k + PIVOT
            side = [[entry(rows[a], later + b) for b in idx] for a in idx]
            later_rows = [row(later + a) for a in idx]
            later_entries = {(a, b): entry(later_rows[a], later + b) for a, b in upper}
        inverse = small_inverse(entries, PIVOT)
        full = [[inverse[(min(a, b), max(a, b))] for b in idx] for a in idx]
        entries = None
        if ahead:
            lift = [[tree_sum(full[a][c] * side[c][b] for c in idx) for b in idx] for a in idx]
            entries = {
                (a, b): later_entries[(a, b)] - tree_sum(side[c][a] * lift[c][b] for c in idx)
                for a, b in upper
            }
        here = (lane >= k) & (lane < k + PIVOT)
        rows = [jnp.where(here, jnp.where(lane == k + a, 1.0, 0.0), rows[a]) for a in idx]
        scaled = [tree_sum(full[a][b] * rows[b] for b in idx) for a in idx]
        updated = []
        for i, part in enumerate(parts):
            columns = [entry(part, k + a) for a in idx]
            base = jnp.where(here, 0.0, part)
            if i == home:
                inside = (sub >= first) & (sub < first + PIVOT)
                base = jnp.where(inside, 0.0, base)
                columns = [
                    jnp.where(inside, jnp.where(sub == first + a, -1.0, 0.0), column)
                    for a, column in enumerate(columns)
                ]
            updated.append(base - tree_sum(columns[a] * scaled[a] for a in idx))
        parts = updated
    return jnp.concatenate(parts, axis=0)


def block_inverse(matrix):
    size = matrix.shape[0]
    if size <= BASE:
        return pivot_inverse(matrix)
    half = size // 2
    corner, side = matrix[:half, :half], matrix[:half, half:]
    first = block_inverse(corner)
    lift = mm(first, side)
    last = block_inverse(matrix[half:, half:] - mm(side.T, lift))
    mixed = mm(lift, last)
    top = jnp.concatenate([first + mm(mixed, lift.T), -mixed], axis=1)
    return jnp.concatenate([top, jnp.concatenate([-mixed.T, last], axis=1)], axis=0)


def assemble(core_ref, own_ref, other_ref, system_ref):
    half = system_ref.shape[0] // 2
    count = half // TILE

    def put(row, column, block):
        system_ref[row : row + TILE, column : column + TILE] = block

    flag = jnp.zeros((TILE, TILE), jnp.int32) + core_ref[0] == 0

    def tile(at, share):
        own, other = own_ref[at : at + TILE, :], other_ref[at : at + TILE, :]
        return jnp.where(flag, own, other) if share == 0 else jnp.where(flag, other, own)

    for share, corner in ((0, 0), (1, half)):
        at = 0
        for i in range(count):
            for j in range(i, count):
                block = tile(at, share)
                at += TILE
                if i == j:
                    put(corner + i * TILE, corner + i * TILE, 0.5 * (block + block.T))
                else:
                    put(corner + i * TILE, corner + j * TILE, block)
                    put(corner + j * TILE, corner + i * TILE, block.T)
    share_columns = count // 2
    for share in (0, 1):
        at = count * (count + 1) // 2 * TILE
        for j in range(share * share_columns, (share + 1) * share_columns):
            for i in range(count):
                block = tile(at, share)
                at += TILE
                put(i * TILE, half + j * TILE, block)
                put(half + j * TILE, i * TILE, block.T)


def eliminate(inverse_ref, begin, end):
    size = inverse_ref.shape[0]
    count = size // TILE
    row_id = lax.broadcasted_iota(jnp.int32, (TILE, TILE), 0)
    column_id = lax.broadcasted_iota(jnp.int32, (TILE, TILE), 1)

    def span(index):
        return pl.ds(pl.multiple_of(index * TILE, TILE), TILE)

    def step(k, carry):
        own = span(k)
        block = block_inverse(inverse_ref[own, own])
        inverse_ref[own, own] = jnp.where(row_id == column_id, 1.0, 0.0)
        scaled = mm(block, inverse_ref[own, :])
        inverse_ref[own, :] = scaled
        for ahead in range(1, count):
            other = span(lax.rem(k + ahead, count))
            column = inverse_ref[other, own]
            inverse_ref[other, own] = jnp.zeros((TILE, TILE), jnp.float32)
            inverse_ref[other, :] = inverse_ref[other, :] - mm(column, scaled)
        return carry

    lax.fori_loop(begin, end, step, 0)


def inverse_kernel(core_ref, own_ref, other_ref, system_ref, inverse_ref, solved_ref):
    assemble(core_ref, own_ref, other_ref, system_ref)
    inverse_ref[...] = system_ref[...]
    count = system_ref.shape[0] // TILE
    eliminate(inverse_ref, 0, count)
    samples = solved_ref.shape[0]
    begin = own_ref.shape[0] - count * samples
    rhs = jnp.concatenate(
        [own_ref[begin + i * samples : begin + (i + 1) * samples, :] for i in range(count)], axis=1
    )
    guess = mm(rhs, inverse_ref[...])
    solved_ref[...] = guess + rough_mm(rhs - mm(guess, system_ref[...]), inverse_ref[...])


def image_kernel(
    core_ref, solved_ref, sketch_ref, own_ref, other_ref, rhs_ref, image_rhs_ref,
    sketches_ref, direction_ref, image_ref, moved_ref, dots_ref,
):
    half, width = own_ref.shape
    core = core_ref[0]
    sketches_ref[:, :width] = sketch_ref[...]
    sketches_ref[pl.ds(pl.multiple_of(core * half, half), half), width:] = own_ref[...]
    sketches_ref[pl.ds(pl.multiple_of((1 - core) * half, half), half), width:] = other_ref[...]
    taken = mm(solved_ref[...], sketches_ref[...])
    rhs = rhs_ref[...]
    direction = (rhs - taken[:, :width]) / noise_variance
    image = (image_rhs_ref[...] - taken[:, width:]) / noise_variance
    direction_ref[...] = direction
    image_ref[...] = image
    moved = mm_t(image, sketch_ref[...])
    samples = rhs.shape[0]
    for i in range(moved.shape[1] // TILE):
        moved_ref[i * samples : (i + 1) * samples, :] = moved[:, i * TILE : (i + 1) * TILE]
    ones = jnp.ones((8, width), jnp.float32)
    dots_ref[...] = jnp.zeros(dots_ref.shape, jnp.float32)
    dots_ref[0:1, :samples] = mm_t(ones, rhs * direction)[0:1, :]
    dots_ref[1:2, :samples] = mm_t(ones, direction * image)[0:1, :]


def prepare_kernel(
    core_ref, points_ref, neighbors_ref, omega_ref, observed_ref, prior_ref, block_ref, meta_ref,
    points_vmem, neighbors_vmem, observed_vmem, prior_vmem, sems,
):
    samples = prior_vmem.shape[0]
    half = block_ref.shape[0] - samples - 8
    begin = pl.multiple_of(core_ref[0] * half, half)
    copies = [
        pltpu.make_async_copy(source, target, sems.at[i])
        for i, (source, target) in enumerate(
            (
                (omega_ref.at[pl.ds(begin, half), :], block_ref.at[0:half, :]),
                (points_ref, points_vmem),
                (neighbors_ref, neighbors_vmem),
                (observed_ref, observed_vmem),
                (prior_ref, prior_vmem),
            )
        )
    ]
    for copy in copies:
        copy.start()
    meta_ref[...] = jnp.full(meta_ref.shape, -1.0, jnp.float32)
    for copy in copies:
        copy.wait()
    block_ref[half : half + samples, :] = observed_vmem[...] - prior_vmem[...]
    meta_ref[0:3, :] = points_vmem[...]
    meta_ref[3:4, : neighbors_vmem.shape[1]] = neighbors_vmem[...].astype(jnp.float32)
    block_ref[half + samples :, :] = meta_ref[...]


def prepare(core, points, neighbors, omega, observed, prior, half):
    width = omega.shape[1]
    samples = prior.shape[0]
    vmem = pl.BlockSpec(memory_space=pltpu.VMEM)
    hbm = pl.BlockSpec(memory_space=pl.ANY)
    shapes = [(half + samples + 8, width), (8, width)]
    return pl.pallas_call(
        prepare_kernel,
        out_shape=tuple(jax.ShapeDtypeStruct(shape, jnp.float32) for shape in shapes),
        in_specs=[pl.BlockSpec(memory_space=pltpu.SMEM)] + [hbm] * 5,
        out_specs=(vmem, vmem),
        scratch_shapes=[
            pltpu.VMEM(points.shape, jnp.float32),
            pltpu.VMEM(neighbors.shape, jnp.int32),
            pltpu.VMEM(observed.shape, jnp.float32),
            pltpu.VMEM(prior.shape, jnp.float32),
            pltpu.SemaphoreType.DMA((5,)),
        ],
        name="prepare",
        cost_estimate=pl.CostEstimate(flops=10**9, bytes_accessed=2**19, transcendentals=0),
    )(core, points, neighbors, omega, observed, prior)


def payload_kernel(core_ref, omega_ref, own_ref, other_ref, rhs_ref, sketch_ref, payload_ref):
    half, width = own_ref.shape
    split = half // 2
    core = core_ref[0]
    begin = pl.multiple_of(core * half, half)
    sketch_ref[pl.ds(begin, half), :] = own_ref[...]
    sketch_ref[pl.ds(pl.multiple_of((1 - core) * half, half), half), :] = other_ref[...]
    own, other = own_ref[...], other_ref[...]
    lifted = noise_variance * omega_ref[...] + own
    count = half // TILE
    at = 0
    for i in range(count):
        product = mm_t(lifted[i * TILE : (i + 1) * TILE], own[i * TILE :])
        for j in range(count - i):
            payload_ref[at : at + TILE, :] = product[:, j * TILE : (j + 1) * TILE]
            at += TILE
    on_first = jnp.zeros((half, width), jnp.int32) + core == 0
    left = jnp.where(on_first, lifted, other)
    right = jnp.where(on_first[:split], other[:split], lifted[split:])
    product = mm_t(left, right)
    for j in range(split // TILE):
        payload_ref[at : at + half, :] = product[:, j * TILE : (j + 1) * TILE]
        at += half
    product = mm_t(rhs_ref[...], sketch_ref[...])
    samples = rhs_ref.shape[0]
    for j in range(2 * count):
        payload_ref[at : at + samples, :] = product[:, j * TILE : (j + 1) * TILE]
        at += samples


def kernel_call(kernel, name, outputs, *operands, blocks=(), flops=10**8):
    vmem = pl.BlockSpec(memory_space=pltpu.VMEM)
    smem = pl.BlockSpec(memory_space=pltpu.SMEM)
    scratch = []
    if blocks:
        scratch = [pltpu.VMEM((len(blocks),) + blocks[0].shape, jnp.float32), pltpu.SemaphoreType.DMA((len(blocks),))]
    return pl.pallas_call(
        kernel,
        out_shape=tuple(jax.ShapeDtypeStruct(shape, jnp.float32) for shape in outputs),
        in_specs=[smem if o.ndim == 1 else vmem for o in operands] + [pl.BlockSpec(memory_space=pltpu.HBM)] * len(blocks),
        out_specs=(vmem,) * len(outputs),
        scratch_shapes=scratch,
        name=name,
        compiler_params=pltpu.CompilerParams(vmem_limit_bytes=32 * 2**20),
        cost_estimate=pl.CostEstimate(flops=flops, bytes_accessed=2**20, transcendentals=0),
    )(*operands, *blocks)


def shifted(values, axis, distance):
    size = lax.axis_size(axis)
    return lax.ppermute(values, axis, [(i, (i + distance) % size) for i in range(size)])


def swapped(values, axis, mask):
    size = lax.axis_size(axis)
    return lax.ppermute(values, axis, [(i, i ^ mask) for i in range(size)])


def slab(values):
    return [values] + [swapped(values, "leaf", m) for m in range(1, lax.axis_size("leaf"))]


def group_size():
    return lax.axis_size(POINT_AXES)


def exchange(values):
    return lax.all_to_all(values, POINT_AXES, 0, 0, tiled=True)


def share_sum(values):
    count = group_size()
    return exchange(values).reshape(count, values.shape[0] // count, values.shape[1]).sum(axis=0)


def spread(values):
    count = group_size()
    sent = jnp.broadcast_to(values[None], (count,) + values.shape).reshape(-1, values.shape[1])
    return exchange(sent).reshape((count,) + values.shape)


def to_tiles(values):
    return jnp.concatenate([values[:, c : c + TILE] for c in range(0, values.shape[1], TILE)], axis=0)


def from_tiles(tiles, rows):
    return jnp.concatenate([tiles[r : r + rows] for r in range(0, tiles.shape[0], rows)], axis=1)


def dot_rows(left, right):
    return jnp.sum(left * right, axis=1)


def local(points, neighbors, omega, observed, prior_draws):
    cycle = lax.axis_size("blk")
    leaves = lax.axis_size("leaf")
    cores = lax.axis_size("samp")
    own_slab, own_leaf, own_core = (lax.axis_index(a) for a in ("blk", "leaf", "samp"))
    sketch_size, width = omega.shape
    half = sketch_size // cores
    samples = prior_draws.shape[0]
    period = 2.0 * cycle

    core = own_core.astype(jnp.int32).reshape(1)
    block, meta = prepare(core, points, neighbors, omega, observed[None, :], prior_draws, half)

    def other_core(values):
        return swapped(values, "samp", 1)

    def sent(upward, downward):
        return shifted(upward, "blk", 1), shifted(downward, "blk", -1)

    blocks = slab(block)
    above, below = shifted(meta, "blk", -1), shifted(meta, "blk", 1)
    sources = jnp.concatenate([b[half + samples : half + samples + 3] for b in blocks], axis=1)
    targets = [above, meta, below]
    source_ids = own_slab * leaves + jnp.stack([own_leaf ^ m for m in range(leaves)])
    target_lists = jnp.stack([t[3, : neighbors.shape[1]] for t in targets])
    usable = (target_lists[None] == source_ids[:, None, None].astype(jnp.float32)).astype(jnp.float32).sum(axis=2)

    def kernel_columns(index):
        offset = sources[:, :, None] - targets[index][:3, None, :]
        along = offset[0]
        along = jnp.where(along >= 0.5 * period, along - period, along)
        along = jnp.where(along < -0.5 * period, along + period, along)
        squared = along * along + offset[1] * offset[1] + offset[2] * offset[2]
        radius = jnp.sqrt(squared) / support_radius
        remain = jnp.maximum(1.0 - radius, 0.0)
        squared_remain = remain * remain
        values = squared_remain * squared_remain * (4.0 * radius + 1.0)
        weight = jnp.repeat(usable[:, index], width)
        return values * weight[:, None]

    columns = [kernel_columns(i) for i in range(3)]

    def sums(values):
        gathered = jnp.concatenate(values, axis=1)
        return mm(gathered, columns[0]), mm(gathered, columns[2]), gathered

    upward, downward, gathered = sums([b[: half + samples] for b in blocks])
    from_below, from_above = sent(upward, downward)
    applied = mm(gathered, columns[1]) + from_below + from_above
    omega_half, rhs = block[:half], block[half : half + samples]
    sketch_half = applied[:half] + sketch_shift * omega_half
    image_rhs = applied[half:] + noise_variance * rhs

    count = half // TILE
    matrix_rows = (count * (count + 1) // 2 + count * count // 2) * TILE
    sketch, payload = kernel_call(
        payload_kernel,
        "payload",
        [(sketch_size, width), (matrix_rows + samples * (sketch_size // TILE), TILE)],
        core,
        omega_half,
        sketch_half,
        other_core(sketch_half),
        rhs,
        flops=10**9,
    )
    payload, late_sketch = lax.optimization_barrier((payload, sketch_half))
    upward, downward, gathered = sums(slab(late_sketch))
    here = mm(gathered, columns[1]) + noise_variance * late_sketch
    reduced = spread(share_sum(payload)).reshape(payload.shape)
    other_reduced = other_core(reduced)
    reduced, upward, downward, here = lax.optimization_barrier((reduced, upward, downward, here))
    from_below, from_above = sent(upward, downward)
    system, inverse, solved = kernel_call(
        inverse_kernel,
        "inverse_and_solve",
        [(sketch_size, sketch_size)] * 2 + [(samples, sketch_size)],
        core,
        reduced,
        other_reduced,
        flops=30 * 10**9,
    )
    from_below, from_above, solved = lax.optimization_barrier((from_below, from_above, solved))
    own_image = here + from_below + from_above

    sketches, direction, image, moved, dots = kernel_call(
        image_kernel,
        "image",
        [(sketch_size, 2 * width)] + [(samples, width)] * 2 + [(samples * (sketch_size // TILE), TILE), (8, TILE)],
        core,
        solved,
        sketch,
        own_image,
        other_core(own_image),
        rhs,
        image_rhs,
    )
    moved, late_image = lax.optimization_barrier((moved, image))
    upward, downward, gathered = sums(slab(late_image))
    from_below, from_above = sent(upward, downward)
    image_twice = mm(gathered, columns[1]) + from_below + from_above + noise_variance * late_image
    moved_share = share_sum(moved)
    inverse, moved_share = lax.optimization_barrier((inverse, moved_share))
    solves = mm(inverse, sketches)
    solves = solves + rough_mm(inverse, sketches - mm(system, solves))

    arrived = spread(jnp.concatenate([moved_share, dots], axis=0))
    rows = moved_share.shape[0]
    moved = from_tiles(arrived[:, :rows].reshape(-1, TILE), samples)
    dots = arrived[:, rows:].sum(axis=0)
    inner_first, curvature = dots[0, :samples, None], dots[1, :samples, None]
    step = inner_first / curvature

    taken = mm(moved, solves)
    precond = direction - step * ((image - taken[:, :width]) / noise_variance)
    image_precond = image - step * ((image_twice - taken[:, width:]) / noise_variance)
    residual = rhs - step * image
    dots = jnp.stack([dot_rows(residual, precond), dot_rows(precond, image_precond), dot_rows(precond, image)])
    dots = spread(jnp.pad(dots, ((0, 5), (0, TILE - samples)))).sum(axis=0)
    inner_second, curvature_precond, mixed = (dots[i, :samples, None] for i in range(3))
    beta = inner_second / inner_first
    step_second = inner_second / (curvature_precond + beta * (2.0 * mixed + beta * curvature))
    weights = step * direction + step_second * (precond + beta * direction)
    residual = residual - step_second * (image_precond + beta * image)
    return (weights, residual)


def solution(mesh):
    in_specs = (
        P(None, ("blk", "leaf")),
        P(("blk", "leaf"), None),
        P(None, ("blk", "leaf")),
        P(("blk", "leaf")),
        P("samp", ("blk", "leaf")),
    )
    out_specs = (P("samp", ("blk", "leaf")), P("samp", ("blk", "leaf")))
    return jax.shard_map(local, mesh=mesh, in_specs=in_specs, out_specs=out_specs, check_vma=False)
```

```python
import functools

import jax
import jax.numpy as jnp
from jax import lax
from jax.experimental import pallas as pl
from jax.experimental.pallas import tpu as pltpu
from jax.sharding import PartitionSpec as P

support_radius = 0.8
noise_variance = 1.0
sketch_shift = 1.0
HIGHEST = lax.Precision.HIGHEST
POINT_AXES = ("blk", "leaf")
TILE = 128
PIVOT, BASE, AHEAD, REFINES = 8, 128, False, 1


def mm(left, right):
    return jnp.dot(left, right, precision=HIGHEST, preferred_element_type=jnp.float32)


def rough_mm(left, right):
    return jnp.dot(left, right, preferred_element_type=jnp.float32)


def mm_t(left, right):
    return lax.dot_general(
        left, right, (((1,), (1,)), ((), ())), precision=HIGHEST, preferred_element_type=jnp.float32
    )


def tree_sum(terms):
    terms = list(terms)
    while len(terms) > 1:
        terms = [
            terms[i] + terms[i + 1] if i + 1 < len(terms) else terms[i] for i in range(0, len(terms), 2)
        ]
    return terms[0]


def reciprocal(value):
    guess = pl.reciprocal(value, approx=True)
    for _ in range(REFINES):
        guess = guess * (2.0 - value * guess)
    return guess


def small_inverse(entries, size):
    def at(table, a, b):
        return table[(min(a, b), max(a, b))]

    if size == 1:
        return {(0, 0): reciprocal(entries[(0, 0)])}
    if size == 2:
        det = entries[(0, 0)] * entries[(1, 1)] - entries[(0, 1)] * entries[(0, 1)]
        inv = reciprocal(det)
        return {(0, 0): entries[(1, 1)] * inv, (1, 1): entries[(0, 0)] * inv, (0, 1): -entries[(0, 1)] * inv}
    half = size // 2
    idx = range(half)
    upper = [(a, b) for a in idx for b in range(a, half)]
    first = small_inverse({(a, b): entries[(a, b)] for a, b in upper}, half)
    cross = [[entries[(a, half + b)] for b in idx] for a in idx]
    lift = [[tree_sum(at(first, a, c) * cross[c][b] for c in idx) for b in idx] for a in idx]
    schur = {
        (a, b): entries[(half + a, half + b)] - tree_sum(cross[c][a] * lift[c][b] for c in idx)
        for a, b in upper
    }
    last = small_inverse(schur, half)
    mixed = [[tree_sum(lift[a][c] * at(last, c, b) for c in idx) for b in idx] for a in idx]
    result = {}
    for a, b in upper:
        result[(half + a, half + b)] = last[(a, b)]
        result[(a, b)] = first[(a, b)] + tree_sum(mixed[a][c] * lift[b][c] for c in idx)
    for a in idx:
        for b in idx:
            result[(a, half + b)] = -mixed[a][b]
    return result


def pivot_inverse(matrix):
    size = matrix.shape[0]
    lane = lax.broadcasted_iota(jnp.int32, (8, size), 1)
    sub = lax.broadcasted_iota(jnp.int32, (8, size), 0)
    parts = [matrix[8 * i : 8 * i + 8, :] for i in range(size // 8)]
    idx = range(PIVOT)
    upper = [(a, b) for a in idx for b in range(a, PIVOT)]

    def row(r):
        return jnp.broadcast_to(parts[r // 8][r % 8 : r % 8 + 1, :], (8, size))

    def entry(values, c):
        return jnp.broadcast_to(values[:, c : c + 1], (8, size))

    entries = None
    for k in range(0, size, PIVOT):
        home, first = k // 8, k % 8
        rows = [row(k + a) for a in idx]
        if entries is None:
            entries = {(a, b): entry(rows[a], k + b) for a, b in upper}
        ahead = AHEAD and k + PIVOT < size
        if ahead:
            later = k + PIVOT
            side = [[entry(rows[a], later + b) for b in idx] for a in idx]
            later_rows = [row(later + a) for a in idx]
            later_entries = {(a, b): entry(later_rows[a], later + b) for a, b in upper}
        inverse = small_inverse(entries, PIVOT)
        full = [[inverse[(min(a, b), max(a, b))] for b in idx] for a in idx]
        entries = None
        if ahead:
            lift = [[tree_sum(full[a][c] * side[c][b] for c in idx) for b in idx] for a in idx]
            entries = {
                (a, b): later_entries[(a, b)] - tree_sum(side[c][a] * lift[c][b] for c in idx)
                for a, b in upper
            }
        here = (lane >= k) & (lane < k + PIVOT)
        rows = [jnp.where(here, jnp.where(lane == k + a, 1.0, 0.0), rows[a]) for a in idx]
        scaled = [tree_sum(full[a][b] * rows[b] for b in idx) for a in idx]
        updated = []
        for i, part in enumerate(parts):
            columns = [entry(part, k + a) for a in idx]
            base = jnp.where(here, 0.0, part)
            if i == home:
                inside = (sub >= first) & (sub < first + PIVOT)
                base = jnp.where(inside, 0.0, base)
                columns = [
                    jnp.where(inside, jnp.where(sub == first + a, -1.0, 0.0), column)
                    for a, column in enumerate(columns)
                ]
            updated.append(base - tree_sum(columns[a] * scaled[a] for a in idx))
        parts = updated
    return jnp.concatenate(parts, axis=0)


def block_inverse(matrix):
    size = matrix.shape[0]
    if size <= BASE:
        return pivot_inverse(matrix)
    half = size // 2
    corner, side = matrix[:half, :half], matrix[:half, half:]
    first = block_inverse(corner)
    lift = mm(first, side)
    last = block_inverse(matrix[half:, half:] - mm(side.T, lift))
    mixed = mm(lift, last)
    top = jnp.concatenate([first + mm(mixed, lift.T), -mixed], axis=1)
    return jnp.concatenate([top, jnp.concatenate([-mixed.T, last], axis=1)], axis=0)


def assemble(core_ref, own_ref, other_ref, system_ref):
    half = system_ref.shape[0] // 2
    count = half // TILE

    def put(row, column, block):
        system_ref[row : row + TILE, column : column + TILE] = block

    flag = jnp.zeros((TILE, TILE), jnp.int32) + core_ref[0] == 0

    def tile(at, share):
        own, other = own_ref[at : at + TILE, :], other_ref[at : at + TILE, :]
        return jnp.where(flag, own, other) if share == 0 else jnp.where(flag, other, own)

    for share, corner in ((0, 0), (1, half)):
        at = 0
        for i in range(count):
            for j in range(i, count):
                block = tile(at, share)
                at += TILE
                if i == j:
                    put(corner + i * TILE, corner + i * TILE, 0.5 * (block + block.T))
                else:
                    put(corner + i * TILE, corner + j * TILE, block)
                    put(corner + j * TILE, corner + i * TILE, block.T)
    share_columns = count // 2
    for share in (0, 1):
        at = count * (count + 1) // 2 * TILE
        for j in range(share * share_columns, (share + 1) * share_columns):
            for i in range(count):
                block = tile(at, share)
                at += TILE
                put(i * TILE, half + j * TILE, block)
                put(half + j * TILE, i * TILE, block.T)


def eliminate(inverse_ref, begin, end):
    size = inverse_ref.shape[0]
    count = size // TILE
    row_id = lax.broadcasted_iota(jnp.int32, (TILE, TILE), 0)
    column_id = lax.broadcasted_iota(jnp.int32, (TILE, TILE), 1)

    def span(index):
        return pl.ds(pl.multiple_of(index * TILE, TILE), TILE)

    def step(k, carry):
        own = span(k)
        block = block_inverse(inverse_ref[own, own])
        inverse_ref[own, own] = jnp.where(row_id == column_id, 1.0, 0.0)
        scaled = mm(block, inverse_ref[own, :])
        inverse_ref[own, :] = scaled
        for ahead in range(1, count):
            other = span(lax.rem(k + ahead, count))
            column = inverse_ref[other, own]
            inverse_ref[other, own] = jnp.zeros((TILE, TILE), jnp.float32)
            inverse_ref[other, :] = inverse_ref[other, :] - mm(column, scaled)
        return carry

    lax.fori_loop(begin, end, step, 0)


def inverse_kernel(place_ref, *refs):
    shares, (system_ref, inverse_ref, solved_ref, own_ref, other_ref) = refs[:-5], refs[-5:]
    leaves = len(shares) // 2
    rows = shares[0].shape[0]
    for m in range(leaves):
        at = pl.ds(pl.multiple_of((place_ref[1] ^ m) * rows, rows), rows)
        own_ref[at, :] = shares[m][...]
        other_ref[at, :] = shares[leaves + m][...]
    assemble(place_ref, own_ref, other_ref, system_ref)
    inverse_ref[...] = system_ref[...]
    count = system_ref.shape[0] // TILE
    eliminate(inverse_ref, 0, count)
    samples = solved_ref.shape[0]
    begin = own_ref.shape[0] - count * samples
    rhs = jnp.concatenate(
        [own_ref[begin + i * samples : begin + (i + 1) * samples, :] for i in range(count)], axis=1
    )
    guess = mm(rhs, inverse_ref[...])
    solved_ref[...] = guess + rough_mm(rhs - mm(guess, system_ref[...]), inverse_ref[...])


def image_kernel(
    core_ref, solved_ref, sketch_ref, own_ref, other_ref, rhs_ref, image_rhs_ref,
    sketches_ref, direction_ref, image_ref, sums_ref,
):
    half, width = own_ref.shape
    core = core_ref[0]
    sketches_ref[:, :width] = sketch_ref[...]
    sketches_ref[pl.ds(pl.multiple_of(core * half, half), half), width:] = own_ref[...]
    sketches_ref[pl.ds(pl.multiple_of((1 - core) * half, half), half), width:] = other_ref[...]
    taken = mm(solved_ref[...], sketches_ref[...])
    rhs = rhs_ref[...]
    direction = (rhs - taken[:, :width]) / noise_variance
    image = (image_rhs_ref[...] - taken[:, width:]) / noise_variance
    direction_ref[...] = direction
    image_ref[...] = image
    moved = mm_t(image, sketch_ref[...])
    samples = rhs.shape[0]
    count = moved.shape[1] // TILE
    for i in range(count):
        sums_ref[i * samples : (i + 1) * samples, :] = moved[:, i * TILE : (i + 1) * TILE]
    at = count * samples
    ones = jnp.ones((8, width), jnp.float32)
    sums_ref[at:, :] = jnp.zeros((8, TILE), jnp.float32)
    sums_ref[at : at + 1, :samples] = mm_t(ones, rhs * direction)[0:1, :]
    sums_ref[at + 1 : at + 2, :samples] = mm_t(ones, direction * image)[0:1, :]


def prepare_kernel(
    core_ref, points_ref, neighbors_ref, omega_ref, observed_ref, prior_ref, first_ref, second_ref, meta_ref,
    points_vmem, neighbors_vmem, observed_vmem, prior_vmem, sems,
):
    split = second_ref.shape[0]
    samples = prior_vmem.shape[0]
    begin = pl.multiple_of(core_ref[0] * (2 * split), 2 * split)
    copies = [
        pltpu.make_async_copy(source, target, sems.at[i])
        for i, (source, target) in enumerate(
            (
                (omega_ref.at[pl.ds(begin, split), :], first_ref.at[0:split, :]),
                (omega_ref.at[pl.ds(begin + split, split), :], second_ref),
                (points_ref, points_vmem),
                (neighbors_ref, neighbors_vmem),
                (observed_ref, observed_vmem),
                (prior_ref, prior_vmem),
            )
        )
    ]
    for copy in copies:
        copy.start()
    meta_ref[...] = jnp.full(meta_ref.shape, -1.0, jnp.float32)
    for copy in copies:
        copy.wait()
    first_ref[split : split + samples, :] = observed_vmem[...] - prior_vmem[...]
    meta_ref[0:3, :] = points_vmem[...]
    meta_ref[3:4, : neighbors_vmem.shape[1]] = neighbors_vmem[...].astype(jnp.float32)
    first_ref[split + samples :, :] = meta_ref[...]


def prepare(core, points, neighbors, omega, observed, prior, split):
    width = omega.shape[1]
    samples = prior.shape[0]
    vmem = pl.BlockSpec(memory_space=pltpu.VMEM)
    hbm = pl.BlockSpec(memory_space=pl.ANY)
    shapes = [(split + samples + 8, width), (split, width), (8, width)]
    return pl.pallas_call(
        prepare_kernel,
        out_shape=tuple(jax.ShapeDtypeStruct(shape, jnp.float32) for shape in shapes),
        in_specs=[pl.BlockSpec(memory_space=pltpu.SMEM)] + [hbm] * 5,
        out_specs=(vmem,) * 3,
        scratch_shapes=[
            pltpu.VMEM(points.shape, jnp.float32),
            pltpu.VMEM(neighbors.shape, jnp.int32),
            pltpu.VMEM(observed.shape, jnp.float32),
            pltpu.VMEM(prior.shape, jnp.float32),
            pltpu.SemaphoreType.DMA((6,)),
        ],
        name="prepare",
        cost_estimate=pl.CostEstimate(flops=10**6, bytes_accessed=2**19, transcendentals=0),
    )(core, points, neighbors, omega, observed, prior)


def payload_kernel(place_ref, omega_ref, own_ref, other_ref, rhs_ref, sketch_ref, *refs):
    half, width = own_ref.shape
    split = half // 2
    core, leaf = place_ref[0], place_ref[1]
    shares, payload_ref = refs[:-1], refs[-1]
    begin = pl.multiple_of(core * half, half)
    sketch_ref[pl.ds(begin, half), :] = own_ref[...]
    sketch_ref[pl.ds(pl.multiple_of((1 - core) * half, half), half), :] = other_ref[...]
    own, other = own_ref[...], other_ref[...]
    lifted = noise_variance * omega_ref[...] + own
    count = half // TILE
    at = 0
    for i in range(count):
        product = mm_t(lifted[i * TILE : (i + 1) * TILE], own[i * TILE :])
        for j in range(count - i):
            payload_ref[at : at + TILE, :] = product[:, j * TILE : (j + 1) * TILE]
            at += TILE
    on_first = jnp.zeros((half, width), jnp.int32) + core == 0
    left = jnp.where(on_first, lifted, other)
    right = jnp.where(on_first[:split], other[:split], lifted[split:])
    product = mm_t(left, right)
    for j in range(split // TILE):
        payload_ref[at : at + half, :] = product[:, j * TILE : (j + 1) * TILE]
        at += half
    product = mm_t(rhs_ref[...], sketch_ref[...])
    samples = rhs_ref.shape[0]
    for j in range(2 * count):
        payload_ref[at : at + samples, :] = product[:, j * TILE : (j + 1) * TILE]
        at += samples
    rows = shares[0].shape[0]
    for m, share in enumerate(shares):
        share[...] = payload_ref[pl.ds(pl.multiple_of((leaf ^ m) * rows, rows), rows), :]


def kernel_call(kernel, name, outputs, *operands, scratch=(), flops=10**8):
    vmem = pl.BlockSpec(memory_space=pltpu.VMEM)
    smem = pl.BlockSpec(memory_space=pltpu.SMEM)
    return pl.pallas_call(
        kernel,
        out_shape=tuple(jax.ShapeDtypeStruct(shape, jnp.float32) for shape in outputs),
        in_specs=[smem if o.ndim == 1 else vmem for o in operands],
        out_specs=(vmem,) * len(outputs),
        scratch_shapes=[pltpu.VMEM(shape, jnp.float32) for shape in scratch],
        name=name,
        compiler_params=pltpu.CompilerParams(vmem_limit_bytes=12 * 2**20),
        cost_estimate=pl.CostEstimate(flops=flops, bytes_accessed=2**20, transcendentals=0),
    )(*operands)


def shifted(values, axis, distance):
    size = lax.axis_size(axis)
    return lax.ppermute(values, axis, [(i, (i + distance) % size) for i in range(size)])


def swapped(values, axis, mask):
    size = lax.axis_size(axis)
    return lax.ppermute(values, axis, [(i, i ^ mask) for i in range(size)])


def slab(values):
    return [values] + [swapped(values, "leaf", m) for m in range(1, lax.axis_size("leaf"))]


def group_size():
    return lax.axis_size(POINT_AXES)


def exchange(values):
    return lax.all_to_all(values, POINT_AXES, 0, 0, tiled=True)


def axis_sum(values, axis):
    if lax.axis_size(axis) != 4:
        return lax.psum(values, axis)
    one, two, three = (swapped(values, axis, m) for m in (1, 2, 3))
    return (values + one) + (two + three)


def spread(values):
    count = group_size()
    sent = jnp.broadcast_to(values[None], (count,) + values.shape).reshape(-1, values.shape[1])
    return exchange(sent).reshape((count,) + values.shape)


def to_tiles(values):
    return jnp.concatenate([values[:, c : c + TILE] for c in range(0, values.shape[1], TILE)], axis=0)


def from_tiles(tiles, rows):
    return jnp.concatenate([tiles[r : r + rows] for r in range(0, tiles.shape[0], rows)], axis=1)


def dot_rows(left, right):
    return jnp.sum(left * right, axis=1)


def local(points, neighbors, omega, observed, prior_draws):
    cycle = lax.axis_size("blk")
    leaves = lax.axis_size("leaf")
    cores = lax.axis_size("samp")
    own_slab, own_leaf, own_core = (lax.axis_index(a) for a in ("blk", "leaf", "samp"))
    sketch_size, width = omega.shape
    half = sketch_size // cores
    samples = prior_draws.shape[0]
    period = 2.0 * cycle

    core = own_core.astype(jnp.int32).reshape(1)
    place = jnp.stack([own_core, own_leaf]).astype(jnp.int32)
    split = half // 2
    first_block, second_block, meta = prepare(
        core, points, neighbors, omega, observed[None, :], prior_draws, split
    )

    def other_core(values):
        return swapped(values, "samp", 1)

    def sent(upward, downward):
        return shifted(upward, "blk", 1), shifted(downward, "blk", -1)

    first_blocks, second_blocks = slab(first_block), slab(second_block)
    above, below = shifted(meta, "blk", -1), shifted(meta, "blk", 1)
    begin = split + samples
    sources = jnp.concatenate([b[begin : begin + 3] for b in first_blocks], axis=1)
    targets = [above, meta, below]
    source_ids = own_slab * leaves + jnp.stack([own_leaf ^ m for m in range(leaves)])
    target_lists = jnp.stack([t[3, : neighbors.shape[1]] for t in targets])
    usable = (target_lists[None] == source_ids[:, None, None].astype(jnp.float32)).astype(jnp.float32).sum(axis=2)

    def kernel_columns(index):
        offset = sources[:, :, None] - targets[index][:3, None, :]
        along = offset[0]
        along = jnp.where(along >= 0.5 * period, along - period, along)
        along = jnp.where(along < -0.5 * period, along + period, along)
        squared = along * along + offset[1] * offset[1] + offset[2] * offset[2]
        radius = jnp.sqrt(squared) / support_radius
        remain = jnp.maximum(1.0 - radius, 0.0)
        squared_remain = remain * remain
        values = squared_remain * squared_remain * (4.0 * radius + 1.0)
        weight = jnp.repeat(usable[:, index], width)
        return values * weight[:, None]

    columns = [kernel_columns(i) for i in range(3)]

    def sums(values):
        gathered = jnp.concatenate(values, axis=1)
        return mm(gathered, columns[0]), mm(gathered, columns[2]), gathered

    upward, downward, gathered = sums([b[:begin] for b in first_blocks])
    _, _, *second_blocks = lax.optimization_barrier((upward, downward, *second_blocks))
    from_below, from_above = sent(upward, downward)
    applied = mm(gathered, columns[1]) + from_below + from_above
    upward, downward, gathered = sums(second_blocks)
    from_below, from_above = sent(upward, downward)
    applied_second = mm(gathered, columns[1]) + from_below + from_above
    rhs = first_block[split:begin]
    omega_half = jnp.concatenate([first_block[:split], second_block], axis=0)
    sketch_half = jnp.concatenate([applied[:split], applied_second], axis=0) + sketch_shift * omega_half
    image_rhs = applied[split:] + noise_variance * rhs

    count = half // TILE
    matrix_rows = (count * (count + 1) // 2 + count * count // 2) * TILE
    payload_rows = matrix_rows + samples * (sketch_size // TILE)
    sketch, *shares = kernel_call(
        payload_kernel,
        "payload",
        [(sketch_size, width)] + [(payload_rows // leaves, TILE)] * leaves,
        place,
        omega_half,
        sketch_half,
        other_core(sketch_half),
        rhs,
        scratch=[(payload_rows, TILE)],
        flops=10**9,
    )

    share = shares[0]
    for m in range(1, leaves):
        share = share + swapped(shares[m], "leaf", m)
    share, late_sketch = lax.optimization_barrier((share, sketch_half))
    upward, downward, gathered = sums(slab(late_sketch))
    here = mm(gathered, columns[1]) + noise_variance * late_sketch
    shares = slab(axis_sum(share, "blk"))
    *shares, upward, downward, here = lax.optimization_barrier((*shares, upward, downward, here))
    other_shares = [other_core(s) for s in shares]
    from_below, from_above = sent(upward, downward)
    system, inverse, solved = kernel_call(
        inverse_kernel,
        "inverse_and_solve",
        [(sketch_size, sketch_size)] * 2 + [(samples, sketch_size)],
        place,
        *shares,
        *other_shares,
        scratch=[(payload_rows, TILE)] * 2,
        flops=30 * 10**9,
    )
    from_below, from_above, solved = lax.optimization_barrier((from_below, from_above, solved))
    own_image = here + from_below + from_above

    sketches, direction, image, partial = kernel_call(
        image_kernel,
        "image",
        [(sketch_size, 2 * width)] + [(samples, width)] * 2 + [(samples * (sketch_size // TILE) + 8, TILE)],
        core,
        solved,
        sketch,
        own_image,
        other_core(own_image),
        rhs,
        image_rhs,
    )
    partial, late_image = lax.optimization_barrier((partial, image))
    upward, downward, gathered = sums(slab(late_image))
    from_below, from_above = sent(upward, downward)
    image_twice = mm(gathered, columns[1]) + from_below + from_above + noise_variance * late_image
    slab_sum = axis_sum(partial, "leaf")
    inverse, _ = lax.optimization_barrier((inverse, slab_sum))
    solves = mm(inverse, sketches)
    solves = solves + rough_mm(inverse, sketches - mm(system, solves))
    total = axis_sum(slab_sum, "blk")
    moved = from_tiles(total[:-8], samples)
    dots = total[-8:]
    inner_first, curvature = dots[0, :samples, None], dots[1, :samples, None]
    step = inner_first / curvature

    taken = mm(moved, solves)
    precond = direction - step * ((image - taken[:, :width]) / noise_variance)
    image_precond = image - step * ((image_twice - taken[:, width:]) / noise_variance)
    residual = rhs - step * image
    dots = jnp.stack([dot_rows(residual, precond), dot_rows(precond, image_precond), dot_rows(precond, image)])
    dots = spread(jnp.pad(dots, ((0, 5), (0, TILE - samples)))).sum(axis=0)
    inner_second, curvature_precond, mixed = (dots[i, :samples, None] for i in range(3))
    beta = inner_second / inner_first
    step_second = inner_second / (curvature_precond + beta * (2.0 * mixed + beta * curvature))
    weights = step * direction + step_second * (precond + beta * direction)
    residual = residual - step_second * (image_precond + beta * image)
    return (weights, residual)


def solution(mesh):
    in_specs = (
        P(None, ("blk", "leaf")),
        P(("blk", "leaf"), None),
        P(None, ("blk", "leaf")),
        P(("blk", "leaf")),
        P("samp", ("blk", "leaf")),
    )
    out_specs = (P("samp", ("blk", "leaf")), P("samp", ("blk", "leaf")))
    return jax.shard_map(local, mesh=mesh, in_specs=in_specs, out_specs=out_specs, check_vma=False)
```

```python
import functools

import jax
import jax.numpy as jnp
from jax import lax
from jax.experimental import pallas as pl
from jax.experimental.pallas import tpu as pltpu
from jax.sharding import PartitionSpec as P

support_radius = 0.8
noise_variance = 1.0
sketch_shift = 1.0
HIGHEST = lax.Precision.HIGHEST
POINT_AXES = ("blk", "leaf")
TILE = 128
PIVOT, BASE, AHEAD, REFINES = 8, 128, False, 1


def mm(left, right):
    return jnp.dot(left, right, precision=HIGHEST, preferred_element_type=jnp.float32)


def rough_mm(left, right):
    return jnp.dot(left, right, preferred_element_type=jnp.float32)


def mm_t(left, right):
    return lax.dot_general(
        left, right, (((1,), (1,)), ((), ())), precision=HIGHEST, preferred_element_type=jnp.float32
    )


def tree_sum(terms):
    terms = list(terms)
    while len(terms) > 1:
        terms = [
            terms[i] + terms[i + 1] if i + 1 < len(terms) else terms[i] for i in range(0, len(terms), 2)
        ]
    return terms[0]


def reciprocal(value):
    guess = pl.reciprocal(value, approx=True)
    for _ in range(REFINES):
        guess = guess * (2.0 - value * guess)
    return guess


def small_inverse(entries, size):
    def at(table, a, b):
        return table[(min(a, b), max(a, b))]

    if size == 1:
        return {(0, 0): reciprocal(entries[(0, 0)])}
    if size == 2:
        det = entries[(0, 0)] * entries[(1, 1)] - entries[(0, 1)] * entries[(0, 1)]
        inv = reciprocal(det)
        return {(0, 0): entries[(1, 1)] * inv, (1, 1): entries[(0, 0)] * inv, (0, 1): -entries[(0, 1)] * inv}
    half = size // 2
    idx = range(half)
    upper = [(a, b) for a in idx for b in range(a, half)]
    first = small_inverse({(a, b): entries[(a, b)] for a, b in upper}, half)
    cross = [[entries[(a, half + b)] for b in idx] for a in idx]
    lift = [[tree_sum(at(first, a, c) * cross[c][b] for c in idx) for b in idx] for a in idx]
    schur = {
        (a, b): entries[(half + a, half + b)] - tree_sum(cross[c][a] * lift[c][b] for c in idx)
        for a, b in upper
    }
    last = small_inverse(schur, half)
    mixed = [[tree_sum(lift[a][c] * at(last, c, b) for c in idx) for b in idx] for a in idx]
    result = {}
    for a, b in upper:
        result[(half + a, half + b)] = last[(a, b)]
        result[(a, b)] = first[(a, b)] + tree_sum(mixed[a][c] * lift[b][c] for c in idx)
    for a in idx:
        for b in idx:
            result[(a, half + b)] = -mixed[a][b]
    return result


def pivot_inverse(matrix):
    size = matrix.shape[0]
    lane = lax.broadcasted_iota(jnp.int32, (8, size), 1)
    sub = lax.broadcasted_iota(jnp.int32, (8, size), 0)
    parts = [matrix[8 * i : 8 * i + 8, :] for i in range(size // 8)]
    idx = range(PIVOT)
    upper = [(a, b) for a in idx for b in range(a, PIVOT)]

    def row(r):
        return jnp.broadcast_to(parts[r // 8][r % 8 : r % 8 + 1, :], (8, size))

    def entry(values, c):
        return jnp.broadcast_to(values[:, c : c + 1], (8, size))

    entries = None
    for k in range(0, size, PIVOT):
        home, first = k // 8, k % 8
        rows = [row(k + a) for a in idx]
        if entries is None:
            entries = {(a, b): entry(rows[a], k + b) for a, b in upper}
        ahead = AHEAD and k + PIVOT < size
        if ahead:
            later = k + PIVOT
            side = [[entry(rows[a], later + b) for b in idx] for a in idx]
            later_rows = [row(later + a) for a in idx]
            later_entries = {(a, b): entry(later_rows[a], later + b) for a, b in upper}
        inverse = small_inverse(entries, PIVOT)
        full = [[inverse[(min(a, b), max(a, b))] for b in idx] for a in idx]
        entries = None
        if ahead:
            lift = [[tree_sum(full[a][c] * side[c][b] for c in idx) for b in idx] for a in idx]
            entries = {
                (a, b): later_entries[(a, b)] - tree_sum(side[c][a] * lift[c][b] for c in idx)
                for a, b in upper
            }
        here = (lane >= k) & (lane < k + PIVOT)
        rows = [jnp.where(here, jnp.where(lane == k + a, 1.0, 0.0), rows[a]) for a in idx]
        scaled = [tree_sum(full[a][b] * rows[b] for b in idx) for a in idx]
        updated = []
        for i, part in enumerate(parts):
            columns = [entry(part, k + a) for a in idx]
            base = jnp.where(here, 0.0, part)
            if i == home:
                inside = (sub >= first) & (sub < first + PIVOT)
                base = jnp.where(inside, 0.0, base)
                columns = [
                    jnp.where(inside, jnp.where(sub == first + a, -1.0, 0.0), column)
                    for a, column in enumerate(columns)
                ]
            updated.append(base - tree_sum(columns[a] * scaled[a] for a in idx))
        parts = updated
    return jnp.concatenate(parts, axis=0)


def block_inverse(matrix):
    size = matrix.shape[0]
    if size <= BASE:
        return pivot_inverse(matrix)
    half = size // 2
    corner, side = matrix[:half, :half], matrix[:half, half:]
    first = block_inverse(corner)
    lift = mm(first, side)
    last = block_inverse(matrix[half:, half:] - mm(side.T, lift))
    mixed = mm(lift, last)
    top = jnp.concatenate([first + mm(mixed, lift.T), -mixed], axis=1)
    return jnp.concatenate([top, jnp.concatenate([-mixed.T, last], axis=1)], axis=0)


def assemble(core_ref, own_ref, other_ref, system_ref):
    half = system_ref.shape[0] // 2
    count = half // TILE

    def put(row, column, block):
        system_ref[row : row + TILE, column : column + TILE] = block

    flag = jnp.zeros((TILE, TILE), jnp.int32) + core_ref[0] == 0

    def tile(at, share):
        own, other = own_ref[at : at + TILE, :], other_ref[at : at + TILE, :]
        return jnp.where(flag, own, other) if share == 0 else jnp.where(flag, other, own)

    for share, corner in ((0, 0), (1, half)):
        at = 0
        for i in range(count):
            for j in range(i, count):
                block = tile(at, share)
                at += TILE
                if i == j:
                    put(corner + i * TILE, corner + i * TILE, 0.5 * (block + block.T))
                else:
                    put(corner + i * TILE, corner + j * TILE, block)
                    put(corner + j * TILE, corner + i * TILE, block.T)
    share_columns = count // 2
    for share in (0, 1):
        at = count * (count + 1) // 2 * TILE
        for j in range(share * share_columns, (share + 1) * share_columns):
            for i in range(count):
                block = tile(at, share)
                at += TILE
                put(i * TILE, half + j * TILE, block)
                put(half + j * TILE, i * TILE, block.T)


def eliminate(inverse_ref, begin, end):
    size = inverse_ref.shape[0]
    count = size // TILE
    row_id = lax.broadcasted_iota(jnp.int32, (TILE, TILE), 0)
    column_id = lax.broadcasted_iota(jnp.int32, (TILE, TILE), 1)

    def span(index):
        return pl.ds(pl.multiple_of(index * TILE, TILE), TILE)

    def step(k, carry):
        own = span(k)
        block = block_inverse(inverse_ref[own, own])
        inverse_ref[own, own] = jnp.where(row_id == column_id, 1.0, 0.0)
        scaled = mm(block, inverse_ref[own, :])
        inverse_ref[own, :] = scaled
        for ahead in range(1, count):
            other = span(lax.rem(k + ahead, count))
            column = inverse_ref[other, own]
            inverse_ref[other, own] = jnp.zeros((TILE, TILE), jnp.float32)
            inverse_ref[other, :] = inverse_ref[other, :] - mm(column, scaled)
        return carry

    lax.fori_loop(begin, end, step, 0)


def inverse_kernel(place_ref, *refs):
    shares, (system_ref, inverse_ref, solved_ref, own_ref, other_ref) = refs[:-5], refs[-5:]
    leaves = len(shares) // 2
    rows = shares[0].shape[0]
    for m in range(leaves):
        at = pl.ds(pl.multiple_of((place_ref[1] ^ m) * rows, rows), rows)
        own_ref[at, :] = shares[m][...]
        other_ref[at, :] = shares[leaves + m][...]
    assemble(place_ref, own_ref, other_ref, system_ref)
    inverse_ref[...] = system_ref[...]
    count = system_ref.shape[0] // TILE
    eliminate(inverse_ref, 0, count)
    samples = solved_ref.shape[0]
    begin = own_ref.shape[0] - count * samples
    rhs = jnp.concatenate(
        [own_ref[begin + i * samples : begin + (i + 1) * samples, :] for i in range(count)], axis=1
    )
    guess = mm(rhs, inverse_ref[...])
    solved_ref[...] = guess + rough_mm(rhs - mm(guess, system_ref[...]), inverse_ref[...])


def image_kernel(
    core_ref, solved_ref, sketch_ref, own_ref, other_ref, rhs_ref, image_rhs_ref,
    sketches_ref, direction_ref, image_ref, packet_ref,
):
    half, width = own_ref.shape
    core = core_ref[0]
    sketches_ref[:, :width] = sketch_ref[...]
    sketches_ref[pl.ds(pl.multiple_of(core * half, half), half), width:] = own_ref[...]
    sketches_ref[pl.ds(pl.multiple_of((1 - core) * half, half), half), width:] = other_ref[...]
    taken = mm(solved_ref[...], sketches_ref[...])
    rhs = rhs_ref[...]
    direction = (rhs - taken[:, :width]) / noise_variance
    image = (image_rhs_ref[...] - taken[:, width:]) / noise_variance
    direction_ref[...] = direction
    image_ref[...] = image
    moved = mm_t(image, sketch_ref[...])
    samples = rhs.shape[0]
    count = moved.shape[1] // TILE
    for i in range(count):
        packet_ref[i * samples : (i + 1) * samples, :] = moved[:, i * TILE : (i + 1) * TILE]
    at = count * samples
    ones = jnp.ones((8, width), jnp.float32)
    packet_ref[at : at + 8, :] = jnp.zeros((8, TILE), jnp.float32)
    packet_ref[at : at + 1, :samples] = mm_t(ones, rhs * direction)[0:1, :]
    packet_ref[at + 1 : at + 2, :samples] = mm_t(ones, direction * image)[0:1, :]
    at += 8
    for i in range(width // TILE):
        packet_ref[at : at + samples, :] = image[:, i * TILE : (i + 1) * TILE]
        at += samples


def prepare_kernel(
    core_ref, points_ref, neighbors_ref, omega_ref, observed_ref, prior_ref, first_ref, second_ref, meta_ref,
    points_vmem, neighbors_vmem, observed_vmem, prior_vmem, sems,
):
    split = second_ref.shape[0]
    samples = prior_vmem.shape[0]
    begin = pl.multiple_of(core_ref[0] * (2 * split), 2 * split)
    copies = [
        pltpu.make_async_copy(source, target, sems.at[i])
        for i, (source, target) in enumerate(
            (
                (omega_ref.at[pl.ds(begin, split), :], first_ref.at[0:split, :]),
                (omega_ref.at[pl.ds(begin + split, split), :], second_ref),
                (points_ref, points_vmem),
                (neighbors_ref, neighbors_vmem),
                (observed_ref, observed_vmem),
                (prior_ref, prior_vmem),
            )
        )
    ]
    for copy in copies:
        copy.start()
    meta_ref[...] = jnp.full(meta_ref.shape, -1.0, jnp.float32)
    for copy in copies:
        copy.wait()
    first_ref[split : split + samples, :] = observed_vmem[...] - prior_vmem[...]
    meta_ref[0:3, :] = points_vmem[...]
    meta_ref[3:4, : neighbors_vmem.shape[1]] = neighbors_vmem[...].astype(jnp.float32)
    first_ref[split + samples :, :] = meta_ref[...]


def prepare(core, points, neighbors, omega, observed, prior, split):
    width = omega.shape[1]
    samples = prior.shape[0]
    vmem = pl.BlockSpec(memory_space=pltpu.VMEM)
    hbm = pl.BlockSpec(memory_space=pl.ANY)
    shapes = [(split + samples + 8, width), (split, width), (8, width)]
    return pl.pallas_call(
        prepare_kernel,
        out_shape=tuple(jax.ShapeDtypeStruct(shape, jnp.float32) for shape in shapes),
        in_specs=[pl.BlockSpec(memory_space=pltpu.SMEM)] + [hbm] * 5,
        out_specs=(vmem,) * 3,
        scratch_shapes=[
            pltpu.VMEM(points.shape, jnp.float32),
            pltpu.VMEM(neighbors.shape, jnp.int32),
            pltpu.VMEM(observed.shape, jnp.float32),
            pltpu.VMEM(prior.shape, jnp.float32),
            pltpu.SemaphoreType.DMA((6,)),
        ],
        name="prepare",
        cost_estimate=pl.CostEstimate(flops=10**6, bytes_accessed=2**19, transcendentals=0),
    )(core, points, neighbors, omega, observed, prior)


def payload_kernel(place_ref, omega_ref, own_ref, other_ref, rhs_ref, sketch_ref, *refs):
    half, width = own_ref.shape
    split = half // 2
    core, leaf = place_ref[0], place_ref[1]
    shares, payload_ref = refs[:-1], refs[-1]
    begin = pl.multiple_of(core * half, half)
    sketch_ref[pl.ds(begin, half), :] = own_ref[...]
    sketch_ref[pl.ds(pl.multiple_of((1 - core) * half, half), half), :] = other_ref[...]
    own, other = own_ref[...], other_ref[...]
    lifted = noise_variance * omega_ref[...] + own
    count = half // TILE
    at = 0
    for i in range(count):
        product = mm_t(lifted[i * TILE : (i + 1) * TILE], own[i * TILE :])
        for j in range(count - i):
            payload_ref[at : at + TILE, :] = product[:, j * TILE : (j + 1) * TILE]
            at += TILE
    on_first = jnp.zeros((half, width), jnp.int32) + core == 0
    left = jnp.where(on_first, lifted, other)
    right = jnp.where(on_first[:split], other[:split], lifted[split:])
    product = mm_t(left, right)
    for j in range(split // TILE):
        payload_ref[at : at + half, :] = product[:, j * TILE : (j + 1) * TILE]
        at += half
    product = mm_t(rhs_ref[...], sketch_ref[...])
    samples = rhs_ref.shape[0]
    for j in range(2 * count):
        payload_ref[at : at + samples, :] = product[:, j * TILE : (j + 1) * TILE]
        at += samples
    rows = shares[0].shape[0]
    for m, share in enumerate(shares):
        share[...] = payload_ref[pl.ds(pl.multiple_of((leaf ^ m) * rows, rows), rows), :]


def kernel_call(kernel, name, outputs, *operands, scratch=(), flops=10**8):
    vmem = pl.BlockSpec(memory_space=pltpu.VMEM)
    smem = pl.BlockSpec(memory_space=pltpu.SMEM)
    return pl.pallas_call(
        kernel,
        out_shape=tuple(jax.ShapeDtypeStruct(shape, jnp.float32) for shape in outputs),
        in_specs=[smem if o.ndim == 1 else vmem for o in operands],
        out_specs=(vmem,) * len(outputs),
        scratch_shapes=[pltpu.VMEM(shape, jnp.float32) for shape in scratch],
        name=name,
        compiler_params=pltpu.CompilerParams(vmem_limit_bytes=12 * 2**20),
        cost_estimate=pl.CostEstimate(flops=flops, bytes_accessed=2**20, transcendentals=0),
    )(*operands)


def shifted(values, axis, distance):
    size = lax.axis_size(axis)
    return lax.ppermute(values, axis, [(i, (i + distance) % size) for i in range(size)])


def swapped(values, axis, mask):
    size = lax.axis_size(axis)
    return lax.ppermute(values, axis, [(i, i ^ mask) for i in range(size)])


def slab(values):
    return [values] + [swapped(values, "leaf", m) for m in range(1, lax.axis_size("leaf"))]


def group_size():
    return lax.axis_size(POINT_AXES)


def exchange(values):
    return lax.all_to_all(values, POINT_AXES, 0, 0, tiled=True)


def axis_sum(values, axis):
    if lax.axis_size(axis) != 4:
        return lax.psum(values, axis)
    one, two, three = (swapped(values, axis, m) for m in (1, 2, 3))
    return (values + one) + (two + three)


def spread(values):
    count = group_size()
    sent = jnp.broadcast_to(values[None], (count,) + values.shape).reshape(-1, values.shape[1])
    return exchange(sent).reshape((count,) + values.shape)


def to_tiles(values):
    return jnp.concatenate([values[:, c : c + TILE] for c in range(0, values.shape[1], TILE)], axis=0)


def from_tiles(tiles, rows):
    return jnp.concatenate([tiles[r : r + rows] for r in range(0, tiles.shape[0], rows)], axis=1)


def dot_rows(left, right):
    return jnp.sum(left * right, axis=1)


def local(points, neighbors, omega, observed, prior_draws):
    cycle = lax.axis_size("blk")
    leaves = lax.axis_size("leaf")
    cores = lax.axis_size("samp")
    own_slab, own_leaf, own_core = (lax.axis_index(a) for a in ("blk", "leaf", "samp"))
    sketch_size, width = omega.shape
    half = sketch_size // cores
    samples = prior_draws.shape[0]
    period = 2.0 * cycle

    core = own_core.astype(jnp.int32).reshape(1)
    place = jnp.stack([own_core, own_leaf]).astype(jnp.int32)
    split = half // 2
    first_block, second_block, meta = prepare(
        core, points, neighbors, omega, observed[None, :], prior_draws, split
    )

    def other_core(values):
        return swapped(values, "samp", 1)

    def sent(upward, downward):
        return shifted(upward, "blk", 1), shifted(downward, "blk", -1)

    first_blocks, second_blocks = slab(first_block), slab(second_block)
    above, below = shifted(meta, "blk", -1), shifted(meta, "blk", 1)
    begin = split + samples
    sources = jnp.concatenate([b[begin : begin + 3] for b in first_blocks], axis=1)
    targets = [above, meta, below]
    source_ids = own_slab * leaves + jnp.stack([own_leaf ^ m for m in range(leaves)])
    target_lists = jnp.stack([t[3, : neighbors.shape[1]] for t in targets])
    usable = (target_lists[None] == source_ids[:, None, None].astype(jnp.float32)).astype(jnp.float32).sum(axis=2)

    def kernel_columns(index):
        offset = sources[:, :, None] - targets[index][:3, None, :]
        along = offset[0]
        along = jnp.where(along >= 0.5 * period, along - period, along)
        along = jnp.where(along < -0.5 * period, along + period, along)
        squared = along * along + offset[1] * offset[1] + offset[2] * offset[2]
        radius = jnp.sqrt(squared) / support_radius
        remain = jnp.maximum(1.0 - radius, 0.0)
        squared_remain = remain * remain
        values = squared_remain * squared_remain * (4.0 * radius + 1.0)
        weight = jnp.repeat(usable[:, index], width)
        return values * weight[:, None]

    columns = [kernel_columns(i) for i in range(3)]

    def sums(values):
        gathered = jnp.concatenate(values, axis=1)
        return mm(gathered, columns[0]), mm(gathered, columns[2]), gathered

    upward, downward, gathered = sums([b[:begin] for b in first_blocks])
    _, _, *second_blocks = lax.optimization_barrier((upward, downward, *second_blocks))
    from_below, from_above = sent(upward, downward)
    applied = mm(gathered, columns[1]) + from_below + from_above
    upward, downward, gathered = sums(second_blocks)
    from_below, from_above = sent(upward, downward)
    applied_second = mm(gathered, columns[1]) + from_below + from_above
    rhs = first_block[split:begin]
    omega_half = jnp.concatenate([first_block[:split], second_block], axis=0)
    sketch_half = jnp.concatenate([applied[:split], applied_second], axis=0) + sketch_shift * omega_half
    image_rhs = applied[split:] + noise_variance * rhs

    count = half // TILE
    matrix_rows = (count * (count + 1) // 2 + count * count // 2) * TILE
    payload_rows = matrix_rows + samples * (sketch_size // TILE)
    sketch, *shares = kernel_call(
        payload_kernel,
        "payload",
        [(sketch_size, width)] + [(payload_rows // leaves, TILE)] * leaves,
        place,
        omega_half,
        sketch_half,
        other_core(sketch_half),
        rhs,
        scratch=[(payload_rows, TILE)],
        flops=10**9,
    )

    *shares, late_sketch = lax.optimization_barrier((*shares, sketch_half))
    share = shares[0]
    for m in range(1, leaves):
        share = share + swapped(shares[m], "leaf", m)
    upward, downward, gathered = sums(slab(late_sketch))
    here = mm(gathered, columns[1]) + noise_variance * late_sketch
    shares = slab(axis_sum(share, "blk"))
    *shares, upward, downward, here = lax.optimization_barrier((*shares, upward, downward, here))
    other_shares = [other_core(s) for s in shares]
    from_below, from_above = sent(upward, downward)
    system, inverse, solved = kernel_call(
        inverse_kernel,
        "inverse_and_solve",
        [(sketch_size, sketch_size)] * 2 + [(samples, sketch_size)],
        place,
        *shares,
        *other_shares,
        scratch=[(payload_rows, TILE)] * 2,
        flops=30 * 10**9,
    )
    from_below, from_above, solved = lax.optimization_barrier((from_below, from_above, solved))
    own_image = here + from_below + from_above

    sum_rows = samples * (sketch_size // TILE) + 8
    sketches, direction, image, packet = kernel_call(
        image_kernel,
        "image",
        [(sketch_size, 2 * width)] + [(samples, width)] * 2 + [(sum_rows + samples * (width // TILE), TILE)],
        core,
        solved,
        sketch,
        own_image,
        other_core(own_image),
        rhs,
        image_rhs,
    )
    packets = slab(packet)
    slab_sum = (packets[0][:sum_rows] + packets[1][:sum_rows]) + (packets[2][:sum_rows] + packets[3][:sum_rows])
    upward, downward, gathered = sums([from_tiles(p[sum_rows:], samples) for p in packets])
    here = mm(gathered, columns[1]) + noise_variance * image
    if cycle == 4:
        even = own_slab % 2 == 0
        one, three = (
            swapped(jnp.concatenate([slab_sum, to_tiles(jnp.where(even, first, second))], axis=0), "blk", m)
            for m, first, second in ((1, upward, downward), (3, downward, upward))
        )
        two = swapped(slab_sum, "blk", 2)
        total = (slab_sum + one[:sum_rows]) + (two + three[:sum_rows])
        from_below, from_above = from_tiles(one[sum_rows:], samples), from_tiles(three[sum_rows:], samples)
    else:
        total = lax.psum(slab_sum, "blk")
        from_below, from_above = sent(upward, downward)
    image_twice = here + from_below + from_above
    solves = mm(inverse, sketches)
    solves = solves + rough_mm(inverse, sketches - mm(system, solves))
    moved = from_tiles(total[:-8], samples)
    dots = total[-8:]
    inner_first, curvature = dots[0, :samples, None], dots[1, :samples, None]
    step = inner_first / curvature

    taken = mm(moved, solves)
    precond = direction - step * ((image - taken[:, :width]) / noise_variance)
    image_precond = image - step * ((image_twice - taken[:, width:]) / noise_variance)
    residual = rhs - step * image
    dots = jnp.stack([dot_rows(residual, precond), dot_rows(precond, image_precond), dot_rows(precond, image)])
    dots = spread(jnp.pad(dots, ((0, 5), (0, TILE - samples)))).sum(axis=0)
    inner_second, curvature_precond, mixed = (dots[i, :samples, None] for i in range(3))
    beta = inner_second / inner_first
    step_second = inner_second / (curvature_precond + beta * (2.0 * mixed + beta * curvature))
    weights = step * direction + step_second * (precond + beta * direction)
    residual = residual - step_second * (image_precond + beta * image)
    return (weights, residual)


def solution(mesh):
    in_specs = (
        P(None, ("blk", "leaf")),
        P(("blk", "leaf"), None),
        P(None, ("blk", "leaf")),
        P(("blk", "leaf")),
        P("samp", ("blk", "leaf")),
    )
    out_specs = (P("samp", ("blk", "leaf")), P("samp", ("blk", "leaf")))
    return jax.shard_map(local, mesh=mesh, in_specs=in_specs, out_specs=out_specs, check_vma=False)
```

```python
import functools

import jax
import jax.numpy as jnp
from jax import lax
from jax.experimental import pallas as pl
from jax.experimental.pallas import tpu as pltpu
from jax.sharding import PartitionSpec as P

support_radius = 0.8
noise_variance = 1.0
sketch_shift = 1.0
HIGHEST = lax.Precision.HIGHEST
POINT_AXES = ("blk", "leaf")
TILE = 128
PIVOT, BASE, AHEAD, REFINES = 8, 128, False, 1


def mm(left, right):
    return jnp.dot(left, right, precision=HIGHEST, preferred_element_type=jnp.float32)


def rough_mm(left, right):
    return jnp.dot(left, right, preferred_element_type=jnp.float32)


def mm_t(left, right):
    return lax.dot_general(
        left, right, (((1,), (1,)), ((), ())), precision=HIGHEST, preferred_element_type=jnp.float32
    )


def tree_sum(terms):
    terms = list(terms)
    while len(terms) > 1:
        terms = [
            terms[i] + terms[i + 1] if i + 1 < len(terms) else terms[i] for i in range(0, len(terms), 2)
        ]
    return terms[0]


def reciprocal(value):
    guess = pl.reciprocal(value, approx=True)
    for _ in range(REFINES):
        guess = guess * (2.0 - value * guess)
    return guess


def small_inverse(entries, size):
    def at(table, a, b):
        return table[(min(a, b), max(a, b))]

    if size == 1:
        return {(0, 0): reciprocal(entries[(0, 0)])}
    if size == 2:
        det = entries[(0, 0)] * entries[(1, 1)] - entries[(0, 1)] * entries[(0, 1)]
        inv = reciprocal(det)
        return {(0, 0): entries[(1, 1)] * inv, (1, 1): entries[(0, 0)] * inv, (0, 1): -entries[(0, 1)] * inv}
    half = size // 2
    idx = range(half)
    upper = [(a, b) for a in idx for b in range(a, half)]
    first = small_inverse({(a, b): entries[(a, b)] for a, b in upper}, half)
    cross = [[entries[(a, half + b)] for b in idx] for a in idx]
    lift = [[tree_sum(at(first, a, c) * cross[c][b] for c in idx) for b in idx] for a in idx]
    schur = {
        (a, b): entries[(half + a, half + b)] - tree_sum(cross[c][a] * lift[c][b] for c in idx)
        for a, b in upper
    }
    last = small_inverse(schur, half)
    mixed = [[tree_sum(lift[a][c] * at(last, c, b) for c in idx) for b in idx] for a in idx]
    result = {}
    for a, b in upper:
        result[(half + a, half + b)] = last[(a, b)]
        result[(a, b)] = first[(a, b)] + tree_sum(mixed[a][c] * lift[b][c] for c in idx)
    for a in idx:
        for b in idx:
            result[(a, half + b)] = -mixed[a][b]
    return result


def pivot_inverse(matrix):
    size = matrix.shape[0]
    lane = lax.broadcasted_iota(jnp.int32, (8, size), 1)
    sub = lax.broadcasted_iota(jnp.int32, (8, size), 0)
    parts = [matrix[8 * i : 8 * i + 8, :] for i in range(size // 8)]
    idx = range(PIVOT)
    upper = [(a, b) for a in idx for b in range(a, PIVOT)]

    def row(r):
        return jnp.broadcast_to(parts[r // 8][r % 8 : r % 8 + 1, :], (8, size))

    def entry(values, c):
        return jnp.broadcast_to(values[:, c : c + 1], (8, size))

    entries = None
    for k in range(0, size, PIVOT):
        home, first = k // 8, k % 8
        rows = [row(k + a) for a in idx]
        if entries is None:
            entries = {(a, b): entry(rows[a], k + b) for a, b in upper}
        ahead = AHEAD and k + PIVOT < size
        if ahead:
            later = k + PIVOT
            side = [[entry(rows[a], later + b) for b in idx] for a in idx]
            later_rows = [row(later + a) for a in idx]
            later_entries = {(a, b): entry(later_rows[a], later + b) for a, b in upper}
        inverse = small_inverse(entries, PIVOT)
        full = [[inverse[(min(a, b), max(a, b))] for b in idx] for a in idx]
        entries = None
        if ahead:
            lift = [[tree_sum(full[a][c] * side[c][b] for c in idx) for b in idx] for a in idx]
            entries = {
                (a, b): later_entries[(a, b)] - tree_sum(side[c][a] * lift[c][b] for c in idx)
                for a, b in upper
            }
        here = (lane >= k) & (lane < k + PIVOT)
        rows = [jnp.where(here, jnp.where(lane == k + a, 1.0, 0.0), rows[a]) for a in idx]
        scaled = [tree_sum(full[a][b] * rows[b] for b in idx) for a in idx]
        updated = []
        for i, part in enumerate(parts):
            columns = [entry(part, k + a) for a in idx]
            base = jnp.where(here, 0.0, part)
            if i == home:
                inside = (sub >= first) & (sub < first + PIVOT)
                base = jnp.where(inside, 0.0, base)
                columns = [
                    jnp.where(inside, jnp.where(sub == first + a, -1.0, 0.0), column)
                    for a, column in enumerate(columns)
                ]
            updated.append(base - tree_sum(columns[a] * scaled[a] for a in idx))
        parts = updated
    return jnp.concatenate(parts, axis=0)


def block_inverse(matrix):
    size = matrix.shape[0]
    if size <= BASE:
        return pivot_inverse(matrix)
    half = size // 2
    corner, side = matrix[:half, :half], matrix[:half, half:]
    first = block_inverse(corner)
    lift = mm(first, side)
    last = block_inverse(matrix[half:, half:] - mm(side.T, lift))
    mixed = mm(lift, last)
    top = jnp.concatenate([first + mm(mixed, lift.T), -mixed], axis=1)
    return jnp.concatenate([top, jnp.concatenate([-mixed.T, last], axis=1)], axis=0)


def assemble(core_ref, own_ref, other_ref, system_ref):
    half = system_ref.shape[0] // 2
    count = half // TILE

    def put(row, column, block):
        system_ref[row : row + TILE, column : column + TILE] = block

    flag = jnp.zeros((TILE, TILE), jnp.int32) + core_ref[0] == 0

    def tile(at, share):
        own, other = own_ref[at : at + TILE, :], other_ref[at : at + TILE, :]
        return jnp.where(flag, own, other) if share == 0 else jnp.where(flag, other, own)

    for share, corner in ((0, 0), (1, half)):
        at = 0
        for i in range(count):
            for j in range(i, count):
                block = tile(at, share)
                at += TILE
                if i == j:
                    put(corner + i * TILE, corner + i * TILE, 0.5 * (block + block.T))
                else:
                    put(corner + i * TILE, corner + j * TILE, block)
                    put(corner + j * TILE, corner + i * TILE, block.T)
    share_columns = count // 2
    for share in (0, 1):
        at = count * (count + 1) // 2 * TILE
        for j in range(share * share_columns, (share + 1) * share_columns):
            for i in range(count):
                block = tile(at, share)
                at += TILE
                put(i * TILE, half + j * TILE, block)
                put(half + j * TILE, i * TILE, block.T)


def eliminate(inverse_ref, begin, end):
    size = inverse_ref.shape[0]
    count = size // TILE
    row_id = lax.broadcasted_iota(jnp.int32, (TILE, TILE), 0)
    column_id = lax.broadcasted_iota(jnp.int32, (TILE, TILE), 1)

    def span(index):
        return pl.ds(pl.multiple_of(index * TILE, TILE), TILE)

    def step(k, carry):
        own = span(k)
        block = block_inverse(inverse_ref[own, own])
        inverse_ref[own, own] = jnp.where(row_id == column_id, 1.0, 0.0)
        scaled = mm(block, inverse_ref[own, :])
        inverse_ref[own, :] = scaled
        for ahead in range(1, count):
            other = span(lax.rem(k + ahead, count))
            column = inverse_ref[other, own]
            inverse_ref[other, own] = jnp.zeros((TILE, TILE), jnp.float32)
            inverse_ref[other, :] = inverse_ref[other, :] - mm(column, scaled)
        return carry

    lax.fori_loop(begin, end, step, 0)


def inverse_kernel(place_ref, *refs):
    shares, (system_ref, inverse_ref, solved_ref, own_ref, other_ref) = refs[:-5], refs[-5:]
    leaves = len(shares) // 2
    rows = shares[0].shape[0]
    for m in range(leaves):
        at = pl.ds(pl.multiple_of((place_ref[1] ^ m) * rows, rows), rows)
        own_ref[at, :] = shares[m][...]
        other_ref[at, :] = shares[leaves + m][...]
    assemble(place_ref, own_ref, other_ref, system_ref)
    inverse_ref[...] = system_ref[...]
    count = system_ref.shape[0] // TILE
    eliminate(inverse_ref, 0, count)
    samples = solved_ref.shape[0]
    begin = own_ref.shape[0] - count * samples
    rhs = jnp.concatenate(
        [own_ref[begin + i * samples : begin + (i + 1) * samples, :] for i in range(count)], axis=1
    )
    guess = mm(rhs, inverse_ref[...])
    solved_ref[...] = guess + rough_mm(rhs - mm(guess, system_ref[...]), inverse_ref[...])


def image_kernel(
    core_ref, solved_ref, sketch_ref, own_ref, other_ref, rhs_ref, image_rhs_ref,
    sketches_ref, direction_ref, image_ref, packet_ref,
):
    half, width = own_ref.shape
    core = core_ref[0]
    sketches_ref[:, :width] = sketch_ref[...]
    sketches_ref[pl.ds(pl.multiple_of(core * half, half), half), width:] = own_ref[...]
    sketches_ref[pl.ds(pl.multiple_of((1 - core) * half, half), half), width:] = other_ref[...]
    taken = mm(solved_ref[...], sketches_ref[...])
    rhs = rhs_ref[...]
    direction = (rhs - taken[:, :width]) / noise_variance
    image = (image_rhs_ref[...] - taken[:, width:]) / noise_variance
    direction_ref[...] = direction
    image_ref[...] = image
    moved = mm_t(image, sketch_ref[...])
    samples = rhs.shape[0]
    count = moved.shape[1] // TILE
    for i in range(count):
        packet_ref[i * samples : (i + 1) * samples, :] = moved[:, i * TILE : (i + 1) * TILE]
    at = count * samples
    ones = jnp.ones((8, width), jnp.float32)
    packet_ref[at : at + 8, :] = jnp.zeros((8, TILE), jnp.float32)
    packet_ref[at : at + 1, :samples] = mm_t(ones, rhs * direction)[0:1, :]
    packet_ref[at + 1 : at + 2, :samples] = mm_t(ones, direction * image)[0:1, :]
    at += 8
    for i in range(width // TILE):
        packet_ref[at : at + samples, :] = image[:, i * TILE : (i + 1) * TILE]
        at += samples


def prepare_kernel(
    core_ref, points_ref, neighbors_ref, omega_ref, observed_ref, prior_ref, first_ref, second_ref, meta_ref, own_ref, rhs_ref,
    points_vmem, neighbors_vmem, observed_vmem, prior_vmem, sems,
):
    split = second_ref.shape[0]
    samples = prior_vmem.shape[0]
    begin = pl.multiple_of(core_ref[0] * (2 * split), 2 * split)
    copies = [
        pltpu.make_async_copy(source, target, sems.at[i])
        for i, (source, target) in enumerate(
            (
                (omega_ref.at[pl.ds(begin, split), :], first_ref.at[0:split, :]),
                (omega_ref.at[pl.ds(begin + split, split), :], second_ref),
                (points_ref, points_vmem),
                (neighbors_ref, neighbors_vmem),
                (observed_ref, observed_vmem),
                (prior_ref, prior_vmem),
            )
        )
    ]
    for copy in copies:
        copy.start()
    meta_ref[...] = jnp.full(meta_ref.shape, -1.0, jnp.float32)
    for copy in copies:
        copy.wait()
    own_ref[0:split, :] = first_ref[0:split, :]
    own_ref[split:, :] = second_ref[...]
    rhs_ref[...] = observed_vmem[...] - prior_vmem[...]
    first_ref[split : split + samples, :] = rhs_ref[...]
    meta_ref[0:3, :] = points_vmem[...]
    meta_ref[3:4, : neighbors_vmem.shape[1]] = neighbors_vmem[...].astype(jnp.float32)
    first_ref[split + samples :, :] = meta_ref[...]


def prepare(core, points, neighbors, omega, observed, prior, split):
    width = omega.shape[1]
    samples = prior.shape[0]
    vmem = pl.BlockSpec(memory_space=pltpu.VMEM)
    hbm = pl.BlockSpec(memory_space=pl.ANY)
    shapes = [(split + samples + 8, width), (split, width), (8, width), (2 * split, width), (samples, width)]
    return pl.pallas_call(
        prepare_kernel,
        out_shape=tuple(jax.ShapeDtypeStruct(shape, jnp.float32) for shape in shapes),
        in_specs=[pl.BlockSpec(memory_space=pltpu.SMEM)] + [hbm] * 5,
        out_specs=(vmem,) * 5,
        scratch_shapes=[
            pltpu.VMEM(points.shape, jnp.float32),
            pltpu.VMEM(neighbors.shape, jnp.int32),
            pltpu.VMEM(observed.shape, jnp.float32),
            pltpu.VMEM(prior.shape, jnp.float32),
            pltpu.SemaphoreType.DMA((6,)),
        ],
        name="prepare",
        cost_estimate=pl.CostEstimate(flops=10**6, bytes_accessed=2**19, transcendentals=0),
    )(core, points, neighbors, omega, observed, prior)


def targets_kernel(ids_ref, *refs):
    count = len(refs) // 3
    width = refs[0].shape[1]
    for meta_ref, rows_ref, weight_ref in zip(refs[:count], refs[count : 2 * count], refs[2 * count :]):
        rows_ref[...] = meta_ref[0:3, :]
        listed = meta_ref[3:4, :]
        for m in range(weight_ref.shape[1] // width):
            same = listed == jnp.zeros((1, width), jnp.float32) + ids_ref[m].astype(jnp.float32)
            found = jnp.sum(jnp.where(same, 1.0, 0.0), axis=1, keepdims=True)
            weight_ref[:, m * width : (m + 1) * width] = jnp.broadcast_to(found, (1, width))


def payload_kernel(place_ref, omega_ref, own_ref, other_ref, rhs_ref, sketch_ref, *refs):
    half, width = own_ref.shape
    split = half // 2
    core, leaf = place_ref[0], place_ref[1]
    shares, payload_ref = refs[:-1], refs[-1]
    begin = pl.multiple_of(core * half, half)
    sketch_ref[pl.ds(begin, half), :] = own_ref[...]
    sketch_ref[pl.ds(pl.multiple_of((1 - core) * half, half), half), :] = other_ref[...]
    own, other = own_ref[...], other_ref[...]
    lifted = noise_variance * omega_ref[...] + own
    count = half // TILE
    at = 0
    for i in range(count):
        product = mm_t(lifted[i * TILE : (i + 1) * TILE], own[i * TILE :])
        for j in range(count - i):
            payload_ref[at : at + TILE, :] = product[:, j * TILE : (j + 1) * TILE]
            at += TILE
    on_first = jnp.zeros((half, width), jnp.int32) + core == 0
    left = jnp.where(on_first, lifted, other)
    right = jnp.where(on_first[:split], other[:split], lifted[split:])
    product = mm_t(left, right)
    for j in range(split // TILE):
        payload_ref[at : at + half, :] = product[:, j * TILE : (j + 1) * TILE]
        at += half
    product = mm_t(rhs_ref[...], sketch_ref[...])
    samples = rhs_ref.shape[0]
    for j in range(2 * count):
        payload_ref[at : at + samples, :] = product[:, j * TILE : (j + 1) * TILE]
        at += samples
    rows = shares[0].shape[0]
    for m, share in enumerate(shares):
        share[...] = payload_ref[pl.ds(pl.multiple_of((leaf ^ m) * rows, rows), rows), :]


def kernel_call(kernel, name, outputs, *operands, scratch=(), flops=10**8):
    vmem = pl.BlockSpec(memory_space=pltpu.VMEM)
    smem = pl.BlockSpec(memory_space=pltpu.SMEM)
    return pl.pallas_call(
        kernel,
        out_shape=tuple(jax.ShapeDtypeStruct(shape, jnp.float32) for shape in outputs),
        in_specs=[smem if o.ndim == 1 else vmem for o in operands],
        out_specs=(vmem,) * len(outputs),
        scratch_shapes=[pltpu.VMEM(shape, jnp.float32) for shape in scratch],
        name=name,
        compiler_params=pltpu.CompilerParams(vmem_limit_bytes=12 * 2**20),
        cost_estimate=pl.CostEstimate(flops=flops, bytes_accessed=2**20, transcendentals=0),
    )(*operands)


def shifted(values, axis, distance):
    size = lax.axis_size(axis)
    return lax.ppermute(values, axis, [(i, (i + distance) % size) for i in range(size)])


def swapped(values, axis, mask):
    size = lax.axis_size(axis)
    return lax.ppermute(values, axis, [(i, i ^ mask) for i in range(size)])


def slab(values):
    return [values] + [swapped(values, "leaf", m) for m in range(1, lax.axis_size("leaf"))]


def group_size():
    return lax.axis_size(POINT_AXES)


def exchange(values):
    return lax.all_to_all(values, POINT_AXES, 0, 0, tiled=True)


def axis_sum(values, axis):
    if lax.axis_size(axis) != 4:
        return lax.psum(values, axis)
    one, two, three = (swapped(values, axis, m) for m in (1, 2, 3))
    return (values + one) + (two + three)


def spread(values):
    count = group_size()
    sent = jnp.broadcast_to(values[None], (count,) + values.shape).reshape(-1, values.shape[1])
    return exchange(sent).reshape((count,) + values.shape)


def to_tiles(values):
    return jnp.concatenate([values[:, c : c + TILE] for c in range(0, values.shape[1], TILE)], axis=0)


def from_tiles(tiles, rows):
    return jnp.concatenate([tiles[r : r + rows] for r in range(0, tiles.shape[0], rows)], axis=1)


def dot_rows(left, right):
    return jnp.sum(left * right, axis=1)


def local(points, neighbors, omega, observed, prior_draws):
    cycle = lax.axis_size("blk")
    leaves = lax.axis_size("leaf")
    cores = lax.axis_size("samp")
    own_slab, own_leaf, own_core = (lax.axis_index(a) for a in ("blk", "leaf", "samp"))
    sketch_size, width = omega.shape
    half = sketch_size // cores
    samples = prior_draws.shape[0]
    period = 2.0 * cycle

    core = own_core.astype(jnp.int32).reshape(1)
    place = jnp.stack([own_core, own_leaf]).astype(jnp.int32)
    split = half // 2
    first_block, second_block, meta, omega_half, rhs = prepare(
        core, points, neighbors, omega, observed[None, :], prior_draws, split
    )

    def other_core(values):
        return swapped(values, "samp", 1)

    def sent(upward, downward):
        return shifted(upward, "blk", 1), shifted(downward, "blk", -1)

    first_blocks, second_blocks = slab(first_block), slab(second_block)
    route = [
        (b * cores + c, (b + (1 if c == 0 else -1)) % cycle * cores + c) for b in range(cycle) for c in range(cores)
    ]
    arrived = lax.ppermute(meta, ("blk", "samp"), route)
    swapped_meta = other_core(arrived)
    above = jnp.where(own_core == 0, swapped_meta, arrived)
    below = jnp.where(own_core == 0, arrived, swapped_meta)
    begin = split + samples
    sources = jnp.concatenate([b[begin : begin + 3] for b in first_blocks], axis=1)
    source_ids = (own_slab * leaves + jnp.stack([own_leaf ^ m for m in range(leaves)])).astype(jnp.int32)
    tables = kernel_call(
        targets_kernel,
        "targets",
        [(3, width)] * 3 + [(1, leaves * width)] * 3,
        source_ids,
        above,
        meta,
        below,
    )
    targets, weights = tables[:3], tables[3:]

    def kernel_columns(index):
        offset = sources[:, :, None] - targets[index][:, None, :]
        along = offset[0]
        along = jnp.where(along >= 0.5 * period, along - period, along)
        along = jnp.where(along < -0.5 * period, along + period, along)
        squared = along * along + offset[1] * offset[1] + offset[2] * offset[2]
        radius = jnp.sqrt(squared) / support_radius
        remain = jnp.maximum(1.0 - radius, 0.0)
        squared_remain = remain * remain
        values = squared_remain * squared_remain * (4.0 * radius + 1.0)
        return values * weights[index].reshape(-1, 1)

    columns = [kernel_columns(i) for i in range(3)]

    def sums(values):
        gathered = jnp.concatenate(values, axis=1)
        return mm(gathered, columns[0]), mm(gathered, columns[2]), gathered

    upward, downward, gathered = sums([b[:begin] for b in first_blocks])
    _, _, *second_blocks = lax.optimization_barrier((upward, downward, *second_blocks))
    from_below, from_above = sent(upward, downward)
    applied = mm(gathered, columns[1]) + from_below + from_above
    upward, downward, gathered = sums(second_blocks)
    from_below, from_above = sent(upward, downward)
    applied_second = mm(gathered, columns[1]) + from_below + from_above
    sketch_half = jnp.concatenate([applied[:split], applied_second], axis=0) + sketch_shift * omega_half
    image_rhs = applied[split:] + noise_variance * rhs

    count = half // TILE
    matrix_rows = (count * (count + 1) // 2 + count * count // 2) * TILE
    payload_rows = matrix_rows + samples * (sketch_size // TILE)
    sketch, *shares = kernel_call(
        payload_kernel,
        "payload",
        [(sketch_size, width)] + [(payload_rows // leaves, TILE)] * leaves,
        place,
        omega_half,
        sketch_half,
        other_core(sketch_half),
        rhs,
        scratch=[(payload_rows, TILE)],
        flops=10**9,
    )

    *shares, late_sketch = lax.optimization_barrier((*shares, sketch_half))
    share = shares[0]
    for m in range(1, leaves):
        share = share + swapped(shares[m], "leaf", m)
    upward, downward, gathered = sums(slab(late_sketch))
    here = mm(gathered, columns[1]) + noise_variance * late_sketch
    shares = slab(axis_sum(share, "blk"))
    *shares, upward, downward, here = lax.optimization_barrier((*shares, upward, downward, here))
    other_shares = [other_core(s) for s in shares]
    from_below, from_above = sent(upward, downward)
    system, inverse, solved = kernel_call(
        inverse_kernel,
        "inverse_and_solve",
        [(sketch_size, sketch_size)] * 2 + [(samples, sketch_size)],
        place,
        *shares,
        *other_shares,
        scratch=[(payload_rows, TILE)] * 2,
        flops=30 * 10**9,
    )
    from_below, from_above, solved = lax.optimization_barrier((from_below, from_above, solved))
    own_image = here + from_below + from_above

    sum_rows = samples * (sketch_size // TILE) + 8
    sketches, direction, image, packet = kernel_call(
        image_kernel,
        "image",
        [(sketch_size, 2 * width)] + [(samples, width)] * 2 + [(sum_rows + samples * (width // TILE), TILE)],
        core,
        solved,
        sketch,
        own_image,
        other_core(own_image),
        rhs,
        image_rhs,
    )
    packets = slab(packet)
    slab_sum = (packets[0][:sum_rows] + packets[1][:sum_rows]) + (packets[2][:sum_rows] + packets[3][:sum_rows])
    upward, downward, gathered = sums([from_tiles(p[sum_rows:], samples) for p in packets])
    here = mm(gathered, columns[1]) + noise_variance * image
    if cycle == 4:
        even = own_slab % 2 == 0
        one, three = (
            swapped(jnp.concatenate([slab_sum, to_tiles(jnp.where(even, first, second))], axis=0), "blk", m)
            for m, first, second in ((1, upward, downward), (3, downward, upward))
        )
        two = swapped(slab_sum, "blk", 2)
        total = (slab_sum + one[:sum_rows]) + (two + three[:sum_rows])
        from_below, from_above = from_tiles(one[sum_rows:], samples), from_tiles(three[sum_rows:], samples)
    else:
        total = lax.psum(slab_sum, "blk")
        from_below, from_above = sent(upward, downward)
    image_twice = here + from_below + from_above
    solves = mm(inverse, sketches)
    solves = solves + rough_mm(inverse, sketches - mm(system, solves))
    moved = from_tiles(total[:-8], samples)
    dots = total[-8:]
    inner_first, curvature = dots[0, :samples, None], dots[1, :samples, None]
    step = inner_first / curvature

    taken = mm(moved, solves)
    precond = direction - step * ((image - taken[:, :width]) / noise_variance)
    image_precond = image - step * ((image_twice - taken[:, width:]) / noise_variance)
    residual = rhs - step * image
    dots = jnp.stack([dot_rows(residual, precond), dot_rows(precond, image_precond), dot_rows(precond, image)])
    dots = spread(jnp.pad(dots, ((0, 5), (0, TILE - samples)))).sum(axis=0)
    inner_second, curvature_precond, mixed = (dots[i, :samples, None] for i in range(3))
    beta = inner_second / inner_first
    step_second = inner_second / (curvature_precond + beta * (2.0 * mixed + beta * curvature))
    weights = step * direction + step_second * (precond + beta * direction)
    residual = residual - step_second * (image_precond + beta * image)
    return (weights, residual)


def solution(mesh):
    in_specs = (
        P(None, ("blk", "leaf")),
        P(("blk", "leaf"), None),
        P(None, ("blk", "leaf")),
        P(("blk", "leaf")),
        P("samp", ("blk", "leaf")),
    )
    out_specs = (P("samp", ("blk", "leaf")), P("samp", ("blk", "leaf")))
    return jax.shard_map(local, mesh=mesh, in_specs=in_specs, out_specs=out_specs, check_vma=False)
```

```python
import functools

import jax
import jax.numpy as jnp
from jax import lax
from jax.experimental import pallas as pl
from jax.experimental.pallas import tpu as pltpu
from jax.sharding import PartitionSpec as P

support_radius = 0.8
noise_variance = 1.0
sketch_shift = 1.0
HIGHEST = lax.Precision.HIGHEST
POINT_AXES = ("blk", "leaf")
TILE = 128
BASE, REFINES = 128, 1


def mm(left, right):
    return jnp.dot(left, right, precision=HIGHEST, preferred_element_type=jnp.float32)


def rough_mm(left, right):
    return jnp.dot(left, right, preferred_element_type=jnp.float32)


def mm_t(left, right):
    return lax.dot_general(
        left, right, (((1,), (1,)), ((), ())), precision=HIGHEST, preferred_element_type=jnp.float32
    )


def tree_sum(terms):
    terms = list(terms)
    while len(terms) > 1:
        terms = [
            terms[i] + terms[i + 1] if i + 1 < len(terms) else terms[i] for i in range(0, len(terms), 2)
        ]
    return terms[0]


def reciprocal(value):
    guess = pl.reciprocal(value, approx=True)
    for _ in range(REFINES):
        guess = guess * (2.0 - value * guess)
    return guess


def pair_inverse(a, b, c):
    inv = reciprocal(a * c - b * b)
    return c * inv, -(b * inv), a * inv


def quad_solve(entries, rows):
    a0, a1, a2 = pair_inverse(entries[(0, 0)], entries[(0, 1)], entries[(1, 1)])
    cross = [[entries[(a, 2 + b)] for b in (0, 1)] for a in (0, 1)]
    lift = [
        [a0 * cross[0][b] + a1 * cross[1][b] for b in (0, 1)],
        [a1 * cross[0][b] + a2 * cross[1][b] for b in (0, 1)],
    ]
    s0, s1, s2 = pair_inverse(
        *(
            entries[(2 + a, 2 + b)] - (cross[0][a] * lift[0][b] + cross[1][a] * lift[1][b])
            for a, b in ((0, 0), (0, 1), (1, 1))
        )
    )
    solved = []
    for r0, r1, r2, r3 in zip(*rows):
        u0 = r2 - (lift[0][0] * r0 + lift[1][0] * r1)
        u1 = r3 - (lift[0][1] * r0 + lift[1][1] * r1)
        x2, x3 = s0 * u0 + s1 * u1, s1 * u0 + s2 * u1
        x0 = (a0 * r0 + a1 * r1) - (lift[0][0] * x2 + lift[0][1] * x3)
        x1 = (a1 * r0 + a2 * r1) - (lift[1][0] * x2 + lift[1][1] * x3)
        solved.append((x0, x1, x2, x3))
    return [list(row) for row in zip(*solved)]


def pivot_inverse(matrix):
    size = matrix.shape[0]
    lane = lax.broadcasted_iota(jnp.int32, (8, size), 1)
    sub = lax.broadcasted_iota(jnp.int32, (8, size), 0)
    parts = [matrix[8 * i : 8 * i + 8, :] for i in range(size // 8)]
    four = range(4)

    def row(values, r):
        return jnp.broadcast_to(values[r : r + 1, :], (8, size))

    def column(values, c):
        return jnp.broadcast_to(values[:, c : c + 1], (8, size))

    for home in range(size // 8):
        k = 8 * home
        here = (lane >= k) & (lane < k + 8)
        pivots = [column(parts[home], k + b) for b in range(8)]
        entries = {(a, b): row(pivots[b], a) for a in range(8) for b in range(a, 8)}
        rows = [
            jnp.where(here, jnp.where(lane == k + a, 1.0, 0.0), row(parts[home], a)) for a in range(8)
        ]
        cross = [[entries[(a, 4 + b)] for b in four] for a in four]
        first = quad_solve(entries, [cross[a] + [rows[a]] for a in four])
        lift = [first[a][:4] for a in four]
        schur = {
            (a, b): entries[(4 + a, 4 + b)] - tree_sum(cross[c][a] * lift[c][b] for c in four)
            for a in four
            for b in range(a, 4)
        }
        last = [[rows[4 + a] - tree_sum(lift[c][a] * rows[c] for c in four)] for a in four]
        last = [values[0] for values in quad_solve(schur, last)]
        scaled = [first[a][4] - tree_sum(lift[a][c] * last[c] for c in four) for a in four] + last
        updated = []
        for i, part in enumerate(parts):
            if i == home:
                fresh = scaled[7]
                for a in range(7):
                    fresh = jnp.where(sub == a, scaled[a], fresh)
                updated.append(fresh)
            else:
                taken = tree_sum(column(part, k + a) * scaled[a] for a in range(8))
                updated.append(jnp.where(here, 0.0, part) - taken)
        parts = updated
    return jnp.concatenate(parts, axis=0)


def block_inverse(matrix):
    size = matrix.shape[0]
    if size <= BASE:
        return pivot_inverse(matrix)
    half = size // 2
    corner, side = matrix[:half, :half], matrix[:half, half:]
    first = block_inverse(corner)
    lift = mm(first, side)
    last = block_inverse(matrix[half:, half:] - mm(side.T, lift))
    mixed = mm(lift, last)
    top = jnp.concatenate([first + mm(mixed, lift.T), -mixed], axis=1)
    return jnp.concatenate([top, jnp.concatenate([-mixed.T, last], axis=1)], axis=0)


def assemble(core_ref, own_ref, other_ref, system_ref):
    half = system_ref.shape[0] // 2
    count = half // TILE

    def put(row, column, block):
        system_ref[row : row + TILE, column : column + TILE] = block

    flag = jnp.zeros((TILE, TILE), jnp.int32) + core_ref[0] == 0

    def tile(at, share):
        own, other = own_ref[at : at + TILE, :], other_ref[at : at + TILE, :]
        return jnp.where(flag, own, other) if share == 0 else jnp.where(flag, other, own)

    for share, corner in ((0, 0), (1, half)):
        at = 0
        for i in range(count):
            for j in range(i, count):
                block = tile(at, share)
                at += TILE
                if i == j:
                    put(corner + i * TILE, corner + i * TILE, 0.5 * (block + block.T))
                else:
                    put(corner + i * TILE, corner + j * TILE, block)
                    put(corner + j * TILE, corner + i * TILE, block.T)
    share_columns = count // 2
    for share in (0, 1):
        at = count * (count + 1) // 2 * TILE
        for j in range(share * share_columns, (share + 1) * share_columns):
            for i in range(count):
                block = tile(at, share)
                at += TILE
                put(i * TILE, half + j * TILE, block)
                put(half + j * TILE, i * TILE, block.T)


def eliminate(inverse_ref, begin, end):
    size = inverse_ref.shape[0]
    count = size // TILE
    row_id = lax.broadcasted_iota(jnp.int32, (TILE, TILE), 0)
    column_id = lax.broadcasted_iota(jnp.int32, (TILE, TILE), 1)

    def span(index):
        return pl.ds(pl.multiple_of(index * TILE, TILE), TILE)

    def step(k, carry):
        own = span(k)
        block = block_inverse(inverse_ref[own, own])
        inverse_ref[own, own] = jnp.where(row_id == column_id, 1.0, 0.0)
        scaled = mm(block, inverse_ref[own, :])
        inverse_ref[own, :] = scaled
        for ahead in range(1, count):
            other = span(lax.rem(k + ahead, count))
            column = inverse_ref[other, own]
            inverse_ref[other, own] = jnp.zeros((TILE, TILE), jnp.float32)
            inverse_ref[other, :] = inverse_ref[other, :] - mm(column, scaled)
        return carry

    lax.fori_loop(begin, end, step, 0)


def inverse_kernel(place_ref, *refs):
    shares, (system_ref, inverse_ref, solved_ref, own_ref, other_ref) = refs[:-5], refs[-5:]
    leaves = len(shares) // 2
    rows = shares[0].shape[0]
    for m in range(leaves):
        at = pl.ds(pl.multiple_of((place_ref[1] ^ m) * rows, rows), rows)
        own_ref[at, :] = shares[m][...]
        other_ref[at, :] = shares[leaves + m][...]
    assemble(place_ref, own_ref, other_ref, system_ref)
    inverse_ref[...] = system_ref[...]
    count = system_ref.shape[0] // TILE
    eliminate(inverse_ref, 0, count)
    samples = solved_ref.shape[0]
    begin = own_ref.shape[0] - count * samples
    rhs = jnp.concatenate(
        [own_ref[begin + i * samples : begin + (i + 1) * samples, :] for i in range(count)], axis=1
    )
    guess = mm(rhs, inverse_ref[...])
    solved_ref[...] = guess + rough_mm(rhs - mm(guess, system_ref[...]), inverse_ref[...])


def image_kernel(
    core_ref, solved_ref, sketch_ref, own_ref, other_ref, rhs_ref, image_rhs_ref,
    sketches_ref, direction_ref, image_ref, packet_ref,
):
    half, width = own_ref.shape
    core = core_ref[0]
    sketches_ref[:, :width] = sketch_ref[...]
    sketches_ref[pl.ds(pl.multiple_of(core * half, half), half), width:] = own_ref[...]
    sketches_ref[pl.ds(pl.multiple_of((1 - core) * half, half), half), width:] = other_ref[...]
    taken = mm(solved_ref[...], sketches_ref[...])
    rhs = rhs_ref[...]
    direction = (rhs - taken[:, :width]) / noise_variance
    image = (image_rhs_ref[...] - taken[:, width:]) / noise_variance
    direction_ref[...] = direction
    image_ref[...] = image
    moved = mm_t(image, sketch_ref[...])
    samples = rhs.shape[0]
    count = moved.shape[1] // TILE
    for i in range(count):
        packet_ref[i * samples : (i + 1) * samples, :] = moved[:, i * TILE : (i + 1) * TILE]
    at = count * samples
    ones = jnp.ones((8, width), jnp.float32)
    packet_ref[at : at + 8, :] = jnp.zeros((8, TILE), jnp.float32)
    packet_ref[at : at + 1, :samples] = mm_t(ones, rhs * direction)[0:1, :]
    packet_ref[at + 1 : at + 2, :samples] = mm_t(ones, direction * image)[0:1, :]
    at += 8
    for i in range(width // TILE):
        packet_ref[at : at + samples, :] = image[:, i * TILE : (i + 1) * TILE]
        at += samples


def prepare_kernel(
    core_ref, points_ref, neighbors_ref, omega_ref, observed_ref, prior_ref, first_ref, second_ref, meta_ref, own_ref, rhs_ref,
    points_vmem, neighbors_vmem, observed_vmem, prior_vmem, sems,
):
    split = second_ref.shape[0]
    samples = prior_vmem.shape[0]
    begin = pl.multiple_of(core_ref[0] * (2 * split), 2 * split)
    copies = [
        pltpu.make_async_copy(source, target, sems.at[i])
        for i, (source, target) in enumerate(
            (
                (omega_ref.at[pl.ds(begin, split), :], first_ref.at[0:split, :]),
                (omega_ref.at[pl.ds(begin + split, split), :], second_ref),
                (points_ref, points_vmem),
                (neighbors_ref, neighbors_vmem),
                (observed_ref, observed_vmem),
                (prior_ref, prior_vmem),
            )
        )
    ]
    for copy in copies:
        copy.start()
    meta_ref[...] = jnp.full(meta_ref.shape, -1.0, jnp.float32)
    for copy in copies:
        copy.wait()
    own_ref[0:split, :] = first_ref[0:split, :]
    own_ref[split:, :] = second_ref[...]
    rhs_ref[...] = observed_vmem[...] - prior_vmem[...]
    first_ref[split : split + samples, :] = rhs_ref[...]
    meta_ref[0:3, :] = points_vmem[...]
    meta_ref[3:4, : neighbors_vmem.shape[1]] = neighbors_vmem[...].astype(jnp.float32)
    first_ref[split + samples :, :] = meta_ref[...]


def prepare(core, points, neighbors, omega, observed, prior, split):
    width = omega.shape[1]
    samples = prior.shape[0]
    vmem = pl.BlockSpec(memory_space=pltpu.VMEM)
    hbm = pl.BlockSpec(memory_space=pl.ANY)
    shapes = [(split + samples + 8, width), (split, width), (8, width), (2 * split, width), (samples, width)]
    return pl.pallas_call(
        prepare_kernel,
        out_shape=tuple(jax.ShapeDtypeStruct(shape, jnp.float32) for shape in shapes),
        in_specs=[pl.BlockSpec(memory_space=pltpu.SMEM)] + [hbm] * 5,
        out_specs=(vmem,) * 5,
        scratch_shapes=[
            pltpu.VMEM(points.shape, jnp.float32),
            pltpu.VMEM(neighbors.shape, jnp.int32),
            pltpu.VMEM(observed.shape, jnp.float32),
            pltpu.VMEM(prior.shape, jnp.float32),
            pltpu.SemaphoreType.DMA((6,)),
        ],
        name="prepare",
        cost_estimate=pl.CostEstimate(flops=10**6, bytes_accessed=2**19, transcendentals=0),
    )(core, points, neighbors, omega, observed, prior)


def targets_kernel(ids_ref, *refs):
    count = len(refs) // 3
    width = refs[0].shape[1]
    for meta_ref, rows_ref, weight_ref in zip(refs[:count], refs[count : 2 * count], refs[2 * count :]):
        rows_ref[...] = meta_ref[0:3, :]
        listed = meta_ref[3:4, :]
        for m in range(weight_ref.shape[1] // width):
            same = listed == jnp.zeros((1, width), jnp.float32) + ids_ref[m].astype(jnp.float32)
            found = jnp.sum(jnp.where(same, 1.0, 0.0), axis=1, keepdims=True)
            weight_ref[:, m * width : (m + 1) * width] = jnp.broadcast_to(found, (1, width))


def payload_kernel(place_ref, omega_ref, own_ref, other_ref, rhs_ref, sketch_ref, *refs):
    half, width = own_ref.shape
    split = half // 2
    core, leaf = place_ref[0], place_ref[1]
    shares, payload_ref = refs[:-1], refs[-1]
    begin = pl.multiple_of(core * half, half)
    sketch_ref[pl.ds(begin, half), :] = own_ref[...]
    sketch_ref[pl.ds(pl.multiple_of((1 - core) * half, half), half), :] = other_ref[...]
    own, other = own_ref[...], other_ref[...]
    lifted = noise_variance * omega_ref[...] + own
    count = half // TILE
    at = 0
    for i in range(count):
        product = mm_t(lifted[i * TILE : (i + 1) * TILE], own[i * TILE :])
        for j in range(count - i):
            payload_ref[at : at + TILE, :] = product[:, j * TILE : (j + 1) * TILE]
            at += TILE
    on_first = jnp.zeros((half, width), jnp.int32) + core == 0
    left = jnp.where(on_first, lifted, other)
    right = jnp.where(on_first[:split], other[:split], lifted[split:])
    product = mm_t(left, right)
    for j in range(split // TILE):
        payload_ref[at : at + half, :] = product[:, j * TILE : (j + 1) * TILE]
        at += half
    product = mm_t(rhs_ref[...], sketch_ref[...])
    samples = rhs_ref.shape[0]
    for j in range(2 * count):
        payload_ref[at : at + samples, :] = product[:, j * TILE : (j + 1) * TILE]
        at += samples
    rows = shares[0].shape[0]
    for m, share in enumerate(shares):
        share[...] = payload_ref[pl.ds(pl.multiple_of((leaf ^ m) * rows, rows), rows), :]


def kernel_call(kernel, name, outputs, *operands, scratch=(), flops=10**8):
    vmem = pl.BlockSpec(memory_space=pltpu.VMEM)
    smem = pl.BlockSpec(memory_space=pltpu.SMEM)
    return pl.pallas_call(
        kernel,
        out_shape=tuple(jax.ShapeDtypeStruct(shape, jnp.float32) for shape in outputs),
        in_specs=[smem if o.ndim == 1 else vmem for o in operands],
        out_specs=(vmem,) * len(outputs),
        scratch_shapes=[pltpu.VMEM(shape, jnp.float32) for shape in scratch],
        name=name,
        compiler_params=pltpu.CompilerParams(vmem_limit_bytes=12 * 2**20),
        cost_estimate=pl.CostEstimate(flops=flops, bytes_accessed=2**20, transcendentals=0),
    )(*operands)


def shifted(values, axis, distance):
    size = lax.axis_size(axis)
    return lax.ppermute(values, axis, [(i, (i + distance) % size) for i in range(size)])


def swapped(values, axis, mask):
    size = lax.axis_size(axis)
    return lax.ppermute(values, axis, [(i, i ^ mask) for i in range(size)])


def slab(values):
    return [values] + [swapped(values, "leaf", m) for m in range(1, lax.axis_size("leaf"))]


def group_size():
    return lax.axis_size(POINT_AXES)


def exchange(values):
    return lax.all_to_all(values, POINT_AXES, 0, 0, tiled=True)


def axis_sum(values, axis):
    if lax.axis_size(axis) != 4:
        return lax.psum(values, axis)
    one, two, three = (swapped(values, axis, m) for m in (1, 2, 3))
    return (values + one) + (two + three)


def spread(values):
    count = group_size()
    sent = jnp.broadcast_to(values[None], (count,) + values.shape).reshape(-1, values.shape[1])
    return exchange(sent).reshape((count,) + values.shape)


def to_tiles(values):
    return jnp.concatenate([values[:, c : c + TILE] for c in range(0, values.shape[1], TILE)], axis=0)


def from_tiles(tiles, rows):
    return jnp.concatenate([tiles[r : r + rows] for r in range(0, tiles.shape[0], rows)], axis=1)


def dot_rows(left, right):
    return jnp.sum(left * right, axis=1)


def local(points, neighbors, omega, observed, prior_draws):
    cycle = lax.axis_size("blk")
    leaves = lax.axis_size("leaf")
    cores = lax.axis_size("samp")
    own_slab, own_leaf, own_core = (lax.axis_index(a) for a in ("blk", "leaf", "samp"))
    sketch_size, width = omega.shape
    half = sketch_size // cores
    samples = prior_draws.shape[0]
    period = 2.0 * cycle

    core = own_core.astype(jnp.int32).reshape(1)
    place = jnp.stack([own_core, own_leaf]).astype(jnp.int32)
    split = half // 2
    first_block, second_block, meta, omega_half, rhs = prepare(
        core, points, neighbors, omega, observed[None, :], prior_draws, split
    )

    def other_core(values):
        return swapped(values, "samp", 1)

    def sent(upward, downward):
        return shifted(upward, "blk", 1), shifted(downward, "blk", -1)

    first_blocks, second_blocks = slab(first_block), slab(second_block)
    route = [
        (b * cores + c, (b + (1 if c == 0 else -1)) % cycle * cores + c) for b in range(cycle) for c in range(cores)
    ]
    arrived = lax.ppermute(meta, ("blk", "samp"), route)
    swapped_meta = other_core(arrived)
    above = jnp.where(own_core == 0, swapped_meta, arrived)
    below = jnp.where(own_core == 0, arrived, swapped_meta)
    begin = split + samples
    sources = jnp.concatenate([b[begin : begin + 3] for b in first_blocks], axis=1)
    source_ids = (own_slab * leaves + jnp.stack([own_leaf ^ m for m in range(leaves)])).astype(jnp.int32)
    tables = kernel_call(
        targets_kernel,
        "targets",
        [(3, width)] * 3 + [(1, leaves * width)] * 3,
        source_ids,
        above,
        meta,
        below,
    )
    targets, weights = tables[:3], tables[3:]

    def kernel_columns(index):
        offset = sources[:, :, None] - targets[index][:, None, :]
        along = offset[0]
        along = jnp.where(along >= 0.5 * period, along - period, along)
        along = jnp.where(along < -0.5 * period, along + period, along)
        squared = along * along + offset[1] * offset[1] + offset[2] * offset[2]
        radius = jnp.sqrt(squared) / support_radius
        remain = jnp.maximum(1.0 - radius, 0.0)
        squared_remain = remain * remain
        values = squared_remain * squared_remain * (4.0 * radius + 1.0)
        return values * weights[index].reshape(-1, 1)

    columns = [kernel_columns(i) for i in range(3)]

    def sums(values):
        gathered = jnp.concatenate(values, axis=1)
        return mm(gathered, columns[0]), mm(gathered, columns[2]), gathered

    upward, downward, gathered = sums([b[:begin] for b in first_blocks])
    _, _, *second_blocks = lax.optimization_barrier((upward, downward, *second_blocks))
    from_below, from_above = sent(upward, downward)
    applied = mm(gathered, columns[1]) + from_below + from_above
    upward, downward, gathered = sums(second_blocks)
    from_below, from_above = sent(upward, downward)
    applied_second = mm(gathered, columns[1]) + from_below + from_above
    sketch_half = jnp.concatenate([applied[:split], applied_second], axis=0) + sketch_shift * omega_half
    image_rhs = applied[split:] + noise_variance * rhs

    count = half // TILE
    matrix_rows = (count * (count + 1) // 2 + count * count // 2) * TILE
    payload_rows = matrix_rows + samples * (sketch_size // TILE)
    sketch, *shares = kernel_call(
        payload_kernel,
        "payload",
        [(sketch_size, width)] + [(payload_rows // leaves, TILE)] * leaves,
        place,
        omega_half,
        sketch_half,
        other_core(sketch_half),
        rhs,
        scratch=[(payload_rows, TILE)],
        flops=10**9,
    )

    *shares, late_sketch = lax.optimization_barrier((*shares, sketch_half))
    share = shares[0]
    for m in range(1, leaves):
        share = share + swapped(shares[m], "leaf", m)
    blocks = slab(late_sketch)
    near = jnp.concatenate(blocks[: leaves // 2], axis=1)
    far = jnp.concatenate(blocks[leaves // 2 :], axis=1)
    cut = near.shape[1]
    upward, here, downward = (mm(near, c[:cut]) + mm(far, c[cut:]) for c in columns)
    here = here + noise_variance * late_sketch
    shares = slab(axis_sum(share, "blk"))
    *shares, upward, downward, here = lax.optimization_barrier((*shares, upward, downward, here))
    other_shares = [other_core(s) for s in shares]
    from_below, from_above = sent(upward, downward)
    system, inverse, solved = kernel_call(
        inverse_kernel,
        "inverse_and_solve",
        [(sketch_size, sketch_size)] * 2 + [(samples, sketch_size)],
        place,
        *shares,
        *other_shares,
        scratch=[(payload_rows, TILE)] * 2,
        flops=30 * 10**9,
    )
    from_below, from_above, solved = lax.optimization_barrier((from_below, from_above, solved))
    own_image = here + from_below + from_above

    sum_rows = samples * (sketch_size // TILE) + 8
    sketches, direction, image, packet = kernel_call(
        image_kernel,
        "image",
        [(sketch_size, 2 * width)] + [(samples, width)] * 2 + [(sum_rows + samples * (width // TILE), TILE)],
        core,
        solved,
        sketch,
        own_image,
        other_core(own_image),
        rhs,
        image_rhs,
    )
    packets = slab(packet)
    slab_sum = (packets[0][:sum_rows] + packets[1][:sum_rows]) + (packets[2][:sum_rows] + packets[3][:sum_rows])
    upward, downward, gathered = sums([from_tiles(p[sum_rows:], samples) for p in packets])
    here = mm(gathered, columns[1]) + noise_variance * image
    if cycle == 4:
        even = own_slab % 2 == 0
        one, three = (
            swapped(jnp.concatenate([slab_sum, to_tiles(jnp.where(even, first, second))], axis=0), "blk", m)
            for m, first, second in ((1, upward, downward), (3, downward, upward))
        )
        two = swapped(slab_sum, "blk", 2)
        total = (slab_sum + one[:sum_rows]) + (two + three[:sum_rows])
        from_below, from_above = from_tiles(one[sum_rows:], samples), from_tiles(three[sum_rows:], samples)
    else:
        total = lax.psum(slab_sum, "blk")
        from_below, from_above = sent(upward, downward)
    image_twice = here + from_below + from_above
    solves = mm(inverse, sketches)
    solves = solves + rough_mm(inverse, sketches - mm(system, solves))
    moved = from_tiles(total[:-8], samples)
    dots = total[-8:]
    inner_first, curvature = dots[0, :samples, None], dots[1, :samples, None]
    step = inner_first / curvature

    taken = mm(moved, solves)
    precond = direction - step * ((image - taken[:, :width]) / noise_variance)
    image_precond = image - step * ((image_twice - taken[:, width:]) / noise_variance)
    residual = rhs - step * image
    dots = jnp.stack([dot_rows(residual, precond), dot_rows(precond, image_precond), dot_rows(precond, image)])
    dots = spread(jnp.pad(dots, ((0, 5), (0, TILE - samples)))).sum(axis=0)
    inner_second, curvature_precond, mixed = (dots[i, :samples, None] for i in range(3))
    beta = inner_second / inner_first
    step_second = inner_second / (curvature_precond + beta * (2.0 * mixed + beta * curvature))
    weights = step * direction + step_second * (precond + beta * direction)
    residual = residual - step_second * (image_precond + beta * image)
    return (weights, residual)


def solution(mesh):
    in_specs = (
        P(None, ("blk", "leaf")),
        P(("blk", "leaf"), None),
        P(None, ("blk", "leaf")),
        P(("blk", "leaf")),
        P("samp", ("blk", "leaf")),
    )
    out_specs = (P("samp", ("blk", "leaf")), P("samp", ("blk", "leaf")))
    return jax.shard_map(local, mesh=mesh, in_specs=in_specs, out_specs=out_specs, check_vma=False)
```

```python
import functools

import jax
import jax.numpy as jnp
from jax import lax
from jax.experimental import pallas as pl
from jax.experimental.pallas import tpu as pltpu
from jax.sharding import PartitionSpec as P

support_radius = 0.8
noise_variance = 1.0
sketch_shift = 1.0
HIGHEST = lax.Precision.HIGHEST
POINT_AXES = ("blk", "leaf")
TILE = 128
BASE, REFINES = 128, 1


def mm(left, right):
    return jnp.dot(left, right, precision=HIGHEST, preferred_element_type=jnp.float32)


def rough_mm(left, right):
    return jnp.dot(left, right, preferred_element_type=jnp.float32)


def mm_t(left, right):
    return lax.dot_general(
        left, right, (((1,), (1,)), ((), ())), precision=HIGHEST, preferred_element_type=jnp.float32
    )


def tree_sum(terms):
    terms = list(terms)
    while len(terms) > 1:
        terms = [
            terms[i] + terms[i + 1] if i + 1 < len(terms) else terms[i] for i in range(0, len(terms), 2)
        ]
    return terms[0]


def reciprocal(value):
    guess = pl.reciprocal(value, approx=True)
    for _ in range(REFINES):
        guess = guess * (2.0 - value * guess)
    return guess


def pair_inverse(a, b, c):
    inv = reciprocal(a * c - b * b)
    return c * inv, -(b * inv), a * inv


def quad_solve(entries, rows):
    a0, a1, a2 = pair_inverse(entries[(0, 0)], entries[(0, 1)], entries[(1, 1)])
    cross = [[entries[(a, 2 + b)] for b in (0, 1)] for a in (0, 1)]
    lift = [
        [a0 * cross[0][b] + a1 * cross[1][b] for b in (0, 1)],
        [a1 * cross[0][b] + a2 * cross[1][b] for b in (0, 1)],
    ]
    s0, s1, s2 = pair_inverse(
        *(
            entries[(2 + a, 2 + b)] - (cross[0][a] * lift[0][b] + cross[1][a] * lift[1][b])
            for a, b in ((0, 0), (0, 1), (1, 1))
        )
    )
    solved = []
    for r0, r1, r2, r3 in zip(*rows):
        u0 = r2 - (lift[0][0] * r0 + lift[1][0] * r1)
        u1 = r3 - (lift[0][1] * r0 + lift[1][1] * r1)
        x2, x3 = s0 * u0 + s1 * u1, s1 * u0 + s2 * u1
        x0 = (a0 * r0 + a1 * r1) - (lift[0][0] * x2 + lift[0][1] * x3)
        x1 = (a1 * r0 + a2 * r1) - (lift[1][0] * x2 + lift[1][1] * x3)
        solved.append((x0, x1, x2, x3))
    return [list(row) for row in zip(*solved)]


def pivot_inverse(matrix):
    size = matrix.shape[0]
    lane = lax.broadcasted_iota(jnp.int32, (8, size), 1)
    sub = lax.broadcasted_iota(jnp.int32, (8, size), 0)
    parts = [matrix[8 * i : 8 * i + 8, :] for i in range(size // 8)]
    four = range(4)

    def row(values, r):
        return jnp.broadcast_to(values[r : r + 1, :], (8, size))

    def column(values, c):
        return jnp.broadcast_to(values[:, c : c + 1], (8, size))

    for home in range(size // 8):
        k = 8 * home
        here = (lane >= k) & (lane < k + 8)
        pivots = [column(parts[home], k + b) for b in range(8)]
        entries = {(a, b): row(pivots[b], a) for a in range(8) for b in range(a, 8)}
        rows = [
            jnp.where(here, jnp.where(lane == k + a, 1.0, 0.0), row(parts[home], a)) for a in range(8)
        ]
        cross = [[entries[(a, 4 + b)] for b in four] for a in four]
        first = quad_solve(entries, [cross[a] + [rows[a]] for a in four])
        lift = [first[a][:4] for a in four]
        schur = {
            (a, b): entries[(4 + a, 4 + b)] - tree_sum(cross[c][a] * lift[c][b] for c in four)
            for a in four
            for b in range(a, 4)
        }
        last = [[rows[4 + a] - tree_sum(lift[c][a] * rows[c] for c in four)] for a in four]
        last = [values[0] for values in quad_solve(schur, last)]
        scaled = [first[a][4] - tree_sum(lift[a][c] * last[c] for c in four) for a in four] + last
        updated = []
        for i, part in enumerate(parts):
            if i == home:
                fresh = scaled[7]
                for a in range(7):
                    fresh = jnp.where(sub == a, scaled[a], fresh)
                updated.append(fresh)
            else:
                taken = tree_sum(column(part, k + a) * scaled[a] for a in range(8))
                updated.append(jnp.where(here, 0.0, part) - taken)
        parts = updated
    return jnp.concatenate(parts, axis=0)


def block_inverse(matrix):
    size = matrix.shape[0]
    if size <= BASE:
        return pivot_inverse(matrix)
    half = size // 2
    corner, side = matrix[:half, :half], matrix[:half, half:]
    first = block_inverse(corner)
    lift = mm(first, side)
    last = block_inverse(matrix[half:, half:] - mm(side.T, lift))
    mixed = mm(lift, last)
    top = jnp.concatenate([first + mm(mixed, lift.T), -mixed], axis=1)
    return jnp.concatenate([top, jnp.concatenate([-mixed.T, last], axis=1)], axis=0)


def assemble(core_ref, own_ref, other_ref, system_ref):
    half = system_ref.shape[0] // 2
    count = half // TILE

    def put(row, column, block):
        system_ref[row : row + TILE, column : column + TILE] = block

    flag = jnp.zeros((TILE, TILE), jnp.int32) + core_ref[0] == 0

    def tile(at, share):
        own, other = own_ref[at : at + TILE, :], other_ref[at : at + TILE, :]
        return jnp.where(flag, own, other) if share == 0 else jnp.where(flag, other, own)

    for share, corner in ((0, 0), (1, half)):
        at = 0
        for i in range(count):
            for j in range(i, count):
                block = tile(at, share)
                at += TILE
                if i == j:
                    put(corner + i * TILE, corner + i * TILE, 0.5 * (block + block.T))
                else:
                    put(corner + i * TILE, corner + j * TILE, block)
                    put(corner + j * TILE, corner + i * TILE, block.T)
    share_columns = count // 2
    for share in (0, 1):
        at = count * (count + 1) // 2 * TILE
        for j in range(share * share_columns, (share + 1) * share_columns):
            for i in range(count):
                block = tile(at, share)
                at += TILE
                put(i * TILE, half + j * TILE, block)
                put(half + j * TILE, i * TILE, block.T)


def eliminate(inverse_ref, begin, end):
    size = inverse_ref.shape[0]
    count = size // TILE
    row_id = lax.broadcasted_iota(jnp.int32, (TILE, TILE), 0)
    column_id = lax.broadcasted_iota(jnp.int32, (TILE, TILE), 1)

    def span(index):
        return pl.ds(pl.multiple_of(index * TILE, TILE), TILE)

    def step(k, carry):
        own = span(k)
        block = block_inverse(inverse_ref[own, own])
        inverse_ref[own, own] = jnp.where(row_id == column_id, 1.0, 0.0)
        scaled = mm(block, inverse_ref[own, :])
        inverse_ref[own, :] = scaled
        for ahead in range(1, count):
            other = span(lax.rem(k + ahead, count))
            column = inverse_ref[other, own]
            inverse_ref[other, own] = jnp.zeros((TILE, TILE), jnp.float32)
            inverse_ref[other, :] = inverse_ref[other, :] - mm(column, scaled)
        return carry

    lax.fori_loop(begin, end, step, 0)


def inverse_kernel(place_ref, *refs):
    shares, (system_ref, inverse_ref, solved_ref, own_ref, other_ref) = refs[:-5], refs[-5:]
    leaves = len(shares) // 2
    rows = shares[0].shape[0]
    for m in range(leaves):
        at = pl.ds(pl.multiple_of((place_ref[1] ^ m) * rows, rows), rows)
        own_ref[at, :] = shares[m][...]
        other_ref[at, :] = shares[leaves + m][...]
    assemble(place_ref, own_ref, other_ref, system_ref)
    inverse_ref[...] = system_ref[...]
    count = system_ref.shape[0] // TILE
    eliminate(inverse_ref, 0, count)
    samples = solved_ref.shape[0]
    begin = own_ref.shape[0] - count * samples
    rhs = jnp.concatenate(
        [own_ref[begin + i * samples : begin + (i + 1) * samples, :] for i in range(count)], axis=1
    )
    guess = mm(rhs, inverse_ref[...])
    solved_ref[...] = guess + rough_mm(rhs - mm(guess, system_ref[...]), inverse_ref[...])


def image_kernel(
    core_ref, solved_ref, sketch_ref, own_ref, other_ref, rhs_ref, image_rhs_ref,
    sketches_ref, direction_ref, image_ref, packet_ref,
):
    half, width = own_ref.shape
    core = core_ref[0]
    sketches_ref[:, :width] = sketch_ref[...]
    sketches_ref[pl.ds(pl.multiple_of(core * half, half), half), width:] = own_ref[...]
    sketches_ref[pl.ds(pl.multiple_of((1 - core) * half, half), half), width:] = other_ref[...]
    taken = mm(solved_ref[...], sketches_ref[...])
    rhs = rhs_ref[...]
    direction = (rhs - taken[:, :width]) / noise_variance
    image = (image_rhs_ref[...] - taken[:, width:]) / noise_variance
    direction_ref[...] = direction
    image_ref[...] = image
    moved = mm_t(image, sketch_ref[...])
    samples = rhs.shape[0]
    count = moved.shape[1] // TILE
    for i in range(count):
        packet_ref[i * samples : (i + 1) * samples, :] = moved[:, i * TILE : (i + 1) * TILE]
    at = count * samples
    ones = jnp.ones((8, width), jnp.float32)
    packet_ref[at : at + 8, :] = jnp.zeros((8, TILE), jnp.float32)
    packet_ref[at : at + 1, :samples] = mm_t(ones, rhs * direction)[0:1, :]
    packet_ref[at + 1 : at + 2, :samples] = mm_t(ones, direction * image)[0:1, :]
    at += 8
    for i in range(width // TILE):
        packet_ref[at : at + samples, :] = image[:, i * TILE : (i + 1) * TILE]
        at += samples


def prepare_kernel(
    core_ref, points_ref, neighbors_ref, omega_ref, observed_ref, prior_ref, first_ref, second_ref, meta_ref, own_ref, rhs_ref,
    points_vmem, neighbors_vmem, observed_vmem, prior_vmem, sems,
):
    split = second_ref.shape[0]
    samples = prior_vmem.shape[0]
    begin = pl.multiple_of(core_ref[0] * (2 * split), 2 * split)
    copies = [
        pltpu.make_async_copy(source, target, sems.at[i])
        for i, (source, target) in enumerate(
            (
                (omega_ref.at[pl.ds(begin, split), :], first_ref.at[0:split, :]),
                (omega_ref.at[pl.ds(begin + split, split), :], second_ref),
                (points_ref, points_vmem),
                (neighbors_ref, neighbors_vmem),
                (observed_ref, observed_vmem),
                (prior_ref, prior_vmem),
            )
        )
    ]
    for copy in copies:
        copy.start()
    meta_ref[...] = jnp.full(meta_ref.shape, -1.0, jnp.float32)
    for copy in copies:
        copy.wait()
    own_ref[0:split, :] = first_ref[0:split, :]
    own_ref[split:, :] = second_ref[...]
    rhs_ref[...] = observed_vmem[...] - prior_vmem[...]
    first_ref[split : split + samples, :] = rhs_ref[...]
    meta_ref[0:3, :] = points_vmem[...]
    meta_ref[3:4, : neighbors_vmem.shape[1]] = neighbors_vmem[...].astype(jnp.float32)
    first_ref[split + samples :, :] = meta_ref[...]


def prepare(core, points, neighbors, omega, observed, prior, split):
    width = omega.shape[1]
    samples = prior.shape[0]
    vmem = pl.BlockSpec(memory_space=pltpu.VMEM)
    hbm = pl.BlockSpec(memory_space=pl.ANY)
    shapes = [(split + samples + 8, width), (split, width), (8, width), (2 * split, width), (samples, width)]
    return pl.pallas_call(
        prepare_kernel,
        out_shape=tuple(jax.ShapeDtypeStruct(shape, jnp.float32) for shape in shapes),
        in_specs=[pl.BlockSpec(memory_space=pltpu.SMEM)] + [hbm] * 5,
        out_specs=(vmem,) * 5,
        scratch_shapes=[
            pltpu.VMEM(points.shape, jnp.float32),
            pltpu.VMEM(neighbors.shape, jnp.int32),
            pltpu.VMEM(observed.shape, jnp.float32),
            pltpu.VMEM(prior.shape, jnp.float32),
            pltpu.SemaphoreType.DMA((6,)),
        ],
        name="prepare",
        cost_estimate=pl.CostEstimate(flops=10**6, bytes_accessed=2**19, transcendentals=0),
    )(core, points, neighbors, omega, observed, prior)


def targets_kernel(ids_ref, *refs):
    count = len(refs) // 3
    width = refs[0].shape[1]
    for meta_ref, rows_ref, weight_ref in zip(refs[:count], refs[count : 2 * count], refs[2 * count :]):
        rows_ref[...] = meta_ref[0:3, :]
        listed = meta_ref[3:4, :]
        for m in range(weight_ref.shape[1] // width):
            same = listed == jnp.zeros((1, width), jnp.float32) + ids_ref[m].astype(jnp.float32)
            found = jnp.sum(jnp.where(same, 1.0, 0.0), axis=1, keepdims=True)
            weight_ref[:, m * width : (m + 1) * width] = jnp.broadcast_to(found, (1, width))


def payload_kernel(place_ref, omega_ref, own_ref, other_ref, rhs_ref, sketch_ref, *refs):
    half, width = own_ref.shape
    split = half // 2
    core, leaf = place_ref[0], place_ref[1]
    shares, payload_ref = refs[:-1], refs[-1]
    begin = pl.multiple_of(core * half, half)
    sketch_ref[pl.ds(begin, half), :] = own_ref[...]
    sketch_ref[pl.ds(pl.multiple_of((1 - core) * half, half), half), :] = other_ref[...]
    own, other = own_ref[...], other_ref[...]
    lifted = noise_variance * omega_ref[...] + own
    count = half // TILE
    at = 0
    for i in range(count):
        product = mm_t(lifted[i * TILE : (i + 1) * TILE], own[i * TILE :])
        for j in range(count - i):
            payload_ref[at : at + TILE, :] = product[:, j * TILE : (j + 1) * TILE]
            at += TILE
    on_first = jnp.zeros((half, width), jnp.int32) + core == 0
    left = jnp.where(on_first, lifted, other)
    right = jnp.where(on_first[:split], other[:split], lifted[split:])
    product = mm_t(left, right)
    for j in range(split // TILE):
        payload_ref[at : at + half, :] = product[:, j * TILE : (j + 1) * TILE]
        at += half
    product = mm_t(rhs_ref[...], sketch_ref[...])
    samples = rhs_ref.shape[0]
    for j in range(2 * count):
        payload_ref[at : at + samples, :] = product[:, j * TILE : (j + 1) * TILE]
        at += samples
    rows = shares[0].shape[0]
    for m, share in enumerate(shares):
        share[...] = payload_ref[pl.ds(pl.multiple_of((leaf ^ m) * rows, rows), rows), :]


def kernel_call(kernel, name, outputs, *operands, scratch=(), flops=10**8):
    vmem = pl.BlockSpec(memory_space=pltpu.VMEM)
    smem = pl.BlockSpec(memory_space=pltpu.SMEM)
    return pl.pallas_call(
        kernel,
        out_shape=tuple(jax.ShapeDtypeStruct(shape, jnp.float32) for shape in outputs),
        in_specs=[smem if o.ndim == 1 else vmem for o in operands],
        out_specs=(vmem,) * len(outputs),
        scratch_shapes=[pltpu.VMEM(shape, jnp.float32) for shape in scratch],
        name=name,
        compiler_params=pltpu.CompilerParams(vmem_limit_bytes=12 * 2**20),
        cost_estimate=pl.CostEstimate(flops=flops, bytes_accessed=2**20, transcendentals=0),
    )(*operands)


def shifted(values, axis, distance):
    size = lax.axis_size(axis)
    return lax.ppermute(values, axis, [(i, (i + distance) % size) for i in range(size)])


def swapped(values, axis, mask):
    size = lax.axis_size(axis)
    return lax.ppermute(values, axis, [(i, i ^ mask) for i in range(size)])


def slab(values):
    return [values] + [swapped(values, "leaf", m) for m in range(1, lax.axis_size("leaf"))]


def group_size():
    return lax.axis_size(POINT_AXES)


def exchange(values):
    return lax.all_to_all(values, POINT_AXES, 0, 0, tiled=True)


def axis_sum(values, axis):
    if lax.axis_size(axis) != 4:
        return lax.psum(values, axis)
    one, two, three = (swapped(values, axis, m) for m in (1, 2, 3))
    return (values + one) + (two + three)


def spread(values):
    count = group_size()
    sent = jnp.broadcast_to(values[None], (count,) + values.shape).reshape(-1, values.shape[1])
    return exchange(sent).reshape((count,) + values.shape)


def to_tiles(values):
    return jnp.concatenate([values[:, c : c + TILE] for c in range(0, values.shape[1], TILE)], axis=0)


def from_tiles(tiles, rows):
    return jnp.concatenate([tiles[r : r + rows] for r in range(0, tiles.shape[0], rows)], axis=1)


def dot_rows(left, right):
    return jnp.sum(left * right, axis=1)


def local(points, neighbors, omega, observed, prior_draws):
    cycle = lax.axis_size("blk")
    leaves = lax.axis_size("leaf")
    cores = lax.axis_size("samp")
    own_slab, own_leaf, own_core = (lax.axis_index(a) for a in ("blk", "leaf", "samp"))
    sketch_size, width = omega.shape
    half = sketch_size // cores
    samples = prior_draws.shape[0]
    period = 2.0 * cycle

    core = own_core.astype(jnp.int32).reshape(1)
    place = jnp.stack([own_core, own_leaf]).astype(jnp.int32)
    split = half // 2
    first_block, second_block, meta, omega_half, rhs = prepare(
        core, points, neighbors, omega, observed[None, :], prior_draws, split
    )

    def other_core(values):
        return swapped(values, "samp", 1)

    def sent(upward, downward):
        return shifted(upward, "blk", 1), shifted(downward, "blk", -1)

    first_blocks, second_blocks = slab(first_block), slab(second_block)
    route = [
        (b * cores + c, (b + (1 if c == 0 else -1)) % cycle * cores + c) for b in range(cycle) for c in range(cores)
    ]
    arrived = lax.ppermute(meta, ("blk", "samp"), route)
    swapped_meta = other_core(arrived)
    above = jnp.where(own_core == 0, swapped_meta, arrived)
    below = jnp.where(own_core == 0, arrived, swapped_meta)
    begin = split + samples
    sources = jnp.concatenate([b[begin : begin + 3] for b in first_blocks], axis=1)
    source_ids = (own_slab * leaves + jnp.stack([own_leaf ^ m for m in range(leaves)])).astype(jnp.int32)
    tables = kernel_call(
        targets_kernel,
        "targets",
        [(3, width)] * 3 + [(1, leaves * width)] * 3,
        source_ids,
        above,
        meta,
        below,
    )
    targets, weights = tables[:3], tables[3:]

    def kernel_columns(index):
        offset = sources[:, :, None] - targets[index][:, None, :]
        along = offset[0]
        along = jnp.where(along >= 0.5 * period, along - period, along)
        along = jnp.where(along < -0.5 * period, along + period, along)
        squared = along * along + offset[1] * offset[1] + offset[2] * offset[2]
        radius = jnp.sqrt(squared) / support_radius
        remain = jnp.maximum(1.0 - radius, 0.0)
        squared_remain = remain * remain
        values = squared_remain * squared_remain * (4.0 * radius + 1.0)
        return values * weights[index].reshape(-1, 1)

    columns = [kernel_columns(i) for i in range(3)]

    def sums(values):
        gathered = jnp.concatenate(values, axis=1)
        return mm(gathered, columns[0]), mm(gathered, columns[2]), gathered

    upward, downward, gathered = sums(first_blocks)
    _, _, *second_blocks = lax.optimization_barrier((upward, downward, *second_blocks))
    from_below, from_above = sent(upward, downward)
    applied = mm(gathered, columns[1]) + from_below + from_above
    upward, downward, gathered = sums(second_blocks)
    from_below, from_above = sent(upward, downward)
    applied_second = mm(gathered, columns[1]) + from_below + from_above
    sketch_half = jnp.concatenate([applied[:split], applied_second], axis=0) + sketch_shift * omega_half
    image_rhs = applied[split:begin] + noise_variance * rhs

    count = half // TILE
    matrix_rows = (count * (count + 1) // 2 + count * count // 2) * TILE
    payload_rows = matrix_rows + samples * (sketch_size // TILE)
    sketch, *shares = kernel_call(
        payload_kernel,
        "payload",
        [(sketch_size, width)] + [(payload_rows // leaves, TILE)] * leaves,
        place,
        omega_half,
        sketch_half,
        other_core(sketch_half),
        rhs,
        scratch=[(payload_rows, TILE)],
        flops=10**9,
    )

    *shares, late_sketch = lax.optimization_barrier((*shares, sketch_half))
    share = shares[0]
    for m in range(1, leaves):
        share = share + swapped(shares[m], "leaf", m)
    blocks = slab(late_sketch)
    near = jnp.concatenate(blocks[: leaves // 2], axis=1)
    far = jnp.concatenate(blocks[leaves // 2 :], axis=1)
    cut = near.shape[1]
    upward, here, downward = (mm(near, c[:cut]) + mm(far, c[cut:]) for c in columns)
    here = here + noise_variance * late_sketch
    shares = slab(axis_sum(share, "blk"))
    *shares, upward, downward, here = lax.optimization_barrier((*shares, upward, downward, here))
    other_shares = [other_core(s) for s in shares]
    from_below, from_above = sent(upward, downward)
    system, inverse, solved = kernel_call(
        inverse_kernel,
        "inverse_and_solve",
        [(sketch_size, sketch_size)] * 2 + [(samples, sketch_size)],
        place,
        *shares,
        *other_shares,
        scratch=[(payload_rows, TILE)] * 2,
        flops=30 * 10**9,
    )
    from_below, from_above, solved = lax.optimization_barrier((from_below, from_above, solved))
    own_image = here + from_below + from_above

    sum_rows = samples * (sketch_size // TILE) + 8
    sketches, direction, image, packet = kernel_call(
        image_kernel,
        "image",
        [(sketch_size, 2 * width)] + [(samples, width)] * 2 + [(sum_rows + samples * (width // TILE), TILE)],
        core,
        solved,
        sketch,
        own_image,
        other_core(own_image),
        rhs,
        image_rhs,
    )
    packets = slab(packet)
    slab_sum = (packets[0][:sum_rows] + packets[1][:sum_rows]) + (packets[2][:sum_rows] + packets[3][:sum_rows])
    upward, downward, gathered = sums([from_tiles(p[sum_rows:], samples) for p in packets])
    here = mm(gathered, columns[1]) + noise_variance * image
    if cycle == 4:
        even = own_slab % 2 == 0
        one, three = (
            swapped(jnp.concatenate([slab_sum, to_tiles(jnp.where(even, first, second))], axis=0), "blk", m)
            for m, first, second in ((1, upward, downward), (3, downward, upward))
        )
        two = swapped(slab_sum, "blk", 2)
        total = (slab_sum + one[:sum_rows]) + (two + three[:sum_rows])
        from_below, from_above = from_tiles(one[sum_rows:], samples), from_tiles(three[sum_rows:], samples)
    else:
        total = lax.psum(slab_sum, "blk")
        from_below, from_above = sent(upward, downward)
    image_twice = here + from_below + from_above
    solves = mm(inverse, sketches)
    solves = solves + rough_mm(inverse, sketches - mm(system, solves))
    moved = from_tiles(total[:-8], samples)
    dots = total[-8:]
    inner_first, curvature = dots[0, :samples, None], dots[1, :samples, None]
    step = inner_first / curvature

    taken = mm(moved, solves)
    precond = direction - step * ((image - taken[:, :width]) / noise_variance)
    image_precond = image - step * ((image_twice - taken[:, width:]) / noise_variance)
    residual = rhs - step * image
    dots = jnp.stack([dot_rows(residual, precond), dot_rows(precond, image_precond), dot_rows(precond, image)])
    dots = spread(jnp.pad(dots, ((0, 5), (0, TILE - samples)))).sum(axis=0)
    inner_second, curvature_precond, mixed = (dots[i, :samples, None] for i in range(3))
    beta = inner_second / inner_first
    step_second = inner_second / (curvature_precond + beta * (2.0 * mixed + beta * curvature))
    weights = step * direction + step_second * (precond + beta * direction)
    residual = residual - step_second * (image_precond + beta * image)
    return (weights, residual)


def solution(mesh):
    in_specs = (
        P(None, ("blk", "leaf")),
        P(("blk", "leaf"), None),
        P(None, ("blk", "leaf")),
        P(("blk", "leaf")),
        P("samp", ("blk", "leaf")),
    )
    out_specs = (P("samp", ("blk", "leaf")), P("samp", ("blk", "leaf")))
    return jax.shard_map(local, mesh=mesh, in_specs=in_specs, out_specs=out_specs, check_vma=False)
```

```python
import functools

import jax
import jax.numpy as jnp
from jax import lax
from jax.experimental import pallas as pl
from jax.experimental.pallas import tpu as pltpu
from jax.sharding import PartitionSpec as P

support_radius = 0.8
noise_variance = 1.0
sketch_shift = 1.0
HIGHEST = lax.Precision.HIGHEST
POINT_AXES = ("blk", "leaf")
TILE = 128
BASE, REFINES = 128, 1


def mm(left, right):
    return jnp.dot(left, right, precision=HIGHEST, preferred_element_type=jnp.float32)


def rough_mm(left, right):
    return jnp.dot(left, right, preferred_element_type=jnp.float32)


def mm_t(left, right):
    return lax.dot_general(
        left, right, (((1,), (1,)), ((), ())), precision=HIGHEST, preferred_element_type=jnp.float32
    )


def tree_sum(terms):
    terms = list(terms)
    while len(terms) > 1:
        terms = [
            terms[i] + terms[i + 1] if i + 1 < len(terms) else terms[i] for i in range(0, len(terms), 2)
        ]
    return terms[0]


def reciprocal(value):
    guess = pl.reciprocal(value, approx=True)
    for _ in range(REFINES):
        guess = guess * (2.0 - value * guess)
    return guess


def pair_inverse(a, b, c):
    inv = reciprocal(a * c - b * b)
    return c * inv, -(b * inv), a * inv


def quad_solve(entries, rows):
    a0, a1, a2 = pair_inverse(entries[(0, 0)], entries[(0, 1)], entries[(1, 1)])
    cross = [[entries[(a, 2 + b)] for b in (0, 1)] for a in (0, 1)]
    lift = [
        [a0 * cross[0][b] + a1 * cross[1][b] for b in (0, 1)],
        [a1 * cross[0][b] + a2 * cross[1][b] for b in (0, 1)],
    ]
    s0, s1, s2 = pair_inverse(
        *(
            entries[(2 + a, 2 + b)] - (cross[0][a] * lift[0][b] + cross[1][a] * lift[1][b])
            for a, b in ((0, 0), (0, 1), (1, 1))
        )
    )
    solved = []
    for r0, r1, r2, r3 in zip(*rows):
        u0 = r2 - (lift[0][0] * r0 + lift[1][0] * r1)
        u1 = r3 - (lift[0][1] * r0 + lift[1][1] * r1)
        x2, x3 = s0 * u0 + s1 * u1, s1 * u0 + s2 * u1
        x0 = (a0 * r0 + a1 * r1) - (lift[0][0] * x2 + lift[0][1] * x3)
        x1 = (a1 * r0 + a2 * r1) - (lift[1][0] * x2 + lift[1][1] * x3)
        solved.append((x0, x1, x2, x3))
    return [list(row) for row in zip(*solved)]


def pivot_inverse(matrix):
    size = matrix.shape[0]
    lane = lax.broadcasted_iota(jnp.int32, (8, size), 1)
    sub = lax.broadcasted_iota(jnp.int32, (8, size), 0)
    parts = [matrix[8 * i : 8 * i + 8, :] for i in range(size // 8)]
    four = range(4)

    def row(values, r):
        return jnp.broadcast_to(values[r : r + 1, :], (8, size))

    def column(values, c):
        return jnp.broadcast_to(values[:, c : c + 1], (8, size))

    for home in range(size // 8):
        k = 8 * home
        here = (lane >= k) & (lane < k + 8)
        pivots = [column(parts[home], k + b) for b in range(8)]
        entries = {(a, b): row(pivots[b], a) for a in range(8) for b in range(a, 8)}
        rows = [
            jnp.where(here, jnp.where(lane == k + a, 1.0, 0.0), row(parts[home], a)) for a in range(8)
        ]
        cross = [[entries[(a, 4 + b)] for b in four] for a in four]
        first = quad_solve(entries, [cross[a] + [rows[a]] for a in four])
        lift = [first[a][:4] for a in four]
        schur = {
            (a, b): entries[(4 + a, 4 + b)] - tree_sum(cross[c][a] * lift[c][b] for c in four)
            for a in four
            for b in range(a, 4)
        }
        last = [[rows[4 + a] - tree_sum(lift[c][a] * rows[c] for c in four)] for a in four]
        last = [values[0] for values in quad_solve(schur, last)]
        scaled = [first[a][4] - tree_sum(lift[a][c] * last[c] for c in four) for a in four] + last
        updated = []
        for i, part in enumerate(parts):
            if i == home:
                fresh = scaled[7]
                for a in range(7):
                    fresh = jnp.where(sub == a, scaled[a], fresh)
                updated.append(fresh)
            else:
                taken = tree_sum(column(part, k + a) * scaled[a] for a in range(8))
                updated.append(jnp.where(here, 0.0, part) - taken)
        parts = updated
    return jnp.concatenate(parts, axis=0)


def block_inverse(matrix):
    size = matrix.shape[0]
    if size <= BASE:
        return pivot_inverse(matrix)
    half = size // 2
    corner, side = matrix[:half, :half], matrix[:half, half:]
    first = block_inverse(corner)
    lift = mm(first, side)
    last = block_inverse(matrix[half:, half:] - mm(side.T, lift))
    mixed = mm(lift, last)
    top = jnp.concatenate([first + mm(mixed, lift.T), -mixed], axis=1)
    return jnp.concatenate([top, jnp.concatenate([-mixed.T, last], axis=1)], axis=0)


def assemble(core_ref, own_ref, other_ref, system_ref):
    half = system_ref.shape[0] // 2
    count = half // TILE

    def put(row, column, block):
        system_ref[row : row + TILE, column : column + TILE] = block

    flag = jnp.zeros((TILE, TILE), jnp.int32) + core_ref[0] == 0

    def tile(at, share):
        own, other = own_ref[at : at + TILE, :], other_ref[at : at + TILE, :]
        return jnp.where(flag, own, other) if share == 0 else jnp.where(flag, other, own)

    for share, corner in ((0, 0), (1, half)):
        at = 0
        for i in range(count):
            for j in range(i, count):
                block = tile(at, share)
                at += TILE
                if i == j:
                    put(corner + i * TILE, corner + i * TILE, 0.5 * (block + block.T))
                else:
                    put(corner + i * TILE, corner + j * TILE, block)
                    put(corner + j * TILE, corner + i * TILE, block.T)
    share_columns = count // 2
    for share in (0, 1):
        at = count * (count + 1) // 2 * TILE
        for j in range(share * share_columns, (share + 1) * share_columns):
            for i in range(count):
                block = tile(at, share)
                at += TILE
                put(i * TILE, half + j * TILE, block)
                put(half + j * TILE, i * TILE, block.T)


def eliminate(inverse_ref, begin, end):
    size = inverse_ref.shape[0]
    count = size // TILE
    row_id = lax.broadcasted_iota(jnp.int32, (TILE, TILE), 0)
    column_id = lax.broadcasted_iota(jnp.int32, (TILE, TILE), 1)

    def span(index):
        return pl.ds(pl.multiple_of(index * TILE, TILE), TILE)

    def step(k, carry):
        own = span(k)
        block = block_inverse(inverse_ref[own, own])
        inverse_ref[own, own] = jnp.where(row_id == column_id, 1.0, 0.0)
        scaled = mm(block, inverse_ref[own, :])
        inverse_ref[own, :] = scaled
        for ahead in range(1, count):
            other = span(lax.rem(k + ahead, count))
            column = inverse_ref[other, own]
            inverse_ref[other, own] = jnp.zeros((TILE, TILE), jnp.float32)
            inverse_ref[other, :] = inverse_ref[other, :] - mm(column, scaled)
        return carry

    lax.fori_loop(begin, end, step, 0)


def inverse_kernel(place_ref, *refs):
    shares, (system_ref, inverse_ref, solved_ref, own_ref, other_ref) = refs[:-5], refs[-5:]
    leaves = len(shares) // 2
    rows = shares[0].shape[0]
    for m in range(leaves):
        at = pl.ds(pl.multiple_of((place_ref[1] ^ m) * rows, rows), rows)
        own_ref[at, :] = shares[m][...]
        other_ref[at, :] = shares[leaves + m][...]
    assemble(place_ref, own_ref, other_ref, system_ref)
    inverse_ref[...] = system_ref[...]
    count = system_ref.shape[0] // TILE
    eliminate(inverse_ref, 0, count)
    samples = solved_ref.shape[0]
    begin = own_ref.shape[0] - count * samples
    rhs = jnp.concatenate(
        [own_ref[begin + i * samples : begin + (i + 1) * samples, :] for i in range(count)], axis=1
    )
    guess = mm(rhs, inverse_ref[...])
    solved_ref[...] = guess + rough_mm(rhs - mm(guess, system_ref[...]), inverse_ref[...])


def image_kernel(
    core_ref, solved_ref, sketch_ref, own_ref, other_ref, rhs_ref, image_rhs_ref,
    sketches_ref, direction_ref, image_ref, packet_ref,
):
    half, width = own_ref.shape
    core = core_ref[0]
    sketches_ref[:, :width] = sketch_ref[...]
    sketches_ref[pl.ds(pl.multiple_of(core * half, half), half), width:] = own_ref[...]
    sketches_ref[pl.ds(pl.multiple_of((1 - core) * half, half), half), width:] = other_ref[...]
    taken = mm(solved_ref[...], sketches_ref[...])
    rhs = rhs_ref[...]
    direction = (rhs - taken[:, :width]) / noise_variance
    image = (image_rhs_ref[...] - taken[:, width:]) / noise_variance
    direction_ref[...] = direction
    image_ref[...] = image
    moved = mm_t(image, sketch_ref[...])
    samples = rhs.shape[0]
    count = moved.shape[1] // TILE
    for i in range(count):
        packet_ref[i * samples : (i + 1) * samples, :] = moved[:, i * TILE : (i + 1) * TILE]
    at = count * samples
    ones = jnp.ones((8, width), jnp.float32)
    packet_ref[at : at + 8, :] = jnp.zeros((8, TILE), jnp.float32)
    packet_ref[at : at + 1, :samples] = mm_t(ones, rhs * direction)[0:1, :]
    packet_ref[at + 1 : at + 2, :samples] = mm_t(ones, direction * image)[0:1, :]
    at += 8
    for i in range(width // TILE):
        packet_ref[at : at + samples, :] = image[:, i * TILE : (i + 1) * TILE]
        at += samples


def prepare_kernel(
    core_ref, points_ref, neighbors_ref, omega_ref, observed_ref, prior_ref, first_ref, second_ref, meta_ref, own_ref, rhs_ref,
    points_vmem, neighbors_vmem, observed_vmem, prior_vmem, sems,
):
    split = second_ref.shape[0]
    samples = prior_vmem.shape[0]
    begin = pl.multiple_of(core_ref[0] * (2 * split), 2 * split)
    copies = [
        pltpu.make_async_copy(source, target, sems.at[i])
        for i, (source, target) in enumerate(
            (
                (omega_ref.at[pl.ds(begin, split), :], first_ref.at[0:split, :]),
                (omega_ref.at[pl.ds(begin + split, split), :], second_ref),
                (points_ref, points_vmem),
                (neighbors_ref, neighbors_vmem),
                (observed_ref, observed_vmem),
                (prior_ref, prior_vmem),
            )
        )
    ]
    for copy in copies:
        copy.start()
    meta_ref[...] = jnp.full(meta_ref.shape, -1.0, jnp.float32)
    for copy in copies:
        copy.wait()
    own_ref[0:split, :] = first_ref[0:split, :]
    own_ref[split:, :] = second_ref[...]
    rhs_ref[...] = observed_vmem[...] - prior_vmem[...]
    first_ref[split : split + samples, :] = rhs_ref[...]
    meta_ref[0:3, :] = points_vmem[...]
    meta_ref[3:4, : neighbors_vmem.shape[1]] = neighbors_vmem[...].astype(jnp.float32)
    first_ref[split + samples :, :] = meta_ref[...]


def prepare(core, points, neighbors, omega, observed, prior, split):
    width = omega.shape[1]
    samples = prior.shape[0]
    vmem = pl.BlockSpec(memory_space=pltpu.VMEM)
    hbm = pl.BlockSpec(memory_space=pl.ANY)
    shapes = [(split + samples + 8, width), (split, width), (8, width), (2 * split, width), (samples, width)]
    return pl.pallas_call(
        prepare_kernel,
        out_shape=tuple(jax.ShapeDtypeStruct(shape, jnp.float32) for shape in shapes),
        in_specs=[pl.BlockSpec(memory_space=pltpu.SMEM)] + [hbm] * 5,
        out_specs=(vmem,) * 5,
        scratch_shapes=[
            pltpu.VMEM(points.shape, jnp.float32),
            pltpu.VMEM(neighbors.shape, jnp.int32),
            pltpu.VMEM(observed.shape, jnp.float32),
            pltpu.VMEM(prior.shape, jnp.float32),
            pltpu.SemaphoreType.DMA((6,)),
        ],
        name="prepare",
        cost_estimate=pl.CostEstimate(flops=10**6, bytes_accessed=2**19, transcendentals=0),
    )(core, points, neighbors, omega, observed, prior)


def targets_kernel(ids_ref, *refs):
    count = len(refs) // 3
    width = refs[0].shape[1]
    for meta_ref, rows_ref, weight_ref in zip(refs[:count], refs[count : 2 * count], refs[2 * count :]):
        rows_ref[...] = meta_ref[0:3, :]
        listed = meta_ref[3:4, :]
        for m in range(weight_ref.shape[1] // width):
            same = listed == jnp.zeros((1, width), jnp.float32) + ids_ref[m].astype(jnp.float32)
            found = jnp.sum(jnp.where(same, 1.0, 0.0), axis=1, keepdims=True)
            weight_ref[:, m * width : (m + 1) * width] = jnp.broadcast_to(found, (1, width))


def payload_kernel(place_ref, omega_ref, own_ref, other_ref, rhs_ref, sketch_ref, *refs):
    half, width = own_ref.shape
    split = half // 2
    core, leaf = place_ref[0], place_ref[1]
    shares, payload_ref = refs[:-1], refs[-1]
    begin = pl.multiple_of(core * half, half)
    sketch_ref[pl.ds(begin, half), :] = own_ref[...]
    sketch_ref[pl.ds(pl.multiple_of((1 - core) * half, half), half), :] = other_ref[...]
    own, other = own_ref[...], other_ref[...]
    lifted = noise_variance * omega_ref[...] + own
    count = half // TILE
    at = 0
    for i in range(count):
        product = mm_t(lifted[i * TILE : (i + 1) * TILE], own[i * TILE :])
        for j in range(count - i):
            payload_ref[at : at + TILE, :] = product[:, j * TILE : (j + 1) * TILE]
            at += TILE
    on_first = jnp.zeros((half, width), jnp.int32) + core == 0
    left = jnp.where(on_first, lifted, other)
    right = jnp.where(on_first[:split], other[:split], lifted[split:])
    product = mm_t(left, right)
    for j in range(split // TILE):
        payload_ref[at : at + half, :] = product[:, j * TILE : (j + 1) * TILE]
        at += half
    product = mm_t(rhs_ref[...], sketch_ref[...])
    samples = rhs_ref.shape[0]
    for j in range(2 * count):
        payload_ref[at : at + samples, :] = product[:, j * TILE : (j + 1) * TILE]
        at += samples
    rows = shares[0].shape[0]
    for m, share in enumerate(shares):
        share[...] = payload_ref[pl.ds(pl.multiple_of((leaf ^ m) * rows, rows), rows), :]


def kernel_call(kernel, name, outputs, *operands, scratch=(), flops=10**8):
    vmem = pl.BlockSpec(memory_space=pltpu.VMEM)
    smem = pl.BlockSpec(memory_space=pltpu.SMEM)
    return pl.pallas_call(
        kernel,
        out_shape=tuple(jax.ShapeDtypeStruct(shape, jnp.float32) for shape in outputs),
        in_specs=[smem if o.ndim == 1 else vmem for o in operands],
        out_specs=(vmem,) * len(outputs),
        scratch_shapes=[pltpu.VMEM(shape, jnp.float32) for shape in scratch],
        name=name,
        compiler_params=pltpu.CompilerParams(vmem_limit_bytes=12 * 2**20),
        cost_estimate=pl.CostEstimate(flops=flops, bytes_accessed=2**20, transcendentals=0),
    )(*operands)


def shifted(values, axis, distance):
    size = lax.axis_size(axis)
    return lax.ppermute(values, axis, [(i, (i + distance) % size) for i in range(size)])


def swapped(values, axis, mask):
    size = lax.axis_size(axis)
    return lax.ppermute(values, axis, [(i, i ^ mask) for i in range(size)])


def slab(values):
    return [values] + [swapped(values, "leaf", m) for m in range(1, lax.axis_size("leaf"))]


def group_size():
    return lax.axis_size(POINT_AXES)


def exchange(values):
    return lax.all_to_all(values, POINT_AXES, 0, 0, tiled=True)


def axis_sum(values, axis):
    if lax.axis_size(axis) != 4:
        return lax.psum(values, axis)
    one, two, three = (swapped(values, axis, m) for m in (1, 2, 3))
    return (values + one) + (two + three)


def spread(values):
    count = group_size()
    sent = jnp.broadcast_to(values[None], (count,) + values.shape).reshape(-1, values.shape[1])
    return exchange(sent).reshape((count,) + values.shape)


def to_tiles(values):
    return jnp.concatenate([values[:, c : c + TILE] for c in range(0, values.shape[1], TILE)], axis=0)


def from_tiles(tiles, rows):
    return jnp.concatenate([tiles[r : r + rows] for r in range(0, tiles.shape[0], rows)], axis=1)


def dot_rows(left, right):
    return jnp.sum(left * right, axis=1)


def local(points, neighbors, omega, observed, prior_draws):
    cycle = lax.axis_size("blk")
    leaves = lax.axis_size("leaf")
    cores = lax.axis_size("samp")
    own_slab, own_leaf, own_core = (lax.axis_index(a) for a in ("blk", "leaf", "samp"))
    sketch_size, width = omega.shape
    half = sketch_size // cores
    samples = prior_draws.shape[0]
    period = 2.0 * cycle

    core = own_core.astype(jnp.int32).reshape(1)
    place = jnp.stack([own_core, own_leaf]).astype(jnp.int32)
    split = half // 2
    first_block, second_block, meta, omega_half, rhs = prepare(
        core, points, neighbors, omega, observed[None, :], prior_draws, split
    )

    def other_core(values):
        return swapped(values, "samp", 1)

    def sent(upward, downward):
        return shifted(upward, "blk", 1), shifted(downward, "blk", -1)

    first_blocks, second_blocks = slab(first_block), slab(second_block)
    route = [
        (b * cores + c, (b + (1 if c == 0 else -1)) % cycle * cores + c) for b in range(cycle) for c in range(cores)
    ]
    arrived = lax.ppermute(meta, ("blk", "samp"), route)
    swapped_meta = other_core(arrived)
    above = jnp.where(own_core == 0, swapped_meta, arrived)
    below = jnp.where(own_core == 0, arrived, swapped_meta)
    begin = split + samples
    sources = jnp.concatenate([b[begin : begin + 3] for b in first_blocks], axis=1)
    source_ids = (own_slab * leaves + jnp.stack([own_leaf ^ m for m in range(leaves)])).astype(jnp.int32)
    tables = kernel_call(
        targets_kernel,
        "targets",
        [(3, width)] * 3 + [(1, leaves * width)] * 3,
        source_ids,
        above,
        meta,
        below,
    )
    targets, weights = tables[:3], tables[3:]

    def kernel_columns(index):
        offset = sources[:, :, None] - targets[index][:, None, :]
        along = offset[0]
        along = jnp.where(along >= 0.5 * period, along - period, along)
        along = jnp.where(along < -0.5 * period, along + period, along)
        squared = along * along + offset[1] * offset[1] + offset[2] * offset[2]
        radius = jnp.sqrt(squared) / support_radius
        remain = jnp.maximum(1.0 - radius, 0.0)
        squared_remain = remain * remain
        values = squared_remain * squared_remain * (4.0 * radius + 1.0)
        return values * weights[index].reshape(-1, 1)

    columns = [kernel_columns(i) for i in range(3)]

    def sums(values):
        gathered = jnp.concatenate(values, axis=1)
        return mm(gathered, columns[0]), mm(gathered, columns[2]), gathered

    upward, downward, gathered = sums([b[:begin] for b in first_blocks])
    _, _, *second_blocks = lax.optimization_barrier((upward, downward, *second_blocks))
    from_below, from_above = sent(upward, downward)
    applied = mm(gathered, columns[1]) + from_below + from_above
    upward, downward, gathered = sums(second_blocks)
    from_below, from_above = sent(upward, downward)
    applied_second = mm(gathered, columns[1]) + from_below + from_above
    sketch_half = jnp.concatenate([applied[:split], applied_second], axis=0) + sketch_shift * omega_half
    image_rhs = applied[split:] + noise_variance * rhs

    count = half // TILE
    matrix_rows = (count * (count + 1) // 2 + count * count // 2) * TILE
    payload_rows = matrix_rows + samples * (sketch_size // TILE)
    sketch, *shares = kernel_call(
        payload_kernel,
        "payload",
        [(sketch_size, width)] + [(payload_rows // leaves, TILE)] * leaves,
        place,
        omega_half,
        sketch_half,
        other_core(sketch_half),
        rhs,
        scratch=[(payload_rows, TILE)],
        flops=10**9,
    )

    *shares, late_sketch = lax.optimization_barrier((*shares, sketch_half))
    share = shares[0]
    for m in range(1, leaves):
        share = share + swapped(shares[m], "leaf", m)
    blocks = slab(late_sketch)
    upward, downward, gathered = sums(blocks)
    here = mm(gathered, columns[1])
    here = here + noise_variance * late_sketch
    shares = slab(axis_sum(share, "blk"))
    *shares, upward, downward, here = lax.optimization_barrier((*shares, upward, downward, here))
    other_shares = [other_core(s) for s in shares]
    from_below, from_above = sent(upward, downward)
    system, inverse, solved = kernel_call(
        inverse_kernel,
        "inverse_and_solve",
        [(sketch_size, sketch_size)] * 2 + [(samples, sketch_size)],
        place,
        *shares,
        *other_shares,
        scratch=[(payload_rows, TILE)] * 2,
        flops=30 * 10**9,
    )
    from_below, from_above, solved = lax.optimization_barrier((from_below, from_above, solved))
    own_image = here + from_below + from_above

    sum_rows = samples * (sketch_size // TILE) + 8
    sketches, direction, image, packet = kernel_call(
        image_kernel,
        "image",
        [(sketch_size, 2 * width)] + [(samples, width)] * 2 + [(sum_rows + samples * (width // TILE), TILE)],
        core,
        solved,
        sketch,
        own_image,
        other_core(own_image),
        rhs,
        image_rhs,
    )
    packets = slab(packet)
    slab_sum = (packets[0][:sum_rows] + packets[1][:sum_rows]) + (packets[2][:sum_rows] + packets[3][:sum_rows])
    upward, downward, gathered = sums([from_tiles(p[sum_rows:], samples) for p in packets])
    here = mm(gathered, columns[1]) + noise_variance * image
    if cycle == 4:
        even = own_slab % 2 == 0
        one, three = (
            swapped(jnp.concatenate([slab_sum, to_tiles(jnp.where(even, first, second))], axis=0), "blk", m)
            for m, first, second in ((1, upward, downward), (3, downward, upward))
        )
        two = swapped(slab_sum, "blk", 2)
        total = (slab_sum + one[:sum_rows]) + (two + three[:sum_rows])
        from_below, from_above = from_tiles(one[sum_rows:], samples), from_tiles(three[sum_rows:], samples)
    else:
        total = lax.psum(slab_sum, "blk")
        from_below, from_above = sent(upward, downward)
    image_twice = here + from_below + from_above
    solves = mm(inverse, sketches)
    solves = solves + rough_mm(inverse, sketches - mm(system, solves))
    moved = from_tiles(total[:-8], samples)
    dots = total[-8:]
    inner_first, curvature = dots[0, :samples, None], dots[1, :samples, None]
    step = inner_first / curvature

    taken = mm(moved, solves)
    precond = direction - step * ((image - taken[:, :width]) / noise_variance)
    image_precond = image - step * ((image_twice - taken[:, width:]) / noise_variance)
    residual = rhs - step * image
    dots = jnp.stack([dot_rows(residual, precond), dot_rows(precond, image_precond), dot_rows(precond, image)])
    dots = spread(jnp.pad(dots, ((0, 5), (0, TILE - samples)))).sum(axis=0)
    inner_second, curvature_precond, mixed = (dots[i, :samples, None] for i in range(3))
    beta = inner_second / inner_first
    step_second = inner_second / (curvature_precond + beta * (2.0 * mixed + beta * curvature))
    weights = step * direction + step_second * (precond + beta * direction)
    residual = residual - step_second * (image_precond + beta * image)
    return (weights, residual)


def solution(mesh):
    in_specs = (
        P(None, ("blk", "leaf")),
        P(("blk", "leaf"), None),
        P(None, ("blk", "leaf")),
        P(("blk", "leaf")),
        P("samp", ("blk", "leaf")),
    )
    out_specs = (P("samp", ("blk", "leaf")), P("samp", ("blk", "leaf")))
    return jax.shard_map(local, mesh=mesh, in_specs=in_specs, out_specs=out_specs, check_vma=False)
```
